128 devices in a mesh: dp: 16 (over x_lo, y, core), tensor: 8 (over z, x_hi).
Axes of the slice: x: 4 (x_hi: 2, x_lo: 2; x = x_hi * 2 + x_lo), y: 4, z: 4, core: 2. Of those that a mesh axis runs over, the one named last changes fastest.
Arguments:
- layer_input: float32 [12288, 2048], P('dp'), may hold values from -6 to 6
- ln_gain: float32 [2048], replicated, may hold values from 0.25 to 1.75
- ln_bias: float32 [2048], replicated, may hold values from -3 to 3
- w_qkv: bfloat16 [2048, 3, 2048], P(None, None, 'tensor'), may hold values from -0.125 to 0.125
- qkv_bias: float32 [3, 2048], P(None, 'tensor'), may hold values from -3 to 3
- w_out: bfloat16 [2048, 2048], P('tensor'), may hold values from -0.375 to 0.375
- out_bias: float32 [2048], replicated, may hold values from -1.75 to 1.75
- w_fc1: bfloat16 [2048, 8192], P(None, 'tensor'), may hold values from -0.125 to 0.125
- fc1_bias: float32 [8192], P('tensor'), may hold values from -3 to 3
- w_fc2: bfloat16 [8192, 2048], P('tensor'), may hold values from -0.09375 to 0.09375
- fc2_bias: float32 [2048], replicated, may hold values from -1.75 to 1.75
- segments: int32 [16, 768], P('dp'), may hold values from 0 to 3, never falling along the last dimension, each value on 1 to 384 neighbouring positions
- positions: int32 [16, 768], P('dp'), may hold values from 0 to 2047
- cotangent: bfloat16 [12288, 2048], P('dp'), may hold values from -6 to 6
Outputs:
- layer_output: float32 [12288, 2048], P('dp')
- d_layer_input: float32 [12288, 2048], P('dp')
- d_ln_gain: float32 [2048], replicated
- d_ln_bias: float32 [2048], replicated
- d_w_qkv: float32 [2048, 3, 2048], P(None, None, 'tensor')
- d_qkv_bias: float32 [3, 2048], P(None, 'tensor')
- d_w_out: float32 [2048, 2048], P('tensor')
- d_out_bias: float32 [2048], replicated
- d_w_fc1: float32 [2048, 8192], P(None, 'tensor')
- d_fc1_bias: float32 [8192], P('tensor')
- d_w_fc2: float32 [8192, 2048], P('tensor')
- d_fc2_bias: float32 [2048], replicated
The draws below stay inside these ranges and needn't reach their ends.
Inputs may be any that keep to these rules, and one draw needn't show every extreme that they name: `segments`: within each packed sequence the numbers never fall; each document has 1 to 384 tokens.
All inputs are finite; a program needn't handle non-finite values.
Results may differ from the reference program's by a relative error of at most 0.012.
Values sent between devices are 32-bit elements; how exact they have to be, the bound alone decides.
No kernel may reach another device: no remote copies, remote signals or barrier semaphores. Data moves between devices by JAX's collectives and lax.ppermute only.
A program may use at most 256 MiB of HBM per device.

```python
import math
import jax
import jax.numpy as jnp
import numpy as np
from jax import lax

D = 2048
HEADS = 32
HEAD_DIM = 64
ROT = 32
FF = 8192
TOK_DEV = 768
DOCS = 4
PACKS = 16
TOKENS = 12288


def plant(entries, rng, smallest, largest):
    longest = entries.shape.index(max(entries.shape))
    spots = []
    for shift in (0, 1):
        where = [jax.random.randint(jax.random.fold_in(rng, axis), (), 0, length) for axis, length in enumerate(entries.shape)]
        where[longest] = (where[longest] + shift) % entries.shape[longest]
        spots.append(tuple(where))
    return entries.at[spots[0]].set(smallest).at[spots[1]].set(largest)


def shard_levels(stream_key, extent, shards, low, largest):
    loudness = 1.0
    for dim, shards_of in shards:
        draws = jax.random.uniform(jax.random.fold_in(jax.random.fold_in(stream_key, 6), dim), (shards_of,), jnp.float32, low / len(shards), largest / len(shards))
        loudness = loudness * jnp.repeat(jnp.exp(draws), extent[dim] // shards_of).reshape((-1,) + (1,) * (len(extent) - 1 - dim))
    return loudness


def profile(number_of, total, limit, slope):
    portions = [(1 << 20) // math.isqrt(rank ** slope) + 1 for rank in range(2, number_of + 1)]
    spare, counts = total - limit - (number_of - 1), [1] * (number_of - 1)
    while spare > 0:
        free = [i for i in range(number_of - 1) if counts[i] < limit]
        whole, left = sum([portions[i] for i in free]), spare
        for i in free:
            addition = min(limit - counts[i], max(1, left * portions[i] // whole), spare)
            counts[i] = counts[i] + addition
            spare = spare - addition
    return np.array([limit] + counts)


def ragged_sizes(stream_key, number_of, total, most, lean):
    if number_of == 2:
        one = jax.random.randint(stream_key, (), max(1, total - most), min(most, total - 1) + 1)
        return jnp.stack([one, total - one])
    tallies = jnp.asarray(profile(number_of, total, most, lean), jnp.int32)
    twos = (number_of - 1) // 2
    source_of, taker = tallies[1:1 + 2 * twos:2], tallies[2:2 + 2 * twos:2]
    slack = jnp.minimum(source_of - 1, most - taker)
    passed = jax.random.randint(jax.random.fold_in(stream_key, 1), (twos,), 0, 1 << 20) % (slack + 1)
    tallies = tallies.at[1:1 + 2 * twos:2].set(source_of - passed).at[2:2 + 2 * twos:2].set(taker + passed)
    return tallies[jax.random.permutation(jax.random.fold_in(stream_key, 2), number_of)]


def centred(stream_key, extent, deviation, reach, pieces=(), dtype=jnp.bfloat16):
    result = jax.random.normal(stream_key, extent, jnp.float32) * deviation
    if len(pieces) > 0:
        result = shard_levels(stream_key, extent, pieces, -0.22, 0.18) * result
    return jnp.clip(result, min=-reach, max=reach).astype(dtype)


def setup_inputs(seed: int = 0) -> dict:
    arg_keys = jax.random.split(jax.random.key(seed), 15)
    layer_input = centred(arg_keys[0], (TOKENS, D), 1.0, 6.0, ((0, 16),), jnp.float32)
    ln_gain = jnp.clip(1.0 + 0.15 * jax.random.normal(arg_keys[1], (D,), jnp.float32), 0.25, 1.75)
    ln_bias = centred(arg_keys[2], (D,), 0.5, 3.0, (), jnp.float32)
    w_qkv = centred(arg_keys[3], (D, 3, D), D ** -0.5, 0.125, ((2, 8),))
    qkv_bias = centred(arg_keys[4], (3, D), 0.5, 3.0, ((1, 8),), jnp.float32)
    w_out = centred(arg_keys[5], (D, D), (D // 8) ** -0.5, 0.375, ((0, 8),))
    out_bias = centred(arg_keys[6], (D,), 0.3, 1.75, (), jnp.float32)
    w_fc1 = centred(arg_keys[7], (D, FF), D ** -0.5, 0.125, ((1, 8),))
    fc1_bias = centred(arg_keys[8], (FF,), 0.5, 3.0, ((0, 8),), jnp.float32)
    w_fc2 = centred(arg_keys[9], (FF, D), (FF // 2) ** -0.5, 0.09375, ((0, 8),))
    fc2_bias = centred(arg_keys[10], (D,), 0.3, 1.75, (), jnp.float32)
    segments = jax.vmap(lambda own: jnp.searchsorted(jnp.cumsum(ragged_sizes(own, DOCS, TOK_DEV, TOK_DEV // 2, 2)), jnp.arange(TOK_DEV), side="right"))(jax.random.split(arg_keys[11], PACKS)).reshape((PACKS, TOK_DEV)).astype(jnp.int32)
    positions = plant(jax.random.randint(arg_keys[12], (PACKS, TOK_DEV), 0, 2048), jax.random.fold_in(arg_keys[12], 1), 0, 2047).astype(jnp.int32)
    cotangent = centred(arg_keys[13], (TOKENS, D), 1.0, 6.0, ((0, 16),))
    return dict(layer_input=layer_input, ln_gain=ln_gain, ln_bias=ln_bias, w_qkv=w_qkv, qkv_bias=qkv_bias, w_out=w_out, out_bias=out_bias, w_fc1=w_fc1, fc1_bias=fc1_bias, w_fc2=w_fc2, fc2_bias=fc2_bias, segments=segments, positions=positions, cotangent=cotangent)


HIGH = lax.Precision.HIGHEST
EPSILON = 1e-05
MASKED = -1e+30

@jax.custom_vjp
def low(v):
    return lax.optimization_barrier(v.astype(jnp.bfloat16)).astype(jnp.float32)

@jax.custom_vjp
def low_back(v):
    return v

def low_keep(v):
    return (low(v), None)

def low_pass(kept, grad):
    return (grad,)

def back_keep(v):
    return (v, None)

def back_low(kept, grad):
    return (low(grad),)
low.defvjp(low_keep, low_pass)
low_back.defvjp(back_keep, back_low)

def rotate_half(values):
    half_dim = values.shape[-1] // 2
    return jnp.concatenate([-values[..., half_dim:], values[..., :half_dim]], axis=-1)

def turn_angles(positions):
    steps_half = jnp.arange(0, ROT, 2).astype(jnp.float32) / ROT
    inverse = 10000.0 ** (-steps_half)
    angles = positions.astype(jnp.float32)[..., None] * inverse
    angles = jnp.concatenate([angles, angles], axis=-1)
    return (jnp.cos(angles), jnp.sin(angles))

def rotate_forward(tensor, cosine, sine_table):
    rotated = tensor[..., :ROT]
    kept_part = tensor[..., ROT:]
    turned = rotated * cosine[..., None, :] + rotate_half(rotated) * sine_table[..., None, :]
    return jnp.concatenate([turned, kept_part], axis=-1)

def attend_row(bundle):
    queries, key_rows, value_rows, doc_ids = bundle
    length = queries.shape[0]
    token_index = jnp.arange(length)
    allowed = (doc_ids[:, None] == doc_ids[None, :]) & (token_index[None, :] <= token_index[:, None])
    scores = low_back(jnp.einsum('qhd,khd->hqk', queries, key_rows, precision=HIGH) * HEAD_DIM ** (-0.5))
    scores = jnp.where(allowed[None], scores, MASKED)
    attn_probs = low(jax.nn.softmax(scores, axis=-1))
    return jnp.einsum('hqk,khd->qhd', attn_probs, value_rows, precision=HIGH)

def forward(layer_input, params, doc_ids, positions):
    ln_gain, ln_bias, w_qkv, qkv_bias, w_out, out_bias, w_fc1, fc1_bias, w_fc2, fc2_bias = params
    amount, length = doc_ids.shape
    center = layer_input - lax.optimization_barrier(jnp.mean(layer_input, axis=-1, keepdims=True))
    normed = center * lax.rsqrt(lax.optimization_barrier(jnp.mean(center * center, axis=-1, keepdims=True)) + EPSILON)
    ln_low = low(normed * ln_gain + ln_bias)
    projected = jnp.einsum('td,dcf->tcf', ln_low, w_qkv, precision=HIGH) + qkv_bias[None]
    projected = low_back(projected).reshape(amount, length, 3, HEADS, HEAD_DIM)
    cosine, sine_table = turn_angles(positions)
    queries = low(rotate_forward(projected[:, :, 0], cosine, sine_table))
    key_rows = low(rotate_forward(projected[:, :, 1], cosine, sine_table))
    value_rows = low(projected[:, :, 2])
    context = lax.map(jax.checkpoint(attend_row), (queries, key_rows, value_rows, doc_ids))
    context = low(low_back(context.reshape(amount * length, HEADS * HEAD_DIM)))
    attn_sum = jnp.dot(context, w_out, precision=HIGH, preferred_element_type=jnp.float32)
    pre_act = low_back(jnp.dot(ln_low, w_fc1, precision=HIGH, preferred_element_type=jnp.float32) + fc1_bias)
    hidden = low(jax.nn.gelu(pre_act, approximate=True))
    mlp_sum = jnp.dot(hidden, w_fc2, precision=HIGH, preferred_element_type=jnp.float32)
    return layer_input + attn_sum + mlp_sum + out_bias + fc2_bias

def reference(layer_input, ln_gain, ln_bias, w_qkv, qkv_bias, w_out, out_bias, w_fc1, fc1_bias, w_fc2, fc2_bias, segments, positions, cotangent):
    params = tuple((weight.astype(jnp.float32) for weight in (ln_gain, ln_bias, w_qkv, qkv_bias, w_out, out_bias, w_fc1, fc1_bias, w_fc2, fc2_bias)))
    per_group = 1
    for amount in range(1, PACKS + 1):
        if PACKS % amount == 0 and amount * TOK_DEV <= 4096:
            per_group = amount
    groups = PACKS // per_group
    group_tokens = per_group * TOK_DEV
    shaped_inputs = layer_input.astype(jnp.float32).reshape(groups, group_tokens, D)
    shaped_cot = cotangent.astype(jnp.float32).reshape(groups, group_tokens, D)
    shaped_docs = segments.astype(jnp.int32).reshape(groups, per_group, TOK_DEV)
    shaped_pos = positions.astype(jnp.int32).reshape(groups, per_group, TOK_DEV)

    def group_step(running, bundle):
        group_inputs, group_cot, group_docs, group_pos = bundle

        def local_forward(inputs_here, params_here):
            return forward(inputs_here, params_here, group_docs, group_pos)
        outputs, pull_back = jax.vjp(local_forward, group_inputs, params)
        grad_inputs, grad_params = pull_back(group_cot)
        running = jax.tree.map(lambda earlier, update: earlier + update, running, grad_params)
        return (running, (outputs, grad_inputs))
    zeros_init = jax.tree.map(jnp.zeros_like, params)
    grad_totals, (outputs, grad_inputs) = lax.scan(group_step, zeros_init, (shaped_inputs, shaped_cot, shaped_docs, shaped_pos))
    return (outputs.reshape(TOKENS, D), grad_inputs.reshape(TOKENS, D), grad_totals[0], grad_totals[1], grad_totals[2], grad_totals[3], grad_totals[4], grad_totals[5], grad_totals[6], grad_totals[7], grad_totals[8], grad_totals[9])
```

```python
from functools import partial

import jax
import jax.numpy as jnp
import numpy as np
from jax import lax
from jax.experimental import pallas as pl
from jax.experimental.pallas import tpu as pltpu
from jax.sharding import PartitionSpec as P

HEAD_DIM = 64
ROT = 32
EPSILON = 1e-05
MASKED = -1e30
F32, BF16 = jnp.float32, jnp.bfloat16
ANY = pl.ANY


def shape(dims, dtype=F32):
    return jax.ShapeDtypeStruct(dims, dtype)


def kernel(body, out, grid, in_specs, out_specs, scratch=(), scalars=0, aliases=None, vmem=40, us=3):
    return pl.pallas_call(
        body,
        out_shape=out,
        grid_spec=pltpu.PrefetchScalarGridSpec(
            num_scalar_prefetch=scalars,
            grid=grid,
            in_specs=in_specs,
            out_specs=out_specs,
            scratch_shapes=scratch,
        ),
        input_output_aliases=aliases or {},
        compiler_params=pltpu.CompilerParams(vmem_limit_bytes=vmem << 20),
        cost_estimate=pl.CostEstimate(
            flops=0, bytes_accessed=int(us * 3e6), transcendentals=0
        ),
    )


def whole(dims):
    return pl.BlockSpec(dims, lambda *_: (0,) * len(dims))


def dot(a, b):
    return jnp.dot(a, b, preferred_element_type=F32)


def dot_nt(a, b):
    return lax.dot_general(a, b, (((1,), (1,)), ((), ())), preferred_element_type=F32)


def dot_tn(a, b):
    return lax.dot_general(a, b, (((0,), (0,)), ((), ())), preferred_element_type=F32)


X_LO, Y, CORE = 2, 4, 2
Z, X_HI = 4, 2


def dp_moves(step):
    pairs = []
    for x in range(X_LO):
        for y in range(Y):
            for c in range(CORE):
                x2, y2, c2 = step(x, y, c)
                there = ((x2 % X_LO) * Y + y2 % Y) * CORE + c2 % CORE
                pairs.append(((x * Y + y) * CORE + c, there))
    return pairs


def tensor_moves(step):
    pairs = []
    for z in range(Z):
        for x in range(X_HI):
            z2, x2 = step(z, x)
            pairs.append((z * X_HI + x, (z2 % Z) * X_HI + x2 % X_HI))
    return pairs


MOVES = {
    "core": ("dp", dp_moves(lambda x, y, c: (x, y, c + 1))),
    "y^1": ("dp", dp_moves(lambda x, y, c: (x, y ^ 1, c))),
    "y^2": ("dp", dp_moves(lambda x, y, c: (x, y ^ 2, c))),
    "xlo": ("dp", dp_moves(lambda x, y, c: (x + 1, y, c))),
    "y^3": ("dp", dp_moves(lambda x, y, c: (x, y ^ 3, c))),
    "z^1": ("tensor", tensor_moves(lambda z, x: (z ^ 1, x))),
    "z^3": ("tensor", tensor_moves(lambda z, x: (z ^ 3, x))),
    "z^2": ("tensor", tensor_moves(lambda z, x: (z ^ 2, x))),
    "xhi": ("tensor", tensor_moves(lambda z, x: (z, x + 1))),
}


def send(array, move):
    axis, pairs = MOVES[move]
    return lax.ppermute(array, axis, pairs)


def norm_rows(x):
    center = x - jnp.mean(x, axis=-1, keepdims=True)
    inv_std = lax.rsqrt(jnp.mean(center * center, axis=-1, keepdims=True) + EPSILON)
    return center * inv_std, inv_std


def ln_body(x_ref, gain_ref, bias_ref, low_ref):
    normed, _ = norm_rows(x_ref[...])
    low_ref[...] = (normed * gain_ref[...] + bias_ref[...]).astype(BF16)


def layer_norm(x, gain, bias):
    rows, width = x.shape
    step = 128
    return kernel(
        ln_body,
        shape((rows, width), BF16),
        (rows // step,),
        [pl.BlockSpec((step, width), lambda i: (i, 0)), whole((1, width)), whole((1, width))],
        pl.BlockSpec((step, width), lambda i: (i, 0)),
        us=5,
        vmem=60,
    )(x, gain, bias)


def fc1_body(ln_ref, w_ref, b_ref, hidden_ref, slope_ref):
    v = dot(ln_ref[...], w_ref[...]) + b_ref[...]
    root = np.float32(np.sqrt(2 / np.pi))
    square = v * v
    t = jnp.tanh(root * (v + np.float32(0.044715) * (square * v)))
    half = 0.5 * (1.0 + t)
    hidden_ref[...] = (v * half).astype(BF16)
    inner = root * (1.0 + np.float32(3 * 0.044715) * square)
    slope_ref[...] = (half + 0.5 * v * (1.0 - t * t) * inner).astype(slope_ref.dtype)


def fc1(ln, w, b):
    rows, width = ln.shape
    cols, step = w.shape[1], 256
    tile = pl.BlockSpec((rows, step), lambda j: (0, j))
    return kernel(
        fc1_body,
        (shape((rows, cols), BF16), shape((rows, cols), BF16)),
        (cols // step,),
        [
            whole((rows, width)),
            pl.BlockSpec((width, step), lambda j: (0, j)),
            pl.BlockSpec((1, step), lambda j: (0, j)),
        ],
        (tile, tile),
        us=8,
        vmem=60,
    )(ln, w, b)


def grad_pre_body(cot_ref, w_ref, slope_ref, out_ref, sum_ref):
    grad = (dot_nt(cot_ref[...], w_ref[...]) * slope_ref[...]).astype(BF16)
    out_ref[...] = grad
    sum_ref[...] = jnp.sum(grad.astype(F32), axis=0, keepdims=True)


def grad_pre_act(cot, w, slope):
    rows, width = cot.shape
    cols, step = w.shape[0], 256
    tile = pl.BlockSpec((rows, step), lambda j: (0, j))
    return kernel(
        grad_pre_body,
        (shape((rows, cols), BF16), shape((1, cols))),
        (cols // step,),
        [whole((rows, width)), pl.BlockSpec((step, width), lambda j: (j, 0)), tile],
        (tile, pl.BlockSpec((1, step), lambda j: (0, j))),
        us=7,
        vmem=60,
    )(cot, w, slope)


def weight_grad_body(left_ref, right_ref, out_ref, turned):
    @pl.when(pl.program_id(0) == 0)
    def _():
        turned[...] = left_ref[...].T

    out_ref[...] = dot(turned[...], right_ref[...])


def weight_grad(left, right, step=512):
    rows, m = left.shape
    n = right.shape[1]
    return kernel(
        weight_grad_body,
        shape((m, n)),
        (n // step,),
        [whole((rows, m)), pl.BlockSpec((rows, step), lambda j: (0, j))],
        pl.BlockSpec((m, step), lambda j: (0, j)),
        scratch=[pltpu.VMEM((m, rows), BF16)],
        us=7,
        vmem=60,
    )(left, right)


def side_grads_body(ln_ref, cot_ref, pre_ref, proj_ref, context_ref, out_ref, turned, cot_turned):
    j = pl.program_id(0)
    last = pl.num_programs(0) - 1

    @pl.when(j == 0)
    def _():
        turned[...] = ln_ref[...].T
        cot_turned[...] = cot_ref[...].T

    @pl.when(j < last - 3)
    def _():
        out_ref[...] = dot(turned[...], pre_ref[...])

    @pl.when((j >= last - 3) & (j < last))
    def _():
        out_ref[...] = dot(turned[...], proj_ref[0])

    @pl.when(j == last)
    def _():
        out_ref[...] = dot(cot_turned[...], context_ref[...])


def side_grads(ln, cot, pre, proj, context):
    rows, m = ln.shape
    n, step = pre.shape[1], proj.shape[2]
    count = n // step
    return kernel(
        side_grads_body,
        shape((m, n + 4 * step)),
        (count + 4,),
        [
            whole((rows, m)),
            whole((rows, m)),
            pl.BlockSpec((rows, step), lambda j: (0, jnp.minimum(j, count - 1))),
            pl.BlockSpec((1, rows, step), lambda j: (jnp.clip(j - count, 0, 2), 0, 0)),
            whole((rows, step)),
        ],
        pl.BlockSpec((m, step), lambda j: (0, j)),
        scratch=[pltpu.VMEM((m, rows), BF16)] * 2,
        us=13,
        vmem=60,
    )(ln, cot, pre, proj, context)


def split_body(side, one, three, turned):
    n, step = one.shape[1], three.shape[2]
    one[...] = side[:, :n]
    for c in range(3):
        three[c] = side[:, n + c * step : n + (c + 1) * step]
    turned[...] = side[:, n + 3 * step :].T


def split_grads(side, n, step, tile=256):
    rows = side.shape[0]
    return kernel(
        split_body,
        (shape((rows, n)), shape((3, rows, step)), shape((step, rows))),
        (rows // tile,),
        [pl.BlockSpec((tile, side.shape[1]), lambda i: (i, 0))],
        (
            pl.BlockSpec((tile, n), lambda i: (i, 0)),
            pl.BlockSpec((3, tile, step), lambda i: (0, i, 0)),
            pl.BlockSpec((step, tile), lambda i: (0, i)),
        ),
        us=12,
        vmem=60,
    )(side)


def swap_halves(u, low, high):
    width = u.shape[1]
    return pltpu.roll(u, width - ROT // 2, 1) * low + pltpu.roll(u, ROT // 2, 1) * high


def fill_tables(pos_ref, rate_ref, cos_ref, low_ref, high_ref):
    angles = pos_ref[...].astype(F32) * rate_ref[...]
    lane = lax.broadcasted_iota(jnp.int32, angles.shape, 1) % HEAD_DIM
    sine = jnp.sin(angles)
    cos_ref[...] = jnp.cos(angles)
    low_ref[...] = jnp.where(lane < ROT // 2, -sine, 0.0)
    high_ref[...] = jnp.where(lane < ROT // 2, 0.0, sine)


def rotary_rates():
    steps_half = jnp.arange(0, ROT, 2).astype(F32) / ROT
    inverse = 10000.0 ** (-steps_half)
    none = jnp.zeros((HEAD_DIM - ROT,), F32)
    return jnp.concatenate([inverse, inverse, none] * 2)[None]


def qkv_body(ln_ref, w_ref, b_ref, pos_ref, rate_ref, out_ref, cos_ref, low_ref, high_ref):
    c = pl.program_id(0)

    @pl.when(c == 0)
    def _():
        fill_tables(pos_ref, rate_ref, cos_ref, low_ref, high_ref)

    u = dot(ln_ref[...], w_ref[0]) + b_ref[0]

    @pl.when(c == 2)
    def _():
        out_ref[0] = u.astype(BF16)

    @pl.when(c < 2)
    def _():
        for lane in range(0, u.shape[1], 128):
            part = u[:, lane : lane + 128]
            turned = part * cos_ref[...] + swap_halves(part, low_ref[...], high_ref[...])
            out_ref[0, :, lane : lane + 128] = turned.astype(BF16)


def project(ln, w_parts, bias, positions, rates):
    rows, width = ln.shape
    cols = w_parts.shape[2]
    return kernel(
        qkv_body,
        (shape((3, rows, cols), BF16),) + (shape((rows, 128)),) * 3,
        (3,),
        [
            whole((rows, width)),
            pl.BlockSpec((1, width, cols), lambda c: (c, 0, 0)),
            pl.BlockSpec((1, 1, cols), lambda c: (c, 0, 0)),
            whole((rows, 1)),
            whole((1, 128)),
        ],
        (pl.BlockSpec((1, rows, cols), lambda c: (c, 0, 0)),) + (whole((rows, 128)),) * 3,
        us=7,
        vmem=60,
    )(ln, w_parts, bias, positions.reshape(rows, 1), rates)


def grad_context_body(cot_ref, w_ref, out_ref, sum_ref):
    @pl.when(pl.program_id(0) == 0)
    def _():
        sum_ref[...] = jnp.zeros_like(sum_ref)

    cot = cot_ref[...]
    out_ref[...] = dot_nt(cot, w_ref[...]).astype(BF16)
    sum_ref[...] += jnp.sum(cot.astype(F32), axis=0, keepdims=True)


def grad_of_context(cot, w, step=256):
    rows, width = cot.shape
    cols = w.shape[0]
    return kernel(
        grad_context_body,
        (shape((rows, cols), BF16), shape((1, width))),
        (rows // step,),
        [pl.BlockSpec((step, width), lambda i: (i, 0)), whole((cols, width))],
        (pl.BlockSpec((step, cols), lambda i: (i, 0)), whole((1, width))),
        us=2,
        vmem=60,
    )(cot, w)


def attention_body(
    q_ref, k_ref, v_ref, g_ref, seg_col, seg_row, cos_ref, low_ref, high_ref,
    context_ref, grad_ref, sum_ref, dq, dk, dv,
):
    rows = q_ref.shape[1]
    step = 256
    scale = np.float32(HEAD_DIM**-0.5)
    lane = lax.broadcasted_iota(jnp.int32, (rows, 128), 1)
    heads = []
    for h in range(2):
        mine = (lane >= h * HEAD_DIM) & (lane < (h + 1) * HEAD_DIM)
        heads.append(
            [
                jnp.where(mine, ref, jnp.zeros_like(ref))
                for ref in (q_ref[0] * scale.astype(BF16), k_ref[0], v_ref[0], g_ref[...])
            ]
        )
    dk[...] = jnp.zeros_like(dk)
    dv[...] = jnp.zeros_like(dv)
    for i in range(rows // step):
        top = slice(i * step, (i + 1) * step)
        seen = (i + 1) * step
        row = lax.broadcasted_iota(jnp.int32, (step, seen), 0) + i * step
        col = lax.broadcasted_iota(jnp.int32, (step, seen), 1)
        allowed = (seg_col[top, :] == seg_row[:, :seen]) & (col <= row)
        context = jnp.zeros((step, 128), F32)
        grad_q = jnp.zeros((step, 128), F32)
        for q, k, v, g in heads:
            scores = jnp.where(allowed, dot_nt(q[top], k[:seen]), MASKED)
            peak = jnp.max(scores, axis=-1, keepdims=True)
            raised = jnp.exp(scores - peak)
            probs = raised * (1.0 / jnp.sum(raised, axis=-1, keepdims=True))
            probs_low = probs.astype(BF16)
            context += dot(probs_low, v[:seen])
            grad_probs = dot_nt(g[top], v[:seen])
            delta = jnp.sum(probs * grad_probs, axis=-1, keepdims=True)
            grad_scores = (probs * (grad_probs - delta)).astype(BF16)
            grad_q += dot(grad_scores, k[:seen])
            dk[:seen, :] += dot_tn(grad_scores, q[top])
            dv[:seen, :] += dot_tn(probs_low, g[top])
        context_ref[top, :] = context.astype(BF16)
        dq[top, :] = grad_q * scale
    for c, grad in enumerate((dq, dk, dv)):
        u = grad[...]
        if c < 2:
            u = u * cos_ref[...] - swap_halves(u, low_ref[...], high_ref[...])
        u = u.astype(BF16)
        grad_ref[c] = u
        sum_ref[c] = jnp.sum(u.astype(F32), axis=0, keepdims=True)


def attention(qkv, grad_context, segments, tables):
    _, rows, cols = qkv.shape
    pair = pl.BlockSpec((rows, 128), lambda p: (0, p))
    return kernel(
        attention_body,
        (shape((rows, cols), BF16), shape((3, rows, cols), BF16), shape((3, 1, cols))),
        (cols // 128,),
        [pl.BlockSpec((1, rows, 128), lambda p, c=c: (c, 0, p)) for c in range(3)]
        + [pair, whole((rows, 1)), whole((1, rows))]
        + [whole((rows, 128))] * 3,
        (
            pair,
            pl.BlockSpec((3, rows, 128), lambda p: (0, 0, p)),
            pl.BlockSpec((3, 1, 128), lambda p: (0, 0, p)),
        ),
        scratch=[pltpu.VMEM((rows, 128), F32)] * 3,
        us=12,
        vmem=60,
    )(qkv, qkv, qkv, grad_context, segments.reshape(rows, 1), segments, *tables)


def chunks_of(z):
    return jnp.stack([z ^ 2, z ^ 1, z ^ 3, z]).astype(jnp.int32)


def put_chunks(outs, total):
    row = 0
    for out in outs:
        out[...] = total[row : row + out.shape[0], :]
        row += out.shape[0]


def chunk_rows(count):
    return [count // 2, count // 2, count, count, count]


def branch_body(at, *refs):
    lefts, rights = refs[:8], refs[8:10]
    outs, hidden, context = refs[10:15], refs[15], refs[16]
    count = outs[-1].shape[0]

    @pl.when(pl.program_id(0) == 0)
    def _():
        for i in range(4):
            hidden[i * count : (i + 1) * count, :] = lefts[i][...]
            context[i * count : (i + 1) * count, :] = lefts[4 + i][...]

    total = dot(hidden[...], rights[0][...]) + dot(context[...], rights[1][...])
    put_chunks(outs, total)


def branch_sums(at, hidden, context, w_fc2, w_out, step=256):
    rows, inner = hidden.shape
    heads = context.shape[1]
    width = w_fc2.shape[1]
    count = rows // 4

    def chunk(cols, i):
        return pl.BlockSpec((count, cols), lambda j, at, i=i: (at[i], 0))

    return kernel(
        branch_body,
        [shape((n, width)) for n in chunk_rows(count)],
        (width // step,),
        [chunk(inner, i) for i in range(4)]
        + [chunk(heads, i) for i in range(4)]
        + [
            pl.BlockSpec((inner, step), lambda j, at: (0, j)),
            pl.BlockSpec((heads, step), lambda j, at: (0, j)),
        ],
        [pl.BlockSpec((n, step), lambda j, at: (0, j)) for n in chunk_rows(count)],
        scratch=[pltpu.VMEM((rows, inner), BF16), pltpu.VMEM((rows, heads), BF16)],
        scalars=1,
        us=9,
        vmem=60,
    )(at, *[hidden] * 4, *[context] * 4, w_fc2, w_out)


def grad_ln_body(at, *refs):
    lefts, rights = refs[:8], refs[8:10]
    outs, pre, proj = refs[10:15], refs[15], refs[16]
    count = outs[-1].shape[0]

    @pl.when(pl.program_id(0) == 0)
    def _():
        for i in range(4):
            pre[i * count : (i + 1) * count, :] = lefts[i][...]
            for c in range(3):
                proj[c, i * count : (i + 1) * count, :] = lefts[4 + i][c]

    total = dot_nt(pre[...], rights[0][...])
    for c in range(3):
        total += dot_nt(proj[c], rights[1][c])
    put_chunks(outs, total)


def grad_ln_sums(at, pre, proj, w_fc1, w_parts, step=256):
    rows, inner = pre.shape
    heads = proj.shape[2]
    width = w_fc1.shape[0]
    count = rows // 4
    return kernel(
        grad_ln_body,
        [shape((n, width)) for n in chunk_rows(count)],
        (width // step,),
        [pl.BlockSpec((count, inner), lambda j, at, i=i: (at[i], 0)) for i in range(4)]
        + [pl.BlockSpec((3, count, heads), lambda j, at, i=i: (0, at[i], 0)) for i in range(4)]
        + [
            pl.BlockSpec((step, inner), lambda j, at: (j, 0)),
            pl.BlockSpec((3, step, heads), lambda j, at: (0, j, 0)),
        ],
        [pl.BlockSpec((n, step), lambda j, at: (0, j)) for n in chunk_rows(count)],
        scratch=[pltpu.VMEM((rows, inner), BF16), pltpu.VMEM((3, rows, heads), BF16)],
        scalars=1,
        us=11,
        vmem=60,
    )(at, *[pre] * 4, *[proj] * 4, w_fc1, w_parts)


def add_pair_body(up_in, down_in, high, low, up, down):
    up[...] = up_in[...] + high[...]
    down[...] = down_in[...] + low[...]


def add_halves(up, down, high, low, parts=2):
    rows, width = low.shape
    step = rows // parts
    first = pl.BlockSpec((step, width), lambda i: (i, 0))
    second = pl.BlockSpec((step, width), lambda i: (i + parts, 0))
    return kernel(
        add_pair_body,
        (shape(up.shape), shape(down.shape)),
        (parts,),
        [second, first, first, first],
        (second, first),
        aliases={0: 0, 1: 1},
        us=2,
        vmem=16,
    )(up, down, high, low)


def sum_body(*refs):
    total = refs[0][...]
    for ref in refs[1:-1]:
        total = total + ref[...]
    refs[-1][...] = total


def sum_of(*arrays, parts=3):
    rows, width = arrays[0].shape
    step = rows // parts
    spec = pl.BlockSpec((step, width), lambda i: (i, 0))
    return kernel(
        sum_body, shape((rows, width)), (rows // step,), [spec] * len(arrays), spec,
        us=3,
        vmem=16,
    )(*arrays)


def last_body(at, chunk, other, x, ob, fb, rows, out):
    del at
    total = chunk[...] + other[...] + x[...] + ob[...] + fb[...]
    rows[...] = total
    out[...] = total


def output_rows(at, chunk, other, x, out_bias, fc2_bias, step=48):
    count, width = chunk.shape
    parts = count // step
    here = pl.BlockSpec((step, width), lambda i, at: (i, 0))
    there = pl.BlockSpec((step, width), lambda i, at: (at[3] * parts + i, 0))
    return kernel(
        last_body,
        (shape((count, width)), shape(x.shape)),
        (parts,),
        [here, here, there, whole((1, width)), whole((1, width))],
        (here, there),
        scalars=1,
        us=4,
        vmem=16,
    )(at, chunk, other, x, out_bias, fc2_bias)


def norm_back_body(at, chunk, other, x, cot, gain, rows, out, sums):
    del at

    @pl.when(pl.program_id(0) == 0)
    def _():
        sums[...] = jnp.zeros_like(sums)

    grad = chunk[...] + other[...]
    normed, inv_std = norm_rows(x[...])
    sums[0:1, :] += jnp.sum(grad * normed, axis=0, keepdims=True)
    sums[1:2, :] += jnp.sum(grad, axis=0, keepdims=True)
    scaled = grad * gain[...]
    mean_scaled = jnp.mean(scaled, axis=-1, keepdims=True)
    mean_cross = jnp.mean(scaled * normed, axis=-1, keepdims=True)
    total = cot[...].astype(F32) + inv_std * (scaled - mean_scaled - normed * mean_cross)
    rows[...] = total
    out[...] = total


def input_grad_rows(at, chunk, other, x, cot, gain, step=48):
    count, width = chunk.shape
    parts = count // step
    here = pl.BlockSpec((step, width), lambda i, at: (i, 0))
    there = pl.BlockSpec((step, width), lambda i, at: (at[3] * parts + i, 0))
    return kernel(
        norm_back_body,
        (shape((count, width)), shape(x.shape), shape((2, width))),
        (parts,),
        [here, here, there, there, whole((1, width))],
        (here, there, whole((2, width))),
        scalars=1,
        us=5,
        vmem=16,
    )(at, chunk, other, x, cot, gain)


def place_body(at, *refs, starts, sizes, copies):
    i = pl.program_id(0)
    count = len(starts)
    pieces, out, extra = refs[:count], refs[count + 1], refs[count + 2 :]
    for piece, start, size in zip(pieces, starts, sizes):

        @pl.when((i >= start) & (i < start + size))
        def _(piece=piece):
            out[...] = piece[...]

    for copy, (which, first, size) in zip(extra, copies):
        begin = starts[which] + first

        @pl.when((i >= begin) & (i < begin + size))
        def _(copy=copy, which=which):
            copy[...] = pieces[which][...]


def place_rows(out, pieces, blocks, copies=(), step=48):
    width = out.shape[1]
    sizes = [piece.shape[0] // step for piece in pieces]
    starts = [sum(sizes[:k]) for k in range(len(sizes))]

    def part(start, size):
        return pl.BlockSpec((step, width), lambda i, at: (jnp.clip(i - start, 0, size - 1), 0))

    return kernel(
        partial(place_body, starts=starts, sizes=sizes, copies=copies),
        [shape(out.shape)] + [shape((size * step, width)) for _, _, size in copies],
        (sum(sizes),),
        [part(start, size) for start, size in zip(starts, sizes)]
        + [pl.BlockSpec(memory_space=ANY)],
        [pl.BlockSpec((step, width), lambda i, at: (at[i], 0))]
        + [part(starts[which] + first, size) for which, first, size in copies],
        scalars=1,
        aliases={1 + len(pieces): 0},
        us=5,
        vmem=16,
    )(blocks, *pieces, out)


def join_body(at, *refs):
    del at
    i = pl.program_id(0)
    both, out = refs[-2:]
    for k in range(2):

        @pl.when(i == k)
        def _(k=k):
            both[...] = refs[k][...]
            out[...] = refs[k][...]


def join_pieces(blocks, first, second, total_rows):
    rows, width = first.shape
    return kernel(
        join_body,
        (shape((2 * rows, width)), shape((total_rows, width))),
        (2,),
        [whole((rows, width))] * 2,
        (
            pl.BlockSpec((rows, width), lambda i, at: (i, 0)),
            pl.BlockSpec((rows, width), lambda i, at: (at[i], 0)),
        ),
        scalars=1,
        us=2,
        vmem=16,
    )(blocks, first, second)


class Order:
    def __init__(self):
        self.last = None

    def __call__(self, step, *args):
        if self.last is not None:
            args, _ = lax.optimization_barrier((args, self.last))
        out = step(*args)
        self.last = jax.tree.leaves(out)[0]
        return out

    def after(self, *arrays):
        arrays, _ = lax.optimization_barrier((arrays, self.last))
        return arrays

    def wait(self, array):
        array, self.last = lax.optimization_barrier((array, self.last))
        return array


def per_device(
    layer_input,
    ln_gain,
    ln_bias,
    w_qkv,
    qkv_bias,
    w_out,
    out_bias,
    w_fc1,
    fc1_bias,
    w_fc2,
    fc2_bias,
    segments,
    positions,
    cotangent,
):
    width = layer_input.shape[1]
    inner, local = w_fc1.shape[1], w_qkv.shape[2]
    at = chunks_of(lax.axis_index("tensor") // X_HI)
    at_dp = lax.axis_index("dp")
    x, y, core = at_dp // (Y * CORE), lax.rem(at_dp // CORE, Y), lax.rem(at_dp, CORE)
    run = Order()
    w_parts = jnp.transpose(w_qkv, (1, 0, 2))
    blocks = at[:3, None] * 4 + jnp.arange(4, dtype=jnp.int32)[None, :]
    near, far = blocks[1:].reshape(-1), blocks[0]
    near_copies = ((0, 0, 2), (1, 2, 2))
    add = partial(sum_of, parts=1)
    place_fc2 = partial(place_rows, step=64)

    def ranks(ys, core):
        xs = jnp.stack([x, 1 - x])
        return (((xs[None, :] * Y + ys[:, None]) * CORE) + core).reshape(-1).astype(jnp.int32)

    ring = chunks_of(y)

    ln = run(layer_norm, layer_input, ln_gain[None], ln_bias[None])
    hidden, slope = run(fc1, ln, w_fc1, fc1_bias[None])
    grad_fc2 = run(weight_grad, hidden, cotangent)
    piece_fc2 = lax.psum_scatter(grad_fc2, "dp", scatter_dimension=0, tiled=True)
    qkv, *tables = run(project, ln, w_parts, qkv_bias[:, None], positions, rotary_rates())
    grad_context, sum_out = run(grad_of_context, cotangent, w_out)
    context, grad_proj, sum_proj = run(attention, qkv, grad_context, segments, tables)
    low, high, up, down, own = run(branch_sums, at, hidden, context, w_fc2, w_out)
    low, high = send(low, "z^1"), send(high, "z^3")
    grad_pre, sum_pre = run(grad_pre_act, cotangent, w_fc2, slope)
    g_low, g_high, g_up, g_down, g_own = run(
        grad_ln_sums, at, grad_pre, grad_proj, w_fc1, w_parts
    )
    g_low, g_high = send(g_low, "z^1"), send(g_high, "z^3")
    side = run(side_grads, ln, cotangent, grad_pre, grad_proj, context)
    up, down = run(add_halves, up, down, high, low)
    g_up, g_down = run(add_halves, g_up, g_down, g_high, g_low)
    piece_fc2 = run.wait(piece_fc2)
    (side,) = run.after(side)
    piece = lax.psum_scatter(side, "dp", scatter_dimension=0, tiled=True)
    from_up, from_down = send(up, "z^1"), send(down, "z^3")
    g_from_up, g_from_down = send(g_up, "z^1"), send(g_down, "z^3")
    other_piece = send(*run.after(piece_fc2), "xlo")
    chunk = run(sum_of, own, from_up, from_down)
    other = send(chunk, "xhi")
    pair, tot_fc2 = run(
        lambda *pieces: join_pieces(ranks(ring[3:], core), *pieces, inner), piece_fc2, other_piece
    )
    f_up, f_down = send(pair, "y^1"), send(pair, "y^3")
    g_chunk = run(sum_of, g_own, g_from_up, g_from_down)
    g_other = send(g_chunk, "xhi")
    rows, output = run(
        output_rows, at, chunk, other, layer_input, out_bias[None], fc2_bias[None]
    )
    near_up, near_down = send(rows, "z^1"), send(rows, "z^3")
    tot_fc2, f_low, f_high = run(
        partial(place_fc2, copies=((0, 0, 1), (1, 1, 1))),
        tot_fc2, [f_up, f_down], ranks(ring[1:3], core),
    )
    f_low, f_high = send(f_low, "y^3"), send(f_high, "y^1")
    g_rows, grad_input, sums = run(
        input_grad_rows, at, g_chunk, g_other, layer_input, cotangent, ln_gain[None]
    )
    output, low, high = run(
        partial(place_rows, copies=near_copies), output, [near_up, near_down], near
    )
    (tot_fc2,) = run(place_fc2, tot_fc2, [f_low, f_high], ranks(ring[:1], core))
    piece = run.wait(piece)
    side = lax.all_gather(piece, "dp", axis=0, tiled=True)
    g_rows, pair, f_up, f_down = run.after(g_rows, pair, f_up, f_down)
    g_near_up, g_near_down = send(g_rows, "z^1"), send(g_rows, "z^3")
    low, high = send(low, "z^3"), send(high, "z^1")
    sums = sums.reshape(8, width // 4)
    sums = run(add, sums, send(sums, "z^1"))
    pair = send(pair, "core")
    (output,) = run(place_rows, output, [low, high], far)
    f_up, f_down = send(*run.after(f_up), "core"), send(*run.after(f_down), "core")
    sums = run(add, sums, send(sums, "z^2"))
    biases = jnp.concatenate(
        [sum_out[0], sum_pre[0], sum_proj.reshape(-1), jnp.zeros((256,), F32)]
    ).reshape(8, width // 4)
    sums = jnp.concatenate([sums, biases], axis=0)
    grad_input, g_low, g_high = run(
        partial(place_rows, copies=near_copies), grad_input, [g_near_up, g_near_down], near
    )
    g_low, g_high = send(g_low, "z^3"), send(g_high, "z^1")
    sums = run(add, sums, send(sums, "core"))
    (tot_fc2,) = run(
        place_fc2, tot_fc2, [pair, f_up, f_down],
        jnp.concatenate([ranks(ring[3:], 1 - core), ranks(ring[1:3], 1 - core)]),
    )
    f_low, f_high = run.after(f_low, f_high)
    f_low, f_high = send(f_low, "core"), send(f_high, "core")
    sums = run(add, sums, send(sums, "y^1"))
    (tot_fc2,) = run(place_fc2, tot_fc2, [f_low, f_high], ranks(ring[:1], 1 - core))
    sums = run(add, sums, send(sums, "y^2"))
    (grad_input,) = run(place_rows, grad_input, [g_low, g_high], far)
    sums = run(add, sums, send(sums, "xlo"))
    tot_fc1, tot_qkv, tot_out = run(lambda side: split_grads(side, inner, local), side)

    sums = sums.reshape(-1)
    gain, shift, tot_out_bias, tot_fc1_bias, tot_qkv_bias = (
        sums[:width],
        sums[width : 2 * width],
        sums[2 * width : 3 * width],
        sums[3 * width : 3 * width + inner],
        sums[3 * width + inner : 3 * width + inner + 3 * local],
    )
    return (
        output,
        grad_input,
        gain,
        shift,
        jnp.transpose(tot_qkv, (1, 0, 2)),
        tot_qkv_bias.reshape(3, local),
        tot_out,
        tot_out_bias,
        tot_fc1,
        tot_fc1_bias,
        tot_fc2,
        tot_out_bias,
    )


def solution(mesh):
    in_specs = (
        P("dp", None),
        P(),
        P(),
        P(None, None, "tensor"),
        P(None, "tensor"),
        P("tensor", None),
        P(),
        P(None, "tensor"),
        P("tensor"),
        P("tensor", None),
        P(),
        P("dp", None),
        P("dp", None),
        P("dp", None),
    )
    out_specs = (
        P("dp", None),
        P("dp", None),
        P(),
        P(),
        P(None, None, "tensor"),
        P(None, "tensor"),
        P("tensor", None),
        P(),
        P(None, "tensor"),
        P("tensor"),
        P("tensor", None),
        P(),
    )
    return jax.shard_map(
        per_device, mesh=mesh, in_specs=in_specs, out_specs=out_specs, check_vma=False
    )
```

```python
from functools import partial

import jax
import jax.numpy as jnp
import numpy as np
from jax import lax
from jax.experimental import pallas as pl
from jax.experimental.pallas import tpu as pltpu
from jax.sharding import PartitionSpec as P

HEAD_DIM = 64
ROT = 32
EPSILON = 1e-05
MASKED = -1e30
F32, BF16 = jnp.float32, jnp.bfloat16
ANY = pl.ANY


def shape(dims, dtype=F32):
    return jax.ShapeDtypeStruct(dims, dtype)


def kernel(body, out, grid, in_specs, out_specs, scratch=(), scalars=0, aliases=None, vmem=40, us=3):
    return pl.pallas_call(
        body,
        out_shape=out,
        grid_spec=pltpu.PrefetchScalarGridSpec(
            num_scalar_prefetch=scalars,
            grid=grid,
            in_specs=in_specs,
            out_specs=out_specs,
            scratch_shapes=scratch,
        ),
        input_output_aliases=aliases or {},
        compiler_params=pltpu.CompilerParams(vmem_limit_bytes=vmem << 20),
        cost_estimate=pl.CostEstimate(
            flops=0, bytes_accessed=int(us * 3e6), transcendentals=0
        ),
    )


def whole(dims):
    return pl.BlockSpec(dims, lambda *_: (0,) * len(dims))


def dot(a, b):
    return jnp.dot(a, b, preferred_element_type=F32)


def dot_nt(a, b):
    return lax.dot_general(a, b, (((1,), (1,)), ((), ())), preferred_element_type=F32)


def dot_tn(a, b):
    return lax.dot_general(a, b, (((0,), (0,)), ((), ())), preferred_element_type=F32)


X_LO, Y, CORE = 2, 4, 2
Z, X_HI = 4, 2


def dp_moves(step):
    pairs = []
    for x in range(X_LO):
        for y in range(Y):
            for c in range(CORE):
                x2, y2, c2 = step(x, y, c)
                there = ((x2 % X_LO) * Y + y2 % Y) * CORE + c2 % CORE
                pairs.append(((x * Y + y) * CORE + c, there))
    return pairs


def tensor_moves(step):
    pairs = []
    for z in range(Z):
        for x in range(X_HI):
            z2, x2 = step(z, x)
            pairs.append((z * X_HI + x, (z2 % Z) * X_HI + x2 % X_HI))
    return pairs


MOVES = {
    "core": ("dp", dp_moves(lambda x, y, c: (x, y, c + 1))),
    "y^1": ("dp", dp_moves(lambda x, y, c: (x, y ^ 1, c))),
    "y^2": ("dp", dp_moves(lambda x, y, c: (x, y ^ 2, c))),
    "xlo": ("dp", dp_moves(lambda x, y, c: (x + 1, y, c))),
    "y^3": ("dp", dp_moves(lambda x, y, c: (x, y ^ 3, c))),
    "z^1": ("tensor", tensor_moves(lambda z, x: (z ^ 1, x))),
    "z^3": ("tensor", tensor_moves(lambda z, x: (z ^ 3, x))),
    "z^2": ("tensor", tensor_moves(lambda z, x: (z ^ 2, x))),
    "xhi": ("tensor", tensor_moves(lambda z, x: (z, x + 1))),
}


def send(array, move):
    axis, pairs = MOVES[move]
    return lax.ppermute(array, axis, pairs)


def norm_rows(x):
    center = x - jnp.mean(x, axis=-1, keepdims=True)
    inv_std = lax.rsqrt(jnp.mean(center * center, axis=-1, keepdims=True) + EPSILON)
    return center * inv_std, inv_std


def gelu_and_slope(v):
    a = np.float32(np.sqrt(2 / np.pi))
    b = np.float32(a * 0.044715)
    square = v * v
    h = 0.5 * jnp.tanh(v * (a + b * square)) + 0.5
    return v * h, h + v * (2 * a + 6 * b * square) * (h - h * h)


def ln_fc1_body(x_ref, gain_ref, bias_ref, w_ref, b_ref, low_ref, hidden_ref, slope_ref):
    i = pl.program_id(0)
    step = x_ref.shape[0]
    blocks = low_ref.shape[0] // step

    @pl.when(i < blocks)
    def _():
        normed, _ = norm_rows(x_ref[...])
        low = (normed * gain_ref[...] + bias_ref[...]).astype(BF16)
        low_ref[pl.ds(pl.multiple_of(i * step, step), step), :] = low

    @pl.when(i >= blocks)
    def _():
        hidden, slope = gelu_and_slope(dot(low_ref[...], w_ref[...]) + b_ref[...])
        hidden_ref[...] = hidden.astype(BF16)
        slope_ref[...] = slope.astype(BF16)


def ln_fc1(x, gain, bias, w, b, block=128, step=256):
    rows, width = x.shape
    cols = w.shape[1]
    blocks, tiles = rows // block, cols // step

    def tile(j):
        return jnp.maximum(j - blocks, 0)

    out = pl.BlockSpec((rows, step), lambda j: (0, tile(j)))
    return kernel(
        ln_fc1_body,
        (shape((rows, width), BF16), shape((rows, cols), BF16), shape((rows, cols), BF16)),
        (blocks + tiles,),
        [
            pl.BlockSpec((block, width), lambda j: (jnp.minimum(j, blocks - 1), 0)),
            whole((1, width)),
            whole((1, width)),
            pl.BlockSpec((width, step), lambda j: (0, tile(j))),
            pl.BlockSpec((1, step), lambda j: (0, tile(j))),
        ],
        (whole((rows, width)), out, out),
        us=13,
        vmem=60,
    )(x, gain, bias, w, b)


def grad_pre_body(cot_ref, w_ref, slope_ref, out_ref, sum_ref):
    grad = (dot_nt(cot_ref[...], w_ref[...]) * slope_ref[...]).astype(BF16)
    out_ref[...] = grad
    sum_ref[...] = jnp.sum(grad.astype(F32), axis=0, keepdims=True)


def grad_pre_act(cot, w, slope):
    rows, width = cot.shape
    cols, step = w.shape[0], 256
    tile = pl.BlockSpec((rows, step), lambda j: (0, j))
    return kernel(
        grad_pre_body,
        (shape((rows, cols), BF16), shape((1, cols))),
        (cols // step,),
        [whole((rows, width)), pl.BlockSpec((step, width), lambda j: (j, 0)), tile],
        (tile, pl.BlockSpec((1, step), lambda j: (0, j))),
        us=7,
        vmem=60,
    )(cot, w, slope)


def cot_products_body(
    left_ref, cot_ref, w_ref, out_ref, context_ref, sum_ref, turned, total
):
    j = pl.program_id(0)

    @pl.when(j == 0)
    def _():
        turned[...] = left_ref[...].T
        total[...] = jnp.zeros_like(total)

    cot = cot_ref[...]
    out_ref[...] = dot(turned[...], cot)
    total[...] += dot_nt(cot, w_ref[...])
    sum_ref[...] = jnp.sum(cot.astype(F32), axis=0, keepdims=True)

    @pl.when(j == pl.num_programs(0) - 1)
    def _():
        context_ref[...] = total[...].astype(BF16)


def cot_products(left, cot, w, step=512):
    rows, m = left.shape
    n, cols = cot.shape[1], w.shape[0]
    return kernel(
        cot_products_body,
        (shape((m, n)), shape((rows, cols), BF16), shape((1, n))),
        (n // step,),
        [
            whole((rows, m)),
            pl.BlockSpec((rows, step), lambda j: (0, j)),
            pl.BlockSpec((cols, step), lambda j: (0, j)),
        ],
        (
            pl.BlockSpec((m, step), lambda j: (0, j)),
            whole((rows, cols)),
            pl.BlockSpec((1, step), lambda j: (0, j)),
        ),
        scratch=[pltpu.VMEM((m, rows), BF16), pltpu.VMEM((rows, cols), F32)],
        us=9,
        vmem=60,
    )(left, cot, w)


def side_grads_body(ln_ref, cot_ref, pre_ref, proj_ref, context_ref, out_ref):
    n, step = pre_ref.shape[1], proj_ref.shape[2]
    turned = ln_ref[...].T
    out_ref[:, :n] = dot(turned, pre_ref[...])
    for c in range(3):
        out_ref[:, n + c * step : n + (c + 1) * step] = dot(turned, proj_ref[c])
    out_ref[:, n + 3 * step :] = dot(cot_ref[...].T, context_ref[...])


def side_grads(ln, cot, pre, proj, context, block=512):
    rows, m = ln.shape
    n, step = pre.shape[1], proj.shape[2]
    tile = pl.BlockSpec((rows, block), lambda j: (0, j))
    return kernel(
        side_grads_body,
        shape((m, n + 4 * step)),
        (m // block,),
        [tile, tile, whole((rows, n)), whole((3, rows, step)), whole((rows, step))],
        pl.BlockSpec((block, n + 4 * step), lambda j: (j, 0)),
        us=13,
        vmem=60,
    )(ln, cot, pre, proj, context)


def split_body(side, one, three, turned):
    n, step = one.shape[1], three.shape[2]
    one[...] = side[:, :n]
    for c in range(3):
        three[c] = side[:, n + c * step : n + (c + 1) * step]
    turned[...] = side[:, n + 3 * step :].T


def split_grads(side, n, step, tile=256):
    rows = side.shape[0]
    return kernel(
        split_body,
        (shape((rows, n)), shape((3, rows, step)), shape((step, rows))),
        (rows // tile,),
        [pl.BlockSpec((tile, side.shape[1]), lambda i: (i, 0))],
        (
            pl.BlockSpec((tile, n), lambda i: (i, 0)),
            pl.BlockSpec((3, tile, step), lambda i: (0, i, 0)),
            pl.BlockSpec((step, tile), lambda i: (0, i)),
        ),
        us=12,
        vmem=60,
    )(side)


def copy_body(source, out):
    out[...] = source[...]


def copy_of(source, step=128):
    rows, width = source.shape
    spec = pl.BlockSpec((step, width), lambda i: (i, 0))
    return kernel(
        copy_body, shape((rows, width)), (rows // step,), [spec], spec, us=6, vmem=16
    )(source)


def swap_halves(u, low, high):
    width = u.shape[1]
    return pltpu.roll(u, width - ROT // 2, 1) * low + pltpu.roll(u, ROT // 2, 1) * high


def fill_tables(pos_ref, rate_ref, cos_ref, low_ref, high_ref):
    angles = rate_ref[...] * pos_ref[...].astype(F32)
    count = ROT // 2
    entry = lax.broadcasted_iota(jnp.int32, (count, 2 * HEAD_DIM), 0)
    lane = lax.broadcasted_iota(jnp.int32, (count, 2 * HEAD_DIM), 1) % HEAD_DIM
    first = jnp.where(lane == entry, 1.0, 0.0).astype(F32)
    second = jnp.where(lane == entry + count, 1.0, 0.0).astype(F32)

    def spread(table, lanes):
        return lax.dot_general(
            table, lanes, (((0,), (0,)), ((), ())),
            precision=lax.Precision.HIGHEST, preferred_element_type=F32,
        )

    sine = jnp.sin(angles)
    kept = jnp.where(lane[:1] >= ROT, 1.0, 0.0)
    cos_ref[...] = spread(jnp.cos(angles), first + second) + kept
    low_ref[...] = spread(sine, -first)
    high_ref[...] = spread(sine, second)


def rotary_rates():
    steps_half = jnp.arange(0, ROT, 2).astype(F32) / ROT
    return (10000.0 ** (-steps_half))[:, None]


def qkv_body(ln_ref, w_ref, b_ref, pos_ref, rate_ref, out_ref, cos_ref, low_ref, high_ref):
    c = pl.program_id(0)

    @pl.when(c == 0)
    def _():
        fill_tables(pos_ref, rate_ref, cos_ref, low_ref, high_ref)

    u = dot(ln_ref[...], w_ref[0]) + b_ref[0]

    @pl.when(c == 2)
    def _():
        out_ref[0] = u.astype(BF16)

    @pl.when(c < 2)
    def _():
        for lane in range(0, u.shape[1], 128):
            part = u[:, lane : lane + 128]
            turned = part * cos_ref[...] + swap_halves(part, low_ref[...], high_ref[...])
            out_ref[0, :, lane : lane + 128] = turned.astype(BF16)


def project(ln, w_parts, bias, positions, rates):
    rows, width = ln.shape
    cols = w_parts.shape[2]
    return kernel(
        qkv_body,
        (shape((3, rows, cols), BF16),) + (shape((rows, 128)),) * 3,
        (3,),
        [
            whole((rows, width)),
            pl.BlockSpec((1, width, cols), lambda c: (c, 0, 0)),
            pl.BlockSpec((1, 1, cols), lambda c: (c, 0, 0)),
            whole((1, rows)),
            whole((ROT // 2, 1)),
        ],
        (pl.BlockSpec((1, rows, cols), lambda c: (c, 0, 0)),) + (whole((rows, 128)),) * 3,
        us=7,
        vmem=60,
    )(ln, w_parts, bias, positions, rates)


def attention_body(
    q_ref, k_ref, v_ref, g_ref, seg_col, seg_row, cos_ref, low_ref, high_ref,
    context_ref, grad_ref, sum_ref, dq, dk, dv,
):
    rows = q_ref.shape[1]
    step = 256
    scale = np.float32(HEAD_DIM**-0.5)
    lane = lax.broadcasted_iota(jnp.int32, (rows, 128), 1)
    heads = []
    for h in range(2):
        mine = (lane >= h * HEAD_DIM) & (lane < (h + 1) * HEAD_DIM)
        heads.append(
            [
                jnp.where(mine, ref, jnp.zeros_like(ref))
                for ref in (q_ref[0] * scale.astype(BF16), k_ref[0], v_ref[0], g_ref[...])
            ]
        )
    dk[...] = jnp.zeros_like(dk)
    dv[...] = jnp.zeros_like(dv)
    for i in range(rows // step):
        top = slice(i * step, (i + 1) * step)
        seen = (i + 1) * step
        row = lax.broadcasted_iota(jnp.int32, (step, seen), 0) + i * step
        col = lax.broadcasted_iota(jnp.int32, (step, seen), 1)
        allowed = (seg_col[top, :] == seg_row[:, :seen]) & (col <= row)
        context = jnp.zeros((step, 128), F32)
        grad_q = jnp.zeros((step, 128), F32)
        for q, k, v, g in heads:
            scores = jnp.where(allowed, dot_nt(q[top], k[:seen]), MASKED)
            peak = jnp.max(scores, axis=-1, keepdims=True)
            raised = jnp.exp(scores - peak)
            probs = raised * (1.0 / jnp.sum(raised, axis=-1, keepdims=True))
            probs_low = probs.astype(BF16)
            context += dot(probs_low, v[:seen])
            grad_probs = dot_nt(g[top], v[:seen])
            delta = jnp.sum(probs * grad_probs, axis=-1, keepdims=True)
            grad_scores = (probs * (grad_probs - delta)).astype(BF16)
            grad_q += dot(grad_scores, k[:seen])
            dk[:seen, :] += dot_tn(grad_scores, q[top])
            dv[:seen, :] += dot_tn(probs_low, g[top])
        context_ref[top, :] = context.astype(BF16)
        dq[top, :] = grad_q * scale
    for c, grad in enumerate((dq, dk, dv)):
        u = grad[...]
        if c < 2:
            u = u * cos_ref[...] - swap_halves(u, low_ref[...], high_ref[...])
        u = u.astype(BF16)
        grad_ref[c] = u
        sum_ref[c] = jnp.sum(u.astype(F32), axis=0, keepdims=True)


def attention(qkv, grad_context, segments, tables):
    _, rows, cols = qkv.shape
    pair = pl.BlockSpec((rows, 128), lambda p: (0, p))
    return kernel(
        attention_body,
        (shape((rows, cols), BF16), shape((3, rows, cols), BF16), shape((3, 1, cols))),
        (cols // 128,),
        [pl.BlockSpec((1, rows, 128), lambda p, c=c: (c, 0, p)) for c in range(3)]
        + [pair, whole((rows, 1)), whole((1, rows))]
        + [whole((rows, 128))] * 3,
        (
            pair,
            pl.BlockSpec((3, rows, 128), lambda p: (0, 0, p)),
            pl.BlockSpec((3, 1, 128), lambda p: (0, 0, p)),
        ),
        scratch=[pltpu.VMEM((rows, 128), F32)] * 3,
        us=12,
        vmem=60,
    )(qkv, qkv, qkv, grad_context, segments.reshape(rows, 1), segments, *tables)


def chunks_of(z):
    return jnp.stack([z ^ 2, z ^ 1, z ^ 3, z]).astype(jnp.int32)


def put_chunks(outs, total):
    row = 0
    for out in outs:
        out[...] = total[row : row + out.shape[0], :]
        row += out.shape[0]


def chunk_rows(count):
    return [count // 2, count // 2, count, count, count]


def branch_body(at, *refs):
    lefts, rights = refs[:8], refs[8:10]
    outs, hidden, context = refs[10:15], refs[15], refs[16]
    count = outs[-1].shape[0]

    @pl.when(pl.program_id(0) == 0)
    def _():
        for i in range(4):
            hidden[i * count : (i + 1) * count, :] = lefts[i][...]
            context[i * count : (i + 1) * count, :] = lefts[4 + i][...]

    total = dot(hidden[...], rights[0][...]) + dot(context[...], rights[1][...])
    put_chunks(outs, total)


def branch_sums(at, hidden, context, w_fc2, w_out, step=512):
    rows, inner = hidden.shape
    heads = context.shape[1]
    width = w_fc2.shape[1]
    count = rows // 4

    def chunk(cols, i):
        return pl.BlockSpec((count, cols), lambda j, at, i=i: (at[i], 0))

    return kernel(
        branch_body,
        [shape((n, width)) for n in chunk_rows(count)],
        (width // step,),
        [chunk(inner, i) for i in range(4)]
        + [chunk(heads, i) for i in range(4)]
        + [
            pl.BlockSpec((inner, step), lambda j, at: (0, j)),
            pl.BlockSpec((heads, step), lambda j, at: (0, j)),
        ],
        [pl.BlockSpec((n, step), lambda j, at: (0, j)) for n in chunk_rows(count)],
        scratch=[pltpu.VMEM((rows, inner), BF16), pltpu.VMEM((rows, heads), BF16)],
        scalars=1,
        us=9,
        vmem=60,
    )(at, *[hidden] * 4, *[context] * 4, w_fc2, w_out)


def grad_ln_body(at, *refs):
    lefts, rights = refs[:8], refs[8:10]
    outs, pre, proj = refs[10:15], refs[15], refs[16]
    count = outs[-1].shape[0]

    @pl.when(pl.program_id(0) == 0)
    def _():
        for i in range(4):
            pre[i * count : (i + 1) * count, :] = lefts[i][...]
            for c in range(3):
                proj[c, i * count : (i + 1) * count, :] = lefts[4 + i][c]

    total = dot_nt(pre[...], rights[0][...])
    for c in range(3):
        total += dot_nt(proj[c], rights[1][c])
    put_chunks(outs, total)


def grad_ln_sums(at, pre, proj, w_fc1, w_parts, step=256):
    rows, inner = pre.shape
    heads = proj.shape[2]
    width = w_fc1.shape[0]
    count = rows // 4
    return kernel(
        grad_ln_body,
        [shape((n, width)) for n in chunk_rows(count)],
        (width // step,),
        [pl.BlockSpec((count, inner), lambda j, at, i=i: (at[i], 0)) for i in range(4)]
        + [pl.BlockSpec((3, count, heads), lambda j, at, i=i: (0, at[i], 0)) for i in range(4)]
        + [
            pl.BlockSpec((step, inner), lambda j, at: (j, 0)),
            pl.BlockSpec((3, step, heads), lambda j, at: (0, j, 0)),
        ],
        [pl.BlockSpec((n, step), lambda j, at: (0, j)) for n in chunk_rows(count)],
        scratch=[pltpu.VMEM((rows, inner), BF16), pltpu.VMEM((3, rows, heads), BF16)],
        scalars=1,
        us=11,
        vmem=60,
    )(at, *[pre] * 4, *[proj] * 4, w_fc1, w_parts)


def add_pair_body(up_in, down_in, high, low, up, down):
    up[...] = up_in[...] + high[...]
    down[...] = down_in[...] + low[...]


def add_halves(up, down, high, low, parts=2):
    rows, width = low.shape
    step = rows // parts
    first = pl.BlockSpec((step, width), lambda i: (i, 0))
    second = pl.BlockSpec((step, width), lambda i: (i + parts, 0))
    return kernel(
        add_pair_body,
        (shape(up.shape), shape(down.shape)),
        (parts,),
        [second, first, first, first],
        (second, first),
        aliases={0: 0, 1: 1},
        us=2,
        vmem=16,
    )(up, down, high, low)


def sum_body(*refs):
    total = refs[0][...]
    for ref in refs[1:-1]:
        total = total + ref[...]
    refs[-1][...] = total


def sum_of(*arrays, parts=3):
    rows, width = arrays[0].shape
    step = rows // parts
    spec = pl.BlockSpec((step, width), lambda i: (i, 0))
    return kernel(
        sum_body, shape((rows, width)), (rows // step,), [spec] * len(arrays), spec,
        us=3,
        vmem=16,
    )(*arrays)


def last_body(at, chunk, other, x, ob, fb, rows, out):
    del at
    total = chunk[...] + other[...] + x[...] + ob[...] + fb[...]
    rows[...] = total
    out[...] = total


def output_rows(at, chunk, other, x, out_bias, fc2_bias, step=48):
    count, width = chunk.shape
    parts = count // step
    here = pl.BlockSpec((step, width), lambda i, at: (i, 0))
    there = pl.BlockSpec((step, width), lambda i, at: (at[3] * parts + i, 0))
    return kernel(
        last_body,
        (shape((count, width)), shape(x.shape)),
        (parts,),
        [here, here, there, whole((1, width)), whole((1, width))],
        (here, there),
        scalars=1,
        us=4,
        vmem=16,
    )(at, chunk, other, x, out_bias, fc2_bias)


def norm_back_body(at, chunk, other, x, cot, gain, rows, out, sums):
    del at

    @pl.when(pl.program_id(0) == 0)
    def _():
        sums[...] = jnp.zeros_like(sums)

    grad = chunk[...] + other[...]
    normed, inv_std = norm_rows(x[...])
    sums[0:1, :] += jnp.sum(grad * normed, axis=0, keepdims=True)
    sums[1:2, :] += jnp.sum(grad, axis=0, keepdims=True)
    scaled = grad * gain[...]
    mean_scaled = jnp.mean(scaled, axis=-1, keepdims=True)
    mean_cross = jnp.mean(scaled * normed, axis=-1, keepdims=True)
    total = cot[...].astype(F32) + inv_std * (scaled - mean_scaled - normed * mean_cross)
    rows[...] = total
    out[...] = total


def input_grad_rows(at, chunk, other, x, cot, gain, step=48):
    count, width = chunk.shape
    parts = count // step
    here = pl.BlockSpec((step, width), lambda i, at: (i, 0))
    there = pl.BlockSpec((step, width), lambda i, at: (at[3] * parts + i, 0))
    return kernel(
        norm_back_body,
        (shape((count, width)), shape(x.shape), shape((2, width))),
        (parts,),
        [here, here, there, there, whole((1, width))],
        (here, there, whole((2, width))),
        scalars=1,
        us=5,
        vmem=16,
    )(at, chunk, other, x, cot, gain)


def place_body(at, *refs, starts, sizes, copies):
    i = pl.program_id(0)
    count = len(starts)
    pieces, out, extra = refs[:count], refs[count + 1], refs[count + 2 :]
    for piece, start, size in zip(pieces, starts, sizes):

        @pl.when((i >= start) & (i < start + size))
        def _(piece=piece):
            out[...] = piece[...]

    for copy, (which, first, size) in zip(extra, copies):
        begin = starts[which] + first

        @pl.when((i >= begin) & (i < begin + size))
        def _(copy=copy, which=which):
            copy[...] = pieces[which][...]


def place_rows(out, pieces, blocks, copies=(), step=48):
    width = out.shape[1]
    sizes = [piece.shape[0] // step for piece in pieces]
    starts = [sum(sizes[:k]) for k in range(len(sizes))]

    def part(start, size):
        return pl.BlockSpec((step, width), lambda i, at: (jnp.clip(i - start, 0, size - 1), 0))

    return kernel(
        partial(place_body, starts=starts, sizes=sizes, copies=copies),
        [shape(out.shape)] + [shape((size * step, width)) for _, _, size in copies],
        (sum(sizes),),
        [part(start, size) for start, size in zip(starts, sizes)]
        + [pl.BlockSpec(memory_space=ANY)],
        [pl.BlockSpec((step, width), lambda i, at: (at[i], 0))]
        + [part(starts[which] + first, size) for which, first, size in copies],
        scalars=1,
        aliases={1 + len(pieces): 0},
        us=5,
        vmem=16,
    )(blocks, *pieces, out)


class Order:
    def __init__(self):
        self.last = None

    def __call__(self, step, *args):
        if self.last is not None:
            args, _ = lax.optimization_barrier((args, self.last))
        out = step(*args)
        self.last = jax.tree.leaves(out)[0]
        return out

    def after(self, *arrays):
        arrays, _ = lax.optimization_barrier((arrays, self.last))
        return arrays

    def wait(self, array):
        array, self.last = lax.optimization_barrier((array, self.last))
        return array


ROW_GROUPS = [[x * Y * CORE + i for i in range(Y * CORE)] for x in range(X_LO)]


def scatter(part):
    return lax.psum_scatter(
        part, "dp", scatter_dimension=0, axis_index_groups=ROW_GROUPS, tiled=True
    )


def gather(piece):
    return lax.all_gather(piece, "dp", axis=0, axis_index_groups=ROW_GROUPS, tiled=True)


def per_device(
    layer_input,
    ln_gain,
    ln_bias,
    w_qkv,
    qkv_bias,
    w_out,
    out_bias,
    w_fc1,
    fc1_bias,
    w_fc2,
    fc2_bias,
    segments,
    positions,
    cotangent,
):
    width = layer_input.shape[1]
    inner, local = w_fc1.shape[1], w_qkv.shape[2]
    at = chunks_of(lax.axis_index("tensor") // X_HI)
    run = Order()
    w_parts = jnp.transpose(w_qkv, (1, 0, 2))
    blocks = at[:3, None] * 4 + jnp.arange(4, dtype=jnp.int32)[None, :]
    near, far = blocks[1:].reshape(-1), blocks[0]
    near_copies = ((0, 0, 2), (1, 2, 2))
    add = partial(sum_of, parts=1)

    ln, hidden, slope = run(
        ln_fc1, layer_input, ln_gain[None], ln_bias[None], w_fc1, fc1_bias[None]
    )
    grad_fc2, grad_context, sum_out = run(cot_products, hidden, cotangent, w_out)
    piece_fc2 = scatter(grad_fc2)
    qkv, *tables = run(project, ln, w_parts, qkv_bias[:, None], positions, rotary_rates())
    context, grad_proj, sum_proj = run(attention, qkv, grad_context, segments, tables)
    low, high, up, down, own = run(branch_sums, at, hidden, context, w_fc2, w_out)
    low, high = send(low, "z^1"), send(high, "z^3")
    grad_pre, sum_pre = run(grad_pre_act, cotangent, w_fc2, slope)
    side = run(side_grads, ln, cotangent, grad_pre, grad_proj, context)
    up, down = run(add_halves, up, down, high, low)
    piece_fc2 = run.wait(piece_fc2)
    (side,) = run.after(side)
    piece = scatter(side)
    up, down = run.after(up, down)
    from_up, from_down = send(up, "z^1"), send(down, "z^3")
    other_fc2 = send(*run.after(piece_fc2), "xlo")
    g_low, g_high, g_up, g_down, g_own = run(
        grad_ln_sums, at, grad_pre, grad_proj, w_fc1, w_parts
    )
    piece_fc2 = run(partial(sum_of, parts=4), piece_fc2, other_fc2)
    chunk = run(sum_of, own, from_up, from_down)
    (piece_fc2,) = run.after(piece_fc2)
    tot_fc2 = gather(piece_fc2)
    g_low, g_high, chunk = run.after(g_low, g_high, chunk)
    g_low, g_high = send(g_low, "z^1"), send(g_high, "z^3")
    other = send(chunk, "xhi")
    g_up, g_down = run(add_halves, g_up, g_down, g_high, g_low)
    g_from_up, g_from_down = send(g_up, "z^1"), send(g_down, "z^3")
    rows, output = run(
        output_rows, at, chunk, other, layer_input, out_bias[None], fc2_bias[None]
    )
    near_up, near_down = send(rows, "z^1"), send(rows, "z^3")
    g_chunk = run(sum_of, g_own, g_from_up, g_from_down)
    piece = run.wait(piece)
    other_piece = send(piece, "xlo")
    output, low, high = run(
        partial(place_rows, copies=near_copies), output, [near_up, near_down], near
    )
    piece = run(partial(sum_of, parts=8), piece, other_piece)
    side = gather(piece)
    g_chunk, low, high = run.after(g_chunk, low, high)
    g_other = send(g_chunk, "xhi")
    low, high = send(low, "z^3"), send(high, "z^1")
    tot_fc2 = run(copy_of, tot_fc2)
    (output,) = run(place_rows, output, [low, high], far)
    g_rows, grad_input, sums = run(
        input_grad_rows, at, g_chunk, g_other, layer_input, cotangent, ln_gain[None]
    )
    sums = sums.reshape(8, width // 4)
    sums = run(add, sums, send(sums, "z^1"))
    (g_rows,) = run.after(g_rows)
    g_near_up, g_near_down = send(g_rows, "z^1"), send(g_rows, "z^3")
    biases = jnp.concatenate(
        [sum_out[0], sum_pre[0], sum_proj.reshape(-1), jnp.zeros((256,), F32)]
    ).reshape(8, width // 4)
    sums = jnp.concatenate([sums, biases], axis=0)
    sums = run(add, sums, send(sums, "core"))
    sums = run(add, sums, send(sums, "y^1"))
    sums = run(add, sums, send(sums, "y^2"))
    sums = run(add, sums, send(sums, "xlo"))
    grad_input, g_low, g_high = run(
        partial(place_rows, copies=near_copies), grad_input, [g_near_up, g_near_down], near
    )
    norm_sums = sums[:8]
    norm_sums = run(add, norm_sums, send(norm_sums, "z^2"))
    g_low, g_high = send(g_low, "z^3"), send(g_high, "z^1")
    (grad_input,) = run(place_rows, grad_input, [g_low, g_high], far)
    tot_fc1, tot_qkv, tot_out = run(lambda side: split_grads(side, inner, local), side)

    sums = jnp.concatenate([norm_sums, sums[8:]], axis=0).reshape(-1)
    gain, shift, tot_out_bias, tot_fc1_bias, tot_qkv_bias = (
        sums[:width],
        sums[width : 2 * width],
        sums[2 * width : 3 * width],
        sums[3 * width : 3 * width + inner],
        sums[3 * width + inner : 3 * width + inner + 3 * local],
    )
    return (
        output,
        grad_input,
        gain,
        shift,
        jnp.transpose(tot_qkv, (1, 0, 2)),
        tot_qkv_bias.reshape(3, local),
        tot_out,
        tot_out_bias,
        tot_fc1,
        tot_fc1_bias,
        tot_fc2,
        tot_out_bias,
    )


def solution(mesh):
    in_specs = (
        P("dp", None),
        P(),
        P(),
        P(None, None, "tensor"),
        P(None, "tensor"),
        P("tensor", None),
        P(),
        P(None, "tensor"),
        P("tensor"),
        P("tensor", None),
        P(),
        P("dp", None),
        P("dp", None),
        P("dp", None),
    )
    out_specs = (
        P("dp", None),
        P("dp", None),
        P(),
        P(),
        P(None, None, "tensor"),
        P(None, "tensor"),
        P("tensor", None),
        P(),
        P(None, "tensor"),
        P("tensor"),
        P("tensor", None),
        P(),
    )
    return jax.shard_map(
        per_device, mesh=mesh, in_specs=in_specs, out_specs=out_specs, check_vma=False
    )
```

```python
from functools import partial

import jax
import jax.numpy as jnp
import numpy as np
from jax import lax
from jax.experimental import pallas as pl
from jax.experimental.pallas import tpu as pltpu
from jax.sharding import PartitionSpec as P

HEAD_DIM = 64
ROT = 32
EPSILON = 1e-05
MASKED = -1e30
F32, BF16 = jnp.float32, jnp.bfloat16
ANY = pl.ANY


def shape(dims, dtype=F32):
    return jax.ShapeDtypeStruct(dims, dtype)


def kernel(body, out, grid, in_specs, out_specs, scratch=(), scalars=0, aliases=None, vmem=40, us=3):
    return pl.pallas_call(
        body,
        out_shape=out,
        grid_spec=pltpu.PrefetchScalarGridSpec(
            num_scalar_prefetch=scalars,
            grid=grid,
            in_specs=in_specs,
            out_specs=out_specs,
            scratch_shapes=scratch,
        ),
        input_output_aliases=aliases or {},
        compiler_params=pltpu.CompilerParams(vmem_limit_bytes=vmem << 20),
        cost_estimate=pl.CostEstimate(
            flops=0, bytes_accessed=int(us * 3e6), transcendentals=0
        ),
    )


def whole(dims):
    return pl.BlockSpec(dims, lambda *_: (0,) * len(dims))


def dot(a, b):
    return jnp.dot(a, b, preferred_element_type=F32)


def dot_nt(a, b):
    return lax.dot_general(a, b, (((1,), (1,)), ((), ())), preferred_element_type=F32)


def dot_tn(a, b):
    return lax.dot_general(a, b, (((0,), (0,)), ((), ())), preferred_element_type=F32)


X_LO, Y, CORE = 2, 4, 2
Z, X_HI = 4, 2


def dp_moves(step):
    pairs = []
    for x in range(X_LO):
        for y in range(Y):
            for c in range(CORE):
                x2, y2, c2 = step(x, y, c)
                there = ((x2 % X_LO) * Y + y2 % Y) * CORE + c2 % CORE
                pairs.append(((x * Y + y) * CORE + c, there))
    return pairs


def tensor_moves(step):
    pairs = []
    for z in range(Z):
        for x in range(X_HI):
            z2, x2 = step(z, x)
            pairs.append((z * X_HI + x, (z2 % Z) * X_HI + x2 % X_HI))
    return pairs


MOVES = {
    "core": ("dp", dp_moves(lambda x, y, c: (x, y, c + 1))),
    "y^1": ("dp", dp_moves(lambda x, y, c: (x, y ^ 1, c))),
    "y^2": ("dp", dp_moves(lambda x, y, c: (x, y ^ 2, c))),
    "xlo": ("dp", dp_moves(lambda x, y, c: (x + 1, y, c))),
    "y^3": ("dp", dp_moves(lambda x, y, c: (x, y ^ 3, c))),
    "z^1": ("tensor", tensor_moves(lambda z, x: (z ^ 1, x))),
    "z^3": ("tensor", tensor_moves(lambda z, x: (z ^ 3, x))),
    "z^2": ("tensor", tensor_moves(lambda z, x: (z ^ 2, x))),
    "xhi": ("tensor", tensor_moves(lambda z, x: (z, x + 1))),
}


def send(array, move):
    axis, pairs = MOVES[move]
    return lax.ppermute(array, axis, pairs)


def norm_rows(x):
    center = x - jnp.mean(x, axis=-1, keepdims=True)
    inv_std = lax.rsqrt(jnp.mean(center * center, axis=-1, keepdims=True) + EPSILON)
    return center * inv_std, inv_std


def gelu_and_slope(v):
    a = np.float32(np.sqrt(2 / np.pi))
    b = np.float32(a * 0.044715)
    square = v * v
    h = 0.5 * jnp.tanh(v * (a + b * square)) + 0.5
    return v * h, h + v * (2 * a + 6 * b * square) * (h - h * h)


def ln_fc1_body(x_ref, gain_ref, bias_ref, w_ref, b_ref, low_ref, hidden_ref, slope_ref):
    i = pl.program_id(0)
    step = x_ref.shape[0]
    blocks = low_ref.shape[0] // step

    @pl.when(i < blocks)
    def _():
        normed, _ = norm_rows(x_ref[...])
        low = (normed * gain_ref[...] + bias_ref[...]).astype(BF16)
        low_ref[pl.ds(pl.multiple_of(i * step, step), step), :] = low

    @pl.when(i >= blocks)
    def _():
        hidden, slope = gelu_and_slope(dot(low_ref[...], w_ref[...]) + b_ref[...])
        hidden_ref[...] = hidden.astype(BF16)
        slope_ref[...] = slope.astype(BF16)


def ln_fc1(x, gain, bias, w, b, block=256, step=256):
    rows, width = x.shape
    cols = w.shape[1]
    blocks, tiles = rows // block, cols // step

    def tile(j):
        return jnp.maximum(j - blocks, 0)

    out = pl.BlockSpec((rows, step), lambda j: (0, tile(j)))
    return kernel(
        ln_fc1_body,
        (shape((rows, width), BF16), shape((rows, cols), BF16), shape((rows, cols), BF16)),
        (blocks + tiles,),
        [
            pl.BlockSpec((block, width), lambda j: (jnp.minimum(j, blocks - 1), 0)),
            whole((1, width)),
            whole((1, width)),
            pl.BlockSpec((width, step), lambda j: (0, tile(j))),
            pl.BlockSpec((1, step), lambda j: (0, tile(j))),
        ],
        (whole((rows, width)), out, out),
        us=13,
        vmem=60,
    )(x, gain, bias, w, b)


def grad_pre_body(cot_ref, w_ref, slope_ref, out_ref, sum_ref):
    grad = (dot_nt(cot_ref[...], w_ref[...]) * slope_ref[...]).astype(BF16)
    out_ref[...] = grad
    sum_ref[...] = jnp.sum(grad.astype(F32), axis=0, keepdims=True)


def grad_pre_act(cot, w, slope):
    rows, width = cot.shape
    cols, step = w.shape[0], 256
    tile = pl.BlockSpec((rows, step), lambda j: (0, j))
    return kernel(
        grad_pre_body,
        (shape((rows, cols), BF16), shape((1, cols))),
        (cols // step,),
        [whole((rows, width)), pl.BlockSpec((step, width), lambda j: (j, 0)), tile],
        (tile, pl.BlockSpec((1, step), lambda j: (0, j))),
        us=7,
        vmem=60,
    )(cot, w, slope)


def cot_products_body(
    left_ref, cot_ref, w_ref, out_ref, context_ref, sum_ref, turned, total
):
    j = pl.program_id(0)

    @pl.when(j == 0)
    def _():
        turned[...] = left_ref[...].T
        total[...] = jnp.zeros_like(total)

    cot = cot_ref[...]
    out_ref[...] = dot(turned[...], cot)
    total[...] += dot_nt(cot, w_ref[...])
    sum_ref[...] = jnp.sum(cot.astype(F32), axis=0, keepdims=True)

    @pl.when(j == pl.num_programs(0) - 1)
    def _():
        context_ref[...] = total[...].astype(BF16)


def cot_products(left, cot, w, step=512):
    rows, m = left.shape
    n, cols = cot.shape[1], w.shape[0]
    return kernel(
        cot_products_body,
        (shape((m, n)), shape((rows, cols), BF16), shape((1, n))),
        (n // step,),
        [
            whole((rows, m)),
            pl.BlockSpec((rows, step), lambda j: (0, j)),
            pl.BlockSpec((cols, step), lambda j: (0, j)),
        ],
        (
            pl.BlockSpec((m, step), lambda j: (0, j)),
            whole((rows, cols)),
            pl.BlockSpec((1, step), lambda j: (0, j)),
        ),
        scratch=[pltpu.VMEM((m, rows), BF16), pltpu.VMEM((rows, cols), F32)],
        us=9,
        vmem=60,
    )(left, cot, w)


def side_grads_body(ln_ref, cot_ref, pre_ref, proj_ref, context_ref, out_ref):
    n, step = pre_ref.shape[1], proj_ref.shape[2]
    turned = ln_ref[...].T
    out_ref[:, :n] = dot(turned, pre_ref[...])
    for c in range(3):
        out_ref[:, n + c * step : n + (c + 1) * step] = dot(turned, proj_ref[c])
    out_ref[:, n + 3 * step :] = dot(cot_ref[...].T, context_ref[...])


def side_grads(ln, cot, pre, proj, context, block=512):
    rows, m = ln.shape
    n, step = pre.shape[1], proj.shape[2]
    tile = pl.BlockSpec((rows, block), lambda j: (0, j))
    return kernel(
        side_grads_body,
        shape((m, n + 4 * step)),
        (m // block,),
        [tile, tile, whole((rows, n)), whole((3, rows, step)), whole((rows, step))],
        pl.BlockSpec((block, n + 4 * step), lambda j: (j, 0)),
        us=13,
        vmem=60,
    )(ln, cot, pre, proj, context)


def split_body(side, one, three, turned):
    n, step = one.shape[1], three.shape[2]
    one[...] = side[:, :n]
    for c in range(3):
        three[c] = side[:, n + c * step : n + (c + 1) * step]
    turned[...] = side[:, n + 3 * step :].T


def split_grads(side, n, step, tile=512):
    rows = side.shape[0]
    return kernel(
        split_body,
        (shape((rows, n)), shape((3, rows, step)), shape((step, rows))),
        (rows // tile,),
        [pl.BlockSpec((tile, side.shape[1]), lambda i: (i, 0))],
        (
            pl.BlockSpec((tile, n), lambda i: (i, 0)),
            pl.BlockSpec((3, tile, step), lambda i: (0, i, 0)),
            pl.BlockSpec((step, tile), lambda i: (0, i)),
        ),
        us=12,
        vmem=40,
    )(side)


def copy_body(source, out):
    out[...] = source[...]


def copy_of(source, step=256):
    rows, width = source.shape
    spec = pl.BlockSpec((step, width), lambda i: (i, 0))
    return kernel(
        copy_body, shape((rows, width)), (rows // step,), [spec], spec, us=6, vmem=60    )(source)


def swap_halves(u, low, high):
    width = u.shape[1]
    return pltpu.roll(u, width - ROT // 2, 1) * low + pltpu.roll(u, ROT // 2, 1) * high


def fill_tables(pos_ref, rate_ref, cos_ref, low_ref, high_ref):
    angles = rate_ref[...] * pos_ref[...].astype(F32)
    count = ROT // 2
    entry = lax.broadcasted_iota(jnp.int32, (count, 2 * HEAD_DIM), 0)
    lane = lax.broadcasted_iota(jnp.int32, (count, 2 * HEAD_DIM), 1) % HEAD_DIM
    first = jnp.where(lane == entry, 1.0, 0.0).astype(F32)
    second = jnp.where(lane == entry + count, 1.0, 0.0).astype(F32)

    def spread(table, lanes):
        return lax.dot_general(
            table, lanes, (((0,), (0,)), ((), ())),
            precision=lax.Precision.HIGHEST, preferred_element_type=F32,
        )

    sine = jnp.sin(angles)
    kept = jnp.where(lane[:1] >= ROT, 1.0, 0.0)
    cos_ref[...] = spread(jnp.cos(angles), first + second) + kept
    low_ref[...] = spread(sine, -first)
    high_ref[...] = spread(sine, second)


def rotary_rates():
    steps_half = jnp.arange(0, ROT, 2).astype(F32) / ROT
    return (10000.0 ** (-steps_half))[:, None]


def qkv_body(ln_ref, w_ref, b_ref, pos_ref, rate_ref, out_ref, cos_ref, low_ref, high_ref):
    c = pl.program_id(0)

    @pl.when(c == 0)
    def _():
        fill_tables(pos_ref, rate_ref, cos_ref, low_ref, high_ref)

    u = dot(ln_ref[...], w_ref[0]) + b_ref[pl.ds(c, 1), :]

    @pl.when(c == 2)
    def _():
        out_ref[0] = u.astype(BF16)

    @pl.when(c < 2)
    def _():
        for lane in range(0, u.shape[1], 128):
            part = u[:, lane : lane + 128]
            turned = part * cos_ref[...] + swap_halves(part, low_ref[...], high_ref[...])
            out_ref[0, :, lane : lane + 128] = turned.astype(BF16)


def project(ln, w_parts, bias, positions, rates):
    rows, width = ln.shape
    cols = w_parts.shape[2]
    return kernel(
        qkv_body,
        (shape((3, rows, cols), BF16),) + (shape((rows, 128)),) * 3,
        (3,),
        [
            whole((rows, width)),
            pl.BlockSpec((1, width, cols), lambda c: (c, 0, 0)),
            whole((3, cols)),
            whole((1, rows)),
            whole((ROT // 2, 1)),
        ],
        (pl.BlockSpec((1, rows, cols), lambda c: (c, 0, 0)),) + (whole((rows, 128)),) * 3,
        us=7,
        vmem=60,
    )(ln, w_parts, bias, positions, rates)


def attention_body(
    q_ref, k_ref, v_ref, g_ref, seg_ref, cos_ref, low_ref, high_ref,
    context_ref, grad_ref, sum_ref, dq, dk, dv,
):
    rows = q_ref.shape[1]
    step = 384
    scale = np.float32(HEAD_DIM**-0.5)
    lane = lax.broadcasted_iota(jnp.int32, (rows, 128), 1)
    heads = []
    for h in range(2):
        mine = (lane >= h * HEAD_DIM) & (lane < (h + 1) * HEAD_DIM)
        heads.append(
            [
                jnp.where(mine, ref, jnp.zeros_like(ref))
                for ref in (q_ref[0] * scale.astype(BF16), k_ref[0], v_ref[0], g_ref[...])
            ]
        )
    seg_row = seg_ref[...].astype(F32)
    seg_col = jnp.broadcast_to(seg_row, (128, rows)).T[:, :1]
    dk[...] = jnp.zeros_like(dk)
    dv[...] = jnp.zeros_like(dv)
    for i in range(rows // step):
        top = slice(i * step, (i + 1) * step)
        seen = (i + 1) * step
        row = lax.broadcasted_iota(jnp.int32, (step, seen), 0) + i * step
        col = lax.broadcasted_iota(jnp.int32, (step, seen), 1)
        allowed = (seg_col[top, :] == seg_row[:, :seen]) & (col <= row)
        context = jnp.zeros((step, 128), F32)
        grad_q = jnp.zeros((step, 128), F32)
        for q, k, v, g in heads:
            scores = jnp.where(allowed, dot_nt(q[top], k[:seen]), MASKED)
            peak = jnp.max(scores, axis=-1, keepdims=True)
            raised = jnp.exp(scores - peak)
            probs = raised * (1.0 / jnp.sum(raised, axis=-1, keepdims=True))
            probs_low = probs.astype(BF16)
            context += dot(probs_low, v[:seen])
            grad_probs = dot_nt(g[top], v[:seen])
            delta = jnp.sum(probs * grad_probs, axis=-1, keepdims=True)
            grad_scores = (probs * (grad_probs - delta)).astype(BF16)
            grad_q += dot(grad_scores, k[:seen])
            dk[:seen, :] += dot_tn(grad_scores, q[top])
            dv[:seen, :] += dot_tn(probs_low, g[top])
        context_ref[top, :] = context.astype(BF16)
        dq[top, :] = grad_q * scale
    for c, grad in enumerate((dq, dk, dv)):
        u = grad[...]
        if c < 2:
            u = u * cos_ref[...] - swap_halves(u, low_ref[...], high_ref[...])
        u = u.astype(BF16)
        grad_ref[c] = u
        sum_ref[c] = jnp.sum(u.astype(F32), axis=0, keepdims=True)


def attention(qkv, grad_context, segments, tables):
    _, rows, cols = qkv.shape
    pair = pl.BlockSpec((rows, 128), lambda p: (0, p))
    return kernel(
        attention_body,
        (shape((rows, cols), BF16), shape((3, rows, cols), BF16), shape((3, 1, cols))),
        (cols // 128,),
        [pl.BlockSpec((1, rows, 128), lambda p, c=c: (c, 0, p)) for c in range(3)]
        + [pair, whole((1, rows))]
        + [whole((rows, 128))] * 3,
        (
            pair,
            pl.BlockSpec((3, rows, 128), lambda p: (0, 0, p)),
            pl.BlockSpec((3, 1, 128), lambda p: (0, 0, p)),
        ),
        scratch=[pltpu.VMEM((rows, 128), F32)] * 3,
        us=12,
        vmem=60,
    )(qkv, qkv, qkv, grad_context, segments, *tables)


def chunks_of(z):
    return jnp.stack([z ^ 2, z ^ 1, z ^ 3, z]).astype(jnp.int32)


def put_chunks(outs, total):
    row = 0
    for out in outs:
        out[...] = total[row : row + out.shape[0], :]
        row += out.shape[0]


def chunk_rows(count):
    return [count // 2, count // 2, count, count, count]


def branch_body(at, *refs):
    lefts, rights = refs[:8], refs[8:10]
    outs, hidden, context = refs[10:15], refs[15], refs[16]
    count = outs[-1].shape[0]

    @pl.when(pl.program_id(0) == 0)
    def _():
        for i in range(4):
            hidden[i * count : (i + 1) * count, :] = lefts[i][...]
            context[i * count : (i + 1) * count, :] = lefts[4 + i][...]

    total = dot(hidden[...], rights[0][...]) + dot(context[...], rights[1][...])
    put_chunks(outs, total)


def branch_sums(at, hidden, context, w_fc2, w_out, step=512):
    rows, inner = hidden.shape
    heads = context.shape[1]
    width = w_fc2.shape[1]
    count = rows // 4

    def chunk(cols, i):
        return pl.BlockSpec((count, cols), lambda j, at, i=i: (at[i], 0))

    return kernel(
        branch_body,
        [shape((n, width)) for n in chunk_rows(count)],
        (width // step,),
        [chunk(inner, i) for i in range(4)]
        + [chunk(heads, i) for i in range(4)]
        + [
            pl.BlockSpec((inner, step), lambda j, at: (0, j)),
            pl.BlockSpec((heads, step), lambda j, at: (0, j)),
        ],
        [pl.BlockSpec((n, step), lambda j, at: (0, j)) for n in chunk_rows(count)],
        scratch=[pltpu.VMEM((rows, inner), BF16), pltpu.VMEM((rows, heads), BF16)],
        scalars=1,
        us=9,
        vmem=60,
    )(at, *[hidden] * 4, *[context] * 4, w_fc2, w_out)


def grad_ln_body(at, *refs):
    lefts, rights = refs[:8], refs[8:10]
    outs, pre, proj = refs[10:15], refs[15], refs[16]
    count = outs[-1].shape[0]

    @pl.when(pl.program_id(0) == 0)
    def _():
        for i in range(4):
            pre[i * count : (i + 1) * count, :] = lefts[i][...]
            for c in range(3):
                proj[c, i * count : (i + 1) * count, :] = lefts[4 + i][c]

    total = dot_nt(pre[...], rights[0][...])
    for c in range(3):
        total += dot_nt(proj[c], rights[1][c])
    put_chunks(outs, total)


def grad_ln_sums(at, pre, proj, w_fc1, w_parts, step=512):
    rows, inner = pre.shape
    heads = proj.shape[2]
    width = w_fc1.shape[0]
    count = rows // 4
    return kernel(
        grad_ln_body,
        [shape((n, width)) for n in chunk_rows(count)],
        (width // step,),
        [pl.BlockSpec((count, inner), lambda j, at, i=i: (at[i], 0)) for i in range(4)]
        + [pl.BlockSpec((3, count, heads), lambda j, at, i=i: (0, at[i], 0)) for i in range(4)]
        + [
            pl.BlockSpec((step, inner), lambda j, at: (j, 0)),
            pl.BlockSpec((3, step, heads), lambda j, at: (0, j, 0)),
        ],
        [pl.BlockSpec((n, step), lambda j, at: (0, j)) for n in chunk_rows(count)],
        scratch=[pltpu.VMEM((rows, inner), BF16), pltpu.VMEM((3, rows, heads), BF16)],
        scalars=1,
        us=11,
        vmem=60,
    )(at, *[pre] * 4, *[proj] * 4, w_fc1, w_parts)


def add_pair_body(up_in, down_in, high, low, up, down):
    up[...] = up_in[...] + high[...]
    down[...] = down_in[...] + low[...]


def add_halves(up, down, high, low, parts=2):
    rows, width = low.shape
    step = rows // parts
    first = pl.BlockSpec((step, width), lambda i: (i, 0))
    second = pl.BlockSpec((step, width), lambda i: (i + parts, 0))
    return kernel(
        add_pair_body,
        (shape(up.shape), shape(down.shape)),
        (parts,),
        [second, first, first, first],
        (second, first),
        aliases={0: 0, 1: 1},
        us=2,
        vmem=16,
    )(up, down, high, low)


def sum_body(*refs):
    total = refs[0][...]
    for ref in refs[1:-1]:
        total = total + ref[...]
    refs[-1][...] = total


def sum_of(*arrays, parts=3):
    rows, width = arrays[0].shape
    step = rows // parts
    spec = pl.BlockSpec((step, width), lambda i: (i, 0))
    return kernel(
        sum_body, shape((rows, width)), (rows // step,), [spec] * len(arrays), spec,
        us=3,
        vmem=16,
    )(*arrays)


def take_body(at, x, cot, x_out, cot_out):
    del at
    x_out[...] = x[...]
    cot_out[...] = cot[...]


def take_rows(at, x, cot, step=48):
    count, width = x.shape[0] // 4, x.shape[1]
    parts = count // step
    here = pl.BlockSpec((step, width), lambda i, at: (i, 0))
    there = pl.BlockSpec((step, width), lambda i, at: (at[3] * parts + i, 0))
    return kernel(
        take_body,
        (shape((count, width)), shape((count, width), BF16)),
        (parts,),
        [there, there],
        (here, here),
        scalars=1,
        us=3,
        vmem=60,
    )(at, x, cot)


def last_body(at, chunk, other, x, ob, fb, rows, out):
    del at
    total = chunk[...] + other[...] + x[...] + ob[...] + fb[...]
    rows[...] = total
    out[...] = total


def output_rows(at, chunk, other, x, out_bias, fc2_bias, step=48):
    count, width = chunk.shape
    parts = count // step
    here = pl.BlockSpec((step, width), lambda i, at: (i, 0))
    there = pl.BlockSpec((step, width), lambda i, at: (at[3] * parts + i, 0))
    return kernel(
        last_body,
        (shape((count, width)), shape((4 * count, width))),
        (parts,),
        [here, here, here, whole((1, width)), whole((1, width))],
        (here, there),
        scalars=1,
        us=4,
        vmem=16,
    )(at, chunk, other, x, out_bias, fc2_bias)


def norm_back_body(at, chunk, other, x, cot, gain, rows, out, sums):
    del at

    @pl.when(pl.program_id(0) == 0)
    def _():
        sums[...] = jnp.zeros_like(sums)

    grad = chunk[...] + other[...]
    normed, inv_std = norm_rows(x[...])
    sums[0:1, :] += jnp.sum(grad * normed, axis=0, keepdims=True)
    sums[1:2, :] += jnp.sum(grad, axis=0, keepdims=True)
    scaled = grad * gain[...]
    mean_scaled = jnp.mean(scaled, axis=-1, keepdims=True)
    mean_cross = jnp.mean(scaled * normed, axis=-1, keepdims=True)
    total = cot[...].astype(F32) + inv_std * (scaled - mean_scaled - normed * mean_cross)
    rows[...] = total
    out[...] = total


def input_grad_rows(at, chunk, other, x, cot, gain, step=48):
    count, width = chunk.shape
    parts = count // step
    here = pl.BlockSpec((step, width), lambda i, at: (i, 0))
    there = pl.BlockSpec((step, width), lambda i, at: (at[3] * parts + i, 0))
    return kernel(
        norm_back_body,
        (shape((count, width)), shape((4 * count, width)), shape((2, width))),
        (parts,),
        [here, here, here, here, whole((1, width))],
        (here, there, whole((2, width))),
        scalars=1,
        us=5,
        vmem=16,
    )(at, chunk, other, x, cot, gain)


def place_body(at, *refs, starts, sizes, copies):
    i = pl.program_id(0)
    count = len(starts)
    pieces, out, extra = refs[:count], refs[count + 1], refs[count + 2 :]
    for piece, start, size in zip(pieces, starts, sizes):

        @pl.when((i >= start) & (i < start + size))
        def _(piece=piece):
            out[...] = piece[...]

    for copy, (which, first, size) in zip(extra, copies):
        begin = starts[which] + first

        @pl.when((i >= begin) & (i < begin + size))
        def _(copy=copy, which=which):
            copy[...] = pieces[which][...]


def place_rows(out, pieces, blocks, copies=(), step=48):
    width = out.shape[1]
    sizes = [piece.shape[0] // step for piece in pieces]
    starts = [sum(sizes[:k]) for k in range(len(sizes))]

    def part(start, size):
        return pl.BlockSpec((step, width), lambda i, at: (jnp.clip(i - start, 0, size - 1), 0))

    return kernel(
        partial(place_body, starts=starts, sizes=sizes, copies=copies),
        [shape(out.shape)] + [shape((size * step, width)) for _, _, size in copies],
        (sum(sizes),),
        [part(start, size) for start, size in zip(starts, sizes)]
        + [pl.BlockSpec(memory_space=ANY)],
        [pl.BlockSpec((step, width), lambda i, at: (at[i], 0))]
        + [part(starts[which] + first, size) for which, first, size in copies],
        scalars=1,
        aliases={1 + len(pieces): 0},
        us=5,
        vmem=16,
    )(blocks, *pieces, out)


class Order:
    def __init__(self):
        self.last = None

    def __call__(self, step, *args):
        if self.last is not None:
            args, _ = lax.optimization_barrier((args, self.last))
        out = step(*args)
        self.last = jax.tree.leaves(out)[0]
        return out

    def after(self, *arrays):
        arrays, _ = lax.optimization_barrier((arrays, self.last))
        return arrays

    def wait(self, array):
        array, self.last = lax.optimization_barrier((array, self.last))
        return array


ROW_GROUPS = [[x * Y * CORE + i for i in range(Y * CORE)] for x in range(X_LO)]


def scatter(part):
    return lax.psum_scatter(
        part, "dp", scatter_dimension=0, axis_index_groups=ROW_GROUPS, tiled=True
    )


def gather(piece):
    return lax.all_gather(piece, "dp", axis=0, axis_index_groups=ROW_GROUPS, tiled=True)


def per_device(
    layer_input,
    ln_gain,
    ln_bias,
    w_qkv,
    qkv_bias,
    w_out,
    out_bias,
    w_fc1,
    fc1_bias,
    w_fc2,
    fc2_bias,
    segments,
    positions,
    cotangent,
):
    width = layer_input.shape[1]
    inner, local = w_fc1.shape[1], w_qkv.shape[2]
    at = chunks_of(lax.axis_index("tensor") // X_HI)
    run = Order()
    w_parts = jnp.transpose(w_qkv, (1, 0, 2))
    blocks = at[:3, None] * 4 + jnp.arange(4, dtype=jnp.int32)[None, :]
    near, far = blocks[1:].reshape(-1), blocks[0]
    near_copies = ((0, 0, 2), (1, 2, 2))
    add = partial(sum_of, parts=1)

    ln, hidden, slope = run(
        ln_fc1, layer_input, ln_gain[None], ln_bias[None], w_fc1, fc1_bias[None]
    )
    grad_fc2, grad_context, sum_out = run(cot_products, hidden, cotangent, w_out)
    piece_fc2 = scatter(grad_fc2)
    qkv, *tables = run(project, ln, w_parts, qkv_bias, positions, rotary_rates())
    context, grad_proj, sum_proj = run(attention, qkv, grad_context, segments, tables)
    low, high, up, down, own = run(branch_sums, at, hidden, context, w_fc2, w_out)
    low, high = send(low, "z^1"), send(high, "z^3")
    grad_pre, sum_pre = run(grad_pre_act, cotangent, w_fc2, slope)
    side = run(side_grads, ln, cotangent, grad_pre, grad_proj, context)
    low, high = run.wait(low), run.wait(high)
    piece_fc2 = run.wait(piece_fc2)
    (side,) = run.after(side)
    piece = scatter(side)
    other_fc2 = send(*run.after(piece_fc2), "xlo")
    up, down = run(add_halves, up, down, high, low)
    from_up, from_down = send(up, "z^1"), send(down, "z^3")
    g_low, g_high, g_up, g_down, g_own = run(
        grad_ln_sums, at, grad_pre, grad_proj, w_fc1, w_parts
    )
    g_low, g_high = send(g_low, "z^1"), send(g_high, "z^3")
    piece_fc2 = run(partial(sum_of, parts=4), piece_fc2, other_fc2)
    chunk = run(sum_of, own, from_up, from_down)
    other = send(chunk, "xhi")
    g_up, g_down = run(add_halves, g_up, g_down, g_high, g_low)
    g_from_up, g_from_down = send(g_up, "z^1"), send(g_down, "z^3")
    x_rows, cot_rows = run(take_rows, at, layer_input, cotangent)
    rows, output = run(output_rows, at, chunk, other, x_rows, out_bias[None], fc2_bias[None])
    g_chunk = run(sum_of, g_own, g_from_up, g_from_down)
    piece = run.wait(piece)
    (piece_fc2,) = run.after(piece_fc2)
    tot_fc2 = gather(piece_fc2)
    rows, piece = run.after(rows, piece)
    other_piece = send(piece, "xlo")
    near_up, near_down = send(rows, "z^1"), send(rows, "z^3")
    output, low, high = run(
        partial(place_rows, copies=near_copies), output, [near_up, near_down], near
    )
    piece = run(partial(sum_of, parts=4), piece, other_piece)
    side = gather(piece)
    g_chunk, low, high = run.after(g_chunk, low, high)
    g_other = send(g_chunk, "xhi")
    low, high = send(low, "z^3"), send(high, "z^1")
    tot_fc2 = run(copy_of, tot_fc2)
    (output,) = run(place_rows, output, [low, high], far)
    g_rows, grad_input, sums = run(
        input_grad_rows, at, g_chunk, g_other, x_rows, cot_rows, ln_gain[None]
    )
    g_near_up, g_near_down = send(g_rows, "z^1"), send(g_rows, "z^3")
    biases = jnp.concatenate(
        [sum_out[0], sum_pre[0], sum_proj.reshape(-1), jnp.zeros((256,), F32)]
    ).reshape(8, width // 4)
    sums = jnp.concatenate([sums.reshape(8, width // 4), biases], axis=0)
    for move in ("core", "y^1", "y^2", "xlo"):
        sums = run(add, sums, send(sums, move))
    norm_sums = sums[:8]
    other_sums = send(norm_sums, "z^1")
    grad_input, g_low, g_high = run(
        partial(place_rows, copies=near_copies), grad_input, [g_near_up, g_near_down], near
    )
    g_low, g_high = send(g_low, "z^3"), send(g_high, "z^1")
    norm_sums = run(add, norm_sums, other_sums)
    other_sums = send(norm_sums, "z^2")
    tot_fc1, tot_qkv, tot_out = run(lambda side: split_grads(side, inner, local), side)
    norm_sums = run(add, norm_sums, other_sums)
    (grad_input,) = run(place_rows, grad_input, [g_low, g_high], far)

    sums = jnp.concatenate([norm_sums, sums[8:]], axis=0).reshape(-1)
    gain, shift, tot_out_bias, tot_fc1_bias, tot_qkv_bias = (
        sums[:width],
        sums[width : 2 * width],
        sums[2 * width : 3 * width],
        sums[3 * width : 3 * width + inner],
        sums[3 * width + inner : 3 * width + inner + 3 * local],
    )
    return (
        output,
        grad_input,
        gain,
        shift,
        jnp.transpose(tot_qkv, (1, 0, 2)),
        tot_qkv_bias.reshape(3, local),
        tot_out,
        tot_out_bias,
        tot_fc1,
        tot_fc1_bias,
        tot_fc2,
        tot_out_bias,
    )


def solution(mesh):
    in_specs = (
        P("dp", None),
        P(),
        P(),
        P(None, None, "tensor"),
        P(None, "tensor"),
        P("tensor", None),
        P(),
        P(None, "tensor"),
        P("tensor"),
        P("tensor", None),
        P(),
        P("dp", None),
        P("dp", None),
        P("dp", None),
    )
    out_specs = (
        P("dp", None),
        P("dp", None),
        P(),
        P(),
        P(None, None, "tensor"),
        P(None, "tensor"),
        P("tensor", None),
        P(),
        P(None, "tensor"),
        P("tensor"),
        P("tensor", None),
        P(),
    )
    return jax.shard_map(
        per_device, mesh=mesh, in_specs=in_specs, out_specs=out_specs, check_vma=False
    )
```

```python
from functools import partial

import jax
import jax.numpy as jnp
import numpy as np
from jax import lax
from jax.experimental import pallas as pl
from jax.experimental.pallas import tpu as pltpu
from jax.sharding import PartitionSpec as P

HEAD_DIM = 64
ROT = 32
EPSILON = 1e-05
MASKED = -1e30
F32, BF16 = jnp.float32, jnp.bfloat16
ANY = pl.ANY


def shape(dims, dtype=F32):
    return jax.ShapeDtypeStruct(dims, dtype)


def kernel(body, out, grid, in_specs, out_specs, scratch=(), scalars=0, aliases=None, vmem=40, us=3):
    return pl.pallas_call(
        body,
        out_shape=out,
        grid_spec=pltpu.PrefetchScalarGridSpec(
            num_scalar_prefetch=scalars,
            grid=grid,
            in_specs=in_specs,
            out_specs=out_specs,
            scratch_shapes=scratch,
        ),
        input_output_aliases=aliases or {},
        compiler_params=pltpu.CompilerParams(vmem_limit_bytes=vmem << 20),
        cost_estimate=pl.CostEstimate(
            flops=0, bytes_accessed=int(us * 3e6), transcendentals=0
        ),
    )


def whole(dims):
    return pl.BlockSpec(dims, lambda *_: (0,) * len(dims))


def dot(a, b):
    return jnp.dot(a, b, preferred_element_type=F32)


def dot_nt(a, b):
    return lax.dot_general(a, b, (((1,), (1,)), ((), ())), preferred_element_type=F32)


def dot_tn(a, b):
    return lax.dot_general(a, b, (((0,), (0,)), ((), ())), preferred_element_type=F32)


X_LO, Y, CORE = 2, 4, 2
Z, X_HI = 4, 2


def dp_moves(step):
    pairs = []
    for x in range(X_LO):
        for y in range(Y):
            for c in range(CORE):
                x2, y2, c2 = step(x, y, c)
                there = ((x2 % X_LO) * Y + y2 % Y) * CORE + c2 % CORE
                pairs.append(((x * Y + y) * CORE + c, there))
    return pairs


def tensor_moves(step):
    pairs = []
    for z in range(Z):
        for x in range(X_HI):
            z2, x2 = step(z, x)
            pairs.append((z * X_HI + x, (z2 % Z) * X_HI + x2 % X_HI))
    return pairs


MOVES = {
    "core": ("dp", dp_moves(lambda x, y, c: (x, y, c + 1))),
    "y^1": ("dp", dp_moves(lambda x, y, c: (x, y ^ 1, c))),
    "y^2": ("dp", dp_moves(lambda x, y, c: (x, y ^ 2, c))),
    "xlo": ("dp", dp_moves(lambda x, y, c: (x + 1, y, c))),
    "y^3": ("dp", dp_moves(lambda x, y, c: (x, y ^ 3, c))),
    "z^1": ("tensor", tensor_moves(lambda z, x: (z ^ 1, x))),
    "z^3": ("tensor", tensor_moves(lambda z, x: (z ^ 3, x))),
    "z^2": ("tensor", tensor_moves(lambda z, x: (z ^ 2, x))),
    "xhi": ("tensor", tensor_moves(lambda z, x: (z, x + 1))),
}


def send(array, move):
    axis, pairs = MOVES[move]
    return lax.ppermute(array, axis, pairs)


def norm_rows(x):
    center = x - jnp.mean(x, axis=-1, keepdims=True)
    inv_std = lax.rsqrt(jnp.mean(center * center, axis=-1, keepdims=True) + EPSILON)
    return center * inv_std, inv_std


def gelu_and_slope(v):
    a = np.float32(np.sqrt(2 / np.pi))
    b = np.float32(a * 0.044715)
    square = v * v
    h = 0.5 * jnp.tanh(v * (a + b * square)) + 0.5
    return v * h, h + v * (2 * a + 6 * b * square) * (h - h * h)


def first_body(
    x_ref, gain_ref, bias_ref, w_ref, b_ref, cot_ref, wo_ref,
    low_ref, hidden_ref, slope_ref, grad_ref, context_ref, sum_ref, turned, total,
):
    i = pl.program_id(0)
    block, step = x_ref.shape[0], w_ref.shape[1]
    blocks, tiles = low_ref.shape[0] // block, turned.shape[0] // step

    @pl.when(i < blocks)
    def _():
        normed, _ = norm_rows(x_ref[...])
        low = (normed * gain_ref[...] + bias_ref[...]).astype(BF16)
        low_ref[pl.ds(pl.multiple_of(i * block, block), block), :] = low

    @pl.when((i >= blocks) & (i < blocks + tiles))
    def _():
        hidden, slope = gelu_and_slope(dot(low_ref[...], w_ref[...]) + b_ref[...])
        hidden = hidden.astype(BF16)
        hidden_ref[...] = hidden
        turned[pl.ds(pl.multiple_of((i - blocks) * step, step), step), :] = hidden.T
        slope_ref[...] = slope.astype(BF16)

    @pl.when(i == blocks + tiles)
    def _():
        total[...] = jnp.zeros_like(total)

    @pl.when(i >= blocks + tiles)
    def _():
        cot = cot_ref[...]
        grad_ref[...] = dot(turned[...], cot)
        total[...] += dot_nt(cot, wo_ref[...])
        sum_ref[...] = jnp.sum(cot.astype(F32), axis=0, keepdims=True)

    @pl.when(i == pl.num_programs(0) - 1)
    def _():
        context_ref[...] = total[...].astype(BF16)


def first_products(x, gain, bias, w, b, cot, w_out, block=256, step=256, wide=512):
    rows, width = x.shape
    cols, heads = w.shape[1], w_out.shape[0]
    blocks, tiles, last = rows // block, cols // step, width // wide

    def tile(j):
        return jnp.clip(j - blocks, 0, tiles - 1)

    def final(j):
        return jnp.maximum(j - blocks - tiles, 0)

    out = pl.BlockSpec((rows, step), lambda j: (0, tile(j)))
    return kernel(
        first_body,
        (
            shape((rows, width), BF16),
            shape((rows, cols), BF16),
            shape((rows, cols), BF16),
            shape((cols, width)),
            shape((rows, heads), BF16),
            shape((1, width)),
        ),
        (blocks + tiles + last,),
        [
            pl.BlockSpec((block, width), lambda j: (jnp.minimum(j, blocks - 1), 0)),
            whole((1, width)),
            whole((1, width)),
            pl.BlockSpec((width, step), lambda j: (0, tile(j))),
            pl.BlockSpec((1, step), lambda j: (0, tile(j))),
            pl.BlockSpec((rows, wide), lambda j: (0, final(j))),
            pl.BlockSpec((heads, wide), lambda j: (0, final(j))),
        ],
        (
            whole((rows, width)),
            out,
            out,
            pl.BlockSpec((cols, wide), lambda j: (0, final(j))),
            whole((rows, heads)),
            pl.BlockSpec((1, wide), lambda j: (0, final(j))),
        ),
        scratch=[pltpu.VMEM((cols, rows), BF16), pltpu.VMEM((rows, heads), F32)],
        us=20,
        vmem=60,
    )(x, gain, bias, w, b, cot, w_out)


def side_body(
    ln_ref, cot_ref, w_ref, slope_ref, proj_ref, context_ref, out_ref, pre_ref, sum_ref
):
    i = pl.program_id(0)
    tile, step = w_ref.shape[0], proj_ref.shape[2]
    n, block = pre_ref.shape[1], ln_ref.shape[1]
    tiles = n // tile

    @pl.when(i < tiles)
    def _():
        grad = (dot_nt(cot_ref[...], w_ref[...]) * slope_ref[...]).astype(BF16)
        pre_ref[:, pl.ds(pl.multiple_of(i * tile, tile), tile)] = grad
        sum_ref[...] = jnp.sum(grad.astype(F32), axis=0, keepdims=True)

    @pl.when(i >= tiles)
    def _():
        turned = ln_ref[...].T
        out_ref[:, :n] = dot(turned, pre_ref[...])
        for c in range(3):
            out_ref[:, n + c * step : n + (c + 1) * step] = dot(turned, proj_ref[c])
        cot = cot_ref[:, pl.ds(pl.multiple_of((i - tiles) * block, block), block)]
        out_ref[:, n + 3 * step :] = dot(cot.T, context_ref[...])


def side_grads(ln, cot, w, slope, proj, context, block=512, tile=256):
    rows, m = ln.shape
    n, step = w.shape[0], proj.shape[2]
    tiles = n // tile

    def first(j):
        return jnp.minimum(j, tiles - 1)

    def second(j):
        return jnp.maximum(j - tiles, 0)

    return kernel(
        side_body,
        (shape((m, n + 4 * step)), shape((rows, n), BF16), shape((1, n))),
        (tiles + m // block,),
        [
            pl.BlockSpec((rows, block), lambda j: (0, second(j))),
            whole((rows, m)),
            pl.BlockSpec((tile, m), lambda j: (first(j), 0)),
            pl.BlockSpec((rows, tile), lambda j: (0, first(j))),
            whole((3, rows, step)),
            whole((rows, step)),
        ],
        (
            pl.BlockSpec((block, n + 4 * step), lambda j: (second(j), 0)),
            whole((rows, n)),
            pl.BlockSpec((1, tile), lambda j: (0, first(j))),
        ),
        us=18,
        vmem=60,
    )(ln, cot, w, slope, proj, context)


def split_body(side, one, three, turned):
    n, step = one.shape[1], three.shape[2]
    one[...] = side[:, :n]
    for c in range(3):
        three[c] = side[:, n + c * step : n + (c + 1) * step]
    turned[...] = side[:, n + 3 * step :].T


def split_grads(side, n, step, tile=512):
    rows = side.shape[0]
    return kernel(
        split_body,
        (shape((rows, n)), shape((3, rows, step)), shape((step, rows))),
        (rows // tile,),
        [pl.BlockSpec((tile, side.shape[1]), lambda i: (i, 0))],
        (
            pl.BlockSpec((tile, n), lambda i: (i, 0)),
            pl.BlockSpec((3, tile, step), lambda i: (0, i, 0)),
            pl.BlockSpec((step, tile), lambda i: (0, i)),
        ),
        us=12,
        vmem=40,
    )(side)


def copy_body(source, out):
    out[...] = source[...]


def copy_of(source, step=256):
    rows, width = source.shape
    spec = pl.BlockSpec((step, width), lambda i: (i, 0))
    return kernel(
        copy_body, shape((rows, width)), (rows // step,), [spec], spec, us=6, vmem=60    )(source)


def swap_halves(u, low, high):
    width = u.shape[1]
    return pltpu.roll(u, width - ROT // 2, 1) * low + pltpu.roll(u, ROT // 2, 1) * high


def fill_tables(pos_ref, rate_ref, cos_ref, low_ref, high_ref):
    angles = rate_ref[...] * pos_ref[...].astype(F32)
    count = ROT // 2
    entry = lax.broadcasted_iota(jnp.int32, (count, 2 * HEAD_DIM), 0)
    lane = lax.broadcasted_iota(jnp.int32, (count, 2 * HEAD_DIM), 1) % HEAD_DIM
    first = jnp.where(lane == entry, 1.0, 0.0).astype(F32)
    second = jnp.where(lane == entry + count, 1.0, 0.0).astype(F32)

    def spread(table, lanes):
        return lax.dot_general(
            table, lanes, (((0,), (0,)), ((), ())),
            precision=lax.Precision.HIGHEST, preferred_element_type=F32,
        )

    sine = jnp.sin(angles)
    kept = jnp.where(lane[:1] >= ROT, 1.0, 0.0)
    cos_ref[...] = spread(jnp.cos(angles), first + second) + kept
    low_ref[...] = spread(sine, -first)
    high_ref[...] = spread(sine, second)


def rotary_rates():
    steps_half = np.arange(0, ROT, 2).astype(np.float32) / np.float32(ROT)
    return jnp.asarray((np.float32(10000.0) ** (-steps_half))[:, None])


def qkv_body(ln_ref, w_ref, b_ref, pos_ref, rate_ref, out_ref, cos_ref, low_ref, high_ref):
    c = pl.program_id(0)

    @pl.when(c == 0)
    def _():
        fill_tables(pos_ref, rate_ref, cos_ref, low_ref, high_ref)

    u = dot(ln_ref[...], w_ref[0]) + b_ref[pl.ds(c, 1), :]

    @pl.when(c == 2)
    def _():
        out_ref[0] = u.astype(BF16)

    @pl.when(c < 2)
    def _():
        for lane in range(0, u.shape[1], 128):
            part = u[:, lane : lane + 128]
            turned = part * cos_ref[...] + swap_halves(part, low_ref[...], high_ref[...])
            out_ref[0, :, lane : lane + 128] = turned.astype(BF16)


def project(ln, w_parts, bias, positions, rates):
    rows, width = ln.shape
    cols = w_parts.shape[2]
    return kernel(
        qkv_body,
        (shape((3, rows, cols), BF16),) + (shape((rows, 128)),) * 3,
        (3,),
        [
            whole((rows, width)),
            pl.BlockSpec((1, width, cols), lambda c: (c, 0, 0)),
            whole((3, cols)),
            whole((1, rows)),
            whole((ROT // 2, 1)),
        ],
        (pl.BlockSpec((1, rows, cols), lambda c: (c, 0, 0)),) + (whole((rows, 128)),) * 3,
        us=7,
        vmem=60,
    )(ln, w_parts, bias, positions, rates)


def attention_body(
    q_ref, k_ref, v_ref, g_ref, seg_ref, cos_ref, low_ref, high_ref,
    context_ref, grad_ref, sum_ref, dq, dk, dv,
):
    rows = q_ref.shape[1]
    step = 384
    scale = np.float32(HEAD_DIM**-0.5)
    lane = lax.broadcasted_iota(jnp.int32, (rows, 128), 1)
    heads = []
    for h in range(2):
        mine = (lane >= h * HEAD_DIM) & (lane < (h + 1) * HEAD_DIM)
        heads.append(
            [
                jnp.where(mine, ref, jnp.zeros_like(ref))
                for ref in (q_ref[0] * scale.astype(BF16), k_ref[0], v_ref[0], g_ref[...])
            ]
        )
    seg_row = seg_ref[...].astype(F32)
    seg_col = jnp.broadcast_to(seg_row, (128, rows)).T[:, :1]
    dk[...] = jnp.zeros_like(dk)
    dv[...] = jnp.zeros_like(dv)
    for i in range(rows // step):
        top = slice(i * step, (i + 1) * step)
        seen = (i + 1) * step
        row = lax.broadcasted_iota(jnp.int32, (step, seen), 0) + i * step
        col = lax.broadcasted_iota(jnp.int32, (step, seen), 1)
        allowed = (seg_col[top, :] == seg_row[:, :seen]) & (col <= row)
        context = jnp.zeros((step, 128), F32)
        grad_q = jnp.zeros((step, 128), F32)
        for q, k, v, g in heads:
            scores = jnp.where(allowed, dot_nt(q[top], k[:seen]), MASKED)
            peak = jnp.max(scores, axis=-1, keepdims=True)
            raised = jnp.exp(scores - peak)
            probs = raised * (1.0 / jnp.sum(raised, axis=-1, keepdims=True))
            probs_low = probs.astype(BF16)
            context += dot(probs_low, v[:seen])
            grad_probs = dot_nt(g[top], v[:seen])
            delta = jnp.sum(probs * grad_probs, axis=-1, keepdims=True)
            grad_scores = (probs * (grad_probs - delta)).astype(BF16)
            grad_q += dot(grad_scores, k[:seen])
            dk[:seen, :] += dot_tn(grad_scores, q[top])
            dv[:seen, :] += dot_tn(probs_low, g[top])
        context_ref[top, :] = context.astype(BF16)
        dq[top, :] = grad_q * scale
    for c, grad in enumerate((dq, dk, dv)):
        u = grad[...]
        if c < 2:
            u = u * cos_ref[...] - swap_halves(u, low_ref[...], high_ref[...])
        u = u.astype(BF16)
        grad_ref[c] = u
        sum_ref[c] = jnp.sum(u.astype(F32), axis=0, keepdims=True)


def attention(qkv, grad_context, segments, tables):
    _, rows, cols = qkv.shape
    pair = pl.BlockSpec((rows, 128), lambda p: (0, p))
    return kernel(
        attention_body,
        (shape((rows, cols), BF16), shape((3, rows, cols), BF16), shape((3, 1, cols))),
        (cols // 128,),
        [pl.BlockSpec((1, rows, 128), lambda p, c=c: (c, 0, p)) for c in range(3)]
        + [pair, whole((1, rows))]
        + [whole((rows, 128))] * 3,
        (
            pair,
            pl.BlockSpec((3, rows, 128), lambda p: (0, 0, p)),
            pl.BlockSpec((3, 1, 128), lambda p: (0, 0, p)),
        ),
        scratch=[pltpu.VMEM((rows, 128), F32)] * 3,
        us=12,
        vmem=60,
    )(qkv, qkv, qkv, grad_context, segments, *tables)


def chunks_of(z):
    return jnp.stack([z ^ 2, z ^ 1, z ^ 3, z]).astype(jnp.int32)


def put_chunks(outs, total):
    row = 0
    for out in outs:
        out[...] = total[row : row + out.shape[0], :]
        row += out.shape[0]


def chunk_rows(count):
    return [count // 2, count // 2, count, count, count]


def branch_body(at, *refs):
    lefts, rights = refs[:8], refs[8:10]
    outs, hidden, context = refs[10:15], refs[15], refs[16]
    count = outs[-1].shape[0]

    @pl.when(pl.program_id(0) == 0)
    def _():
        for i in range(4):
            hidden[i * count : (i + 1) * count, :] = lefts[i][...]
            context[i * count : (i + 1) * count, :] = lefts[4 + i][...]

    total = dot(hidden[...], rights[0][...]) + dot(context[...], rights[1][...])
    put_chunks(outs, total)


def branch_sums(at, hidden, context, w_fc2, w_out, step=512):
    rows, inner = hidden.shape
    heads = context.shape[1]
    width = w_fc2.shape[1]
    count = rows // 4

    def chunk(cols, i):
        return pl.BlockSpec((count, cols), lambda j, at, i=i: (at[i], 0))

    return kernel(
        branch_body,
        [shape((n, width)) for n in chunk_rows(count)],
        (width // step,),
        [chunk(inner, i) for i in range(4)]
        + [chunk(heads, i) for i in range(4)]
        + [
            pl.BlockSpec((inner, step), lambda j, at: (0, j)),
            pl.BlockSpec((heads, step), lambda j, at: (0, j)),
        ],
        [pl.BlockSpec((n, step), lambda j, at: (0, j)) for n in chunk_rows(count)],
        scratch=[pltpu.VMEM((rows, inner), BF16), pltpu.VMEM((rows, heads), BF16)],
        scalars=1,
        us=9,
        vmem=60,
    )(at, *[hidden] * 4, *[context] * 4, w_fc2, w_out)


def grad_ln_body(at, *refs):
    lefts, rights = refs[:8], refs[8:10]
    outs, pre, proj = refs[10:15], refs[15], refs[16]
    count = outs[-1].shape[0]

    @pl.when(pl.program_id(0) == 0)
    def _():
        for i in range(4):
            pre[i * count : (i + 1) * count, :] = lefts[i][...]
            for c in range(3):
                proj[c, i * count : (i + 1) * count, :] = lefts[4 + i][c]

    total = dot_nt(pre[...], rights[0][...])
    for c in range(3):
        total += dot_nt(proj[c], rights[1][c])
    put_chunks(outs, total)


def grad_ln_sums(at, pre, proj, w_fc1, w_parts, step=512):
    rows, inner = pre.shape
    heads = proj.shape[2]
    width = w_fc1.shape[0]
    count = rows // 4
    return kernel(
        grad_ln_body,
        [shape((n, width)) for n in chunk_rows(count)],
        (width // step,),
        [pl.BlockSpec((count, inner), lambda j, at, i=i: (at[i], 0)) for i in range(4)]
        + [pl.BlockSpec((3, count, heads), lambda j, at, i=i: (0, at[i], 0)) for i in range(4)]
        + [
            pl.BlockSpec((step, inner), lambda j, at: (j, 0)),
            pl.BlockSpec((3, step, heads), lambda j, at: (0, j, 0)),
        ],
        [pl.BlockSpec((n, step), lambda j, at: (0, j)) for n in chunk_rows(count)],
        scratch=[pltpu.VMEM((rows, inner), BF16), pltpu.VMEM((3, rows, heads), BF16)],
        scalars=1,
        us=11,
        vmem=60,
    )(at, *[pre] * 4, *[proj] * 4, w_fc1, w_parts)


def add_pair_body(up_in, down_in, high, low, up, down):
    up[...] = up_in[...] + high[...]
    down[...] = down_in[...] + low[...]


def add_halves(up, down, high, low, parts=2):
    rows, width = low.shape
    step = rows // parts
    first = pl.BlockSpec((step, width), lambda i: (i, 0))
    second = pl.BlockSpec((step, width), lambda i: (i + parts, 0))
    return kernel(
        add_pair_body,
        (shape(up.shape), shape(down.shape)),
        (parts,),
        [second, first, first, first],
        (second, first),
        aliases={0: 0, 1: 1},
        us=2,
        vmem=16,
    )(up, down, high, low)


def sum_body(*refs):
    total = refs[0][...]
    for ref in refs[1:-1]:
        total = total + ref[...]
    refs[-1][...] = total


def sum_of(*arrays, parts=3):
    rows, width = arrays[0].shape
    step = rows // parts
    spec = pl.BlockSpec((step, width), lambda i: (i, 0))
    return kernel(
        sum_body, shape((rows, width)), (rows // step,), [spec] * len(arrays), spec,
        us=3,
        vmem=16,
    )(*arrays)


def take_body(at, x, cot, x_out, cot_out):
    del at
    x_out[...] = x[...]
    cot_out[...] = cot[...]


def take_rows(at, x, cot, step=48):
    count, width = x.shape[0] // 4, x.shape[1]
    parts = count // step
    here = pl.BlockSpec((step, width), lambda i, at: (i, 0))
    there = pl.BlockSpec((step, width), lambda i, at: (at[3] * parts + i, 0))
    return kernel(
        take_body,
        (shape((count, width)), shape((count, width), BF16)),
        (parts,),
        [there, there],
        (here, here),
        scalars=1,
        us=3,
        vmem=60,
    )(at, x, cot)


def last_body(at, chunk, other, x, ob, fb, rows, out):
    del at
    total = chunk[...] + other[...] + x[...] + ob[...] + fb[...]
    rows[...] = total
    out[...] = total


def output_rows(at, chunk, other, x, out_bias, fc2_bias, step=48):
    count, width = chunk.shape
    parts = count // step
    here = pl.BlockSpec((step, width), lambda i, at: (i, 0))
    there = pl.BlockSpec((step, width), lambda i, at: (at[3] * parts + i, 0))
    return kernel(
        last_body,
        (shape((count, width)), shape((4 * count, width))),
        (parts,),
        [here, here, here, whole((1, width)), whole((1, width))],
        (here, there),
        scalars=1,
        us=4,
        vmem=16,
    )(at, chunk, other, x, out_bias, fc2_bias)


def norm_back_body(at, chunk, other, x, cot, gain, rows, out, sums):
    del at

    @pl.when(pl.program_id(0) == 0)
    def _():
        sums[...] = jnp.zeros_like(sums)

    grad = chunk[...] + other[...]
    normed, inv_std = norm_rows(x[...])
    sums[0:1, :] += jnp.sum(grad * normed, axis=0, keepdims=True)
    sums[1:2, :] += jnp.sum(grad, axis=0, keepdims=True)
    scaled = grad * gain[...]
    mean_scaled = jnp.mean(scaled, axis=-1, keepdims=True)
    mean_cross = jnp.mean(scaled * normed, axis=-1, keepdims=True)
    total = cot[...].astype(F32) + inv_std * (scaled - mean_scaled - normed * mean_cross)
    rows[...] = total
    out[...] = total


def input_grad_rows(at, chunk, other, x, cot, gain, step=48):
    count, width = chunk.shape
    parts = count // step
    here = pl.BlockSpec((step, width), lambda i, at: (i, 0))
    there = pl.BlockSpec((step, width), lambda i, at: (at[3] * parts + i, 0))
    return kernel(
        norm_back_body,
        (shape((count, width)), shape((4 * count, width)), shape((2, width))),
        (parts,),
        [here, here, here, here, whole((1, width))],
        (here, there, whole((2, width))),
        scalars=1,
        us=5,
        vmem=16,
    )(at, chunk, other, x, cot, gain)


def place_body(at, *refs, starts, sizes, copies):
    i = pl.program_id(0)
    count = len(starts)
    pieces, out, extra = refs[:count], refs[count + 1], refs[count + 2 :]
    for piece, start, size in zip(pieces, starts, sizes):

        @pl.when((i >= start) & (i < start + size))
        def _(piece=piece):
            out[...] = piece[...]

    for copy, (which, first, size) in zip(extra, copies):
        begin = starts[which] + first

        @pl.when((i >= begin) & (i < begin + size))
        def _(copy=copy, which=which):
            copy[...] = pieces[which][...]


def place_rows(out, pieces, blocks, copies=(), step=48):
    width = out.shape[1]
    sizes = [piece.shape[0] // step for piece in pieces]
    starts = [sum(sizes[:k]) for k in range(len(sizes))]

    def part(start, size):
        return pl.BlockSpec((step, width), lambda i, at: (jnp.clip(i - start, 0, size - 1), 0))

    return kernel(
        partial(place_body, starts=starts, sizes=sizes, copies=copies),
        [shape(out.shape)] + [shape((size * step, width)) for _, _, size in copies],
        (sum(sizes),),
        [part(start, size) for start, size in zip(starts, sizes)]
        + [pl.BlockSpec(memory_space=ANY)],
        [pl.BlockSpec((step, width), lambda i, at: (at[i], 0))]
        + [part(starts[which] + first, size) for which, first, size in copies],
        scalars=1,
        aliases={1 + len(pieces): 0},
        us=5,
        vmem=16,
    )(blocks, *pieces, out)


class Order:
    def __init__(self):
        self.last = None

    def __call__(self, step, *args):
        if self.last is not None:
            args, _ = lax.optimization_barrier((args, self.last))
        out = step(*args)
        self.last = jax.tree.leaves(out)[0]
        return out

    def after(self, *arrays):
        arrays, _ = lax.optimization_barrier((arrays, self.last))
        return arrays

    def wait(self, array):
        array, self.last = lax.optimization_barrier((array, self.last))
        return array


ROW_GROUPS = [[x * Y * CORE + i for i in range(Y * CORE)] for x in range(X_LO)]


def scatter(part):
    return lax.psum_scatter(
        part, "dp", scatter_dimension=0, axis_index_groups=ROW_GROUPS, tiled=True
    )


def gather(piece):
    return lax.all_gather(piece, "dp", axis=0, axis_index_groups=ROW_GROUPS, tiled=True)


def per_device(
    layer_input,
    ln_gain,
    ln_bias,
    w_qkv,
    qkv_bias,
    w_out,
    out_bias,
    w_fc1,
    fc1_bias,
    w_fc2,
    fc2_bias,
    segments,
    positions,
    cotangent,
):
    width = layer_input.shape[1]
    inner, local = w_fc1.shape[1], w_qkv.shape[2]
    at = chunks_of(lax.axis_index("tensor") // X_HI)
    run = Order()
    w_parts = jnp.transpose(w_qkv, (1, 0, 2))
    blocks = at[:3, None] * 4 + jnp.arange(4, dtype=jnp.int32)[None, :]
    near, far = blocks[1:].reshape(-1), blocks[0]
    near_copies = ((0, 0, 2), (1, 2, 2))
    add = partial(sum_of, parts=1)

    ln, hidden, slope, grad_fc2, grad_context, sum_out = run(
        first_products,
        layer_input, ln_gain[None], ln_bias[None], w_fc1, fc1_bias[None], cotangent, w_out,
    )
    piece_fc2 = scatter(grad_fc2)
    qkv, *tables = run(project, ln, w_parts, qkv_bias, positions, rotary_rates())
    context, grad_proj, sum_proj = run(attention, qkv, grad_context, segments, tables)
    low, high, up, down, own = run(branch_sums, at, hidden, context, w_fc2, w_out)
    low, high = send(low, "z^1"), send(high, "z^3")
    side, grad_pre, sum_pre = run(side_grads, ln, cotangent, w_fc2, slope, grad_proj, context)
    low, high = run.wait(low), run.wait(high)
    piece_fc2 = run.wait(piece_fc2)
    (side,) = run.after(side)
    piece = scatter(side)
    other_fc2 = send(*run.after(piece_fc2), "xlo")
    up, down = run(add_halves, up, down, high, low)
    from_up, from_down = send(up, "z^1"), send(down, "z^3")
    g_low, g_high, g_up, g_down, g_own = run(
        grad_ln_sums, at, grad_pre, grad_proj, w_fc1, w_parts
    )
    g_low, g_high = send(g_low, "z^1"), send(g_high, "z^3")
    piece_fc2 = run(partial(sum_of, parts=4), piece_fc2, other_fc2)
    chunk = run(sum_of, own, from_up, from_down)
    other = send(chunk, "xhi")
    g_up, g_down = run(add_halves, g_up, g_down, g_high, g_low)
    g_from_up, g_from_down = send(g_up, "z^1"), send(g_down, "z^3")
    x_rows, cot_rows = run(take_rows, at, layer_input, cotangent)
    rows, output = run(output_rows, at, chunk, other, x_rows, out_bias[None], fc2_bias[None])
    g_from_up, g_from_down = run.wait(g_from_up), run.wait(g_from_down)
    piece = run.wait(piece)
    (piece_fc2,) = run.after(piece_fc2)
    tot_fc2 = gather(piece_fc2)
    rows, piece = run.after(rows, piece)
    other_piece = send(piece, "xlo")
    near_up, near_down = send(rows, "z^1"), send(rows, "z^3")
    g_chunk = run(sum_of, g_own, g_from_up, g_from_down)
    output, low, high = run(
        partial(place_rows, copies=near_copies), output, [near_up, near_down], near
    )
    piece = run(partial(sum_of, parts=4), piece, other_piece)
    side = gather(piece)
    g_chunk, low, high = run.after(g_chunk, low, high)
    g_other = send(g_chunk, "xhi")
    low, high = send(low, "z^3"), send(high, "z^1")
    tot_fc2 = run(copy_of, tot_fc2)
    (output,) = run(place_rows, output, [low, high], far)
    g_rows, grad_input, sums = run(
        input_grad_rows, at, g_chunk, g_other, x_rows, cot_rows, ln_gain[None]
    )
    g_near_up, g_near_down = send(g_rows, "z^1"), send(g_rows, "z^3")
    biases = jnp.concatenate(
        [sum_out[0], sum_pre[0], sum_proj.reshape(-1), jnp.zeros((256,), F32)]
    ).reshape(8, width // 4)
    sums = jnp.concatenate([sums.reshape(8, width // 4), biases], axis=0)
    for move in ("core", "y^1", "y^2", "xlo"):
        sums = run(add, sums, send(sums, move))
    norm_sums = run.wait(sums[:8])
    other_sums = send(norm_sums, "z^1")
    rest = sums[8:].reshape(-1)
    tot_out_bias = run.wait(rest[:width])
    tot_fc1_bias = run.wait(rest[width : width + inner])
    tot_qkv_bias = run.wait(rest[width + inner : width + inner + 3 * local].reshape(3, local))
    tot_fc2_bias = run(add, tot_out_bias[None])[0]
    norm_sums = run(add, norm_sums, other_sums)
    other_sums = send(norm_sums, "z^2")
    grad_input, g_low, g_high = run(
        partial(place_rows, copies=near_copies), grad_input, [g_near_up, g_near_down], near
    )
    g_low, g_high = send(g_low, "z^3"), send(g_high, "z^1")
    tot_fc1, tot_qkv, tot_out = run(lambda side: split_grads(side, inner, local), side)
    norm_sums = run(add, norm_sums, other_sums)
    (grad_input,) = run(place_rows, grad_input, [g_low, g_high], far)
    gain, shift = norm_sums.reshape(2, width)
    return (
        output,
        grad_input,
        gain,
        shift,
        jnp.transpose(tot_qkv, (1, 0, 2)),
        tot_qkv_bias,
        tot_out,
        tot_out_bias,
        tot_fc1,
        tot_fc1_bias,
        tot_fc2,
        tot_fc2_bias,
    )


def solution(mesh):
    in_specs = (
        P("dp", None),
        P(),
        P(),
        P(None, None, "tensor"),
        P(None, "tensor"),
        P("tensor", None),
        P(),
        P(None, "tensor"),
        P("tensor"),
        P("tensor", None),
        P(),
        P("dp", None),
        P("dp", None),
        P("dp", None),
    )
    out_specs = (
        P("dp", None),
        P("dp", None),
        P(),
        P(),
        P(None, None, "tensor"),
        P(None, "tensor"),
        P("tensor", None),
        P(),
        P(None, "tensor"),
        P("tensor"),
        P("tensor", None),
        P(),
    )
    return jax.shard_map(
        per_device, mesh=mesh, in_specs=in_specs, out_specs=out_specs, check_vma=False
    )
```

```python
from functools import partial

import jax
import jax.numpy as jnp
import numpy as np
from jax import lax
from jax.experimental import pallas as pl
from jax.experimental.pallas import tpu as pltpu
from jax.sharding import PartitionSpec as P

HEAD_DIM = 64
ROT = 32
EPSILON = 1e-05
MASKED = -1e30
F32, BF16 = jnp.float32, jnp.bfloat16
ANY = pl.ANY


def shape(dims, dtype=F32):
    return jax.ShapeDtypeStruct(dims, dtype)


def kernel(body, out, grid, in_specs, out_specs, scratch=(), scalars=0, aliases=None, vmem=40, us=3):
    return pl.pallas_call(
        body,
        out_shape=out,
        grid_spec=pltpu.PrefetchScalarGridSpec(
            num_scalar_prefetch=scalars,
            grid=grid,
            in_specs=in_specs,
            out_specs=out_specs,
            scratch_shapes=scratch,
        ),
        input_output_aliases=aliases or {},
        compiler_params=pltpu.CompilerParams(vmem_limit_bytes=vmem << 20),
        cost_estimate=pl.CostEstimate(
            flops=0, bytes_accessed=int(us * 3e6), transcendentals=0
        ),
    )


def whole(dims):
    return pl.BlockSpec(dims, lambda *_: (0,) * len(dims))


def dot(a, b):
    return jnp.dot(a, b, preferred_element_type=F32)


def dot_nt(a, b):
    return lax.dot_general(a, b, (((1,), (1,)), ((), ())), preferred_element_type=F32)


def dot_tn(a, b):
    return lax.dot_general(a, b, (((0,), (0,)), ((), ())), preferred_element_type=F32)


X_LO, Y, CORE = 2, 4, 2
Z, X_HI = 4, 2


def dp_moves(step):
    pairs = []
    for x in range(X_LO):
        for y in range(Y):
            for c in range(CORE):
                x2, y2, c2 = step(x, y, c)
                there = ((x2 % X_LO) * Y + y2 % Y) * CORE + c2 % CORE
                pairs.append(((x * Y + y) * CORE + c, there))
    return pairs


def tensor_moves(step):
    pairs = []
    for z in range(Z):
        for x in range(X_HI):
            z2, x2 = step(z, x)
            pairs.append((z * X_HI + x, (z2 % Z) * X_HI + x2 % X_HI))
    return pairs


MOVES = {
    "core": ("dp", dp_moves(lambda x, y, c: (x, y, c + 1))),
    "y^1": ("dp", dp_moves(lambda x, y, c: (x, y ^ 1, c))),
    "y^2": ("dp", dp_moves(lambda x, y, c: (x, y ^ 2, c))),
    "xlo": ("dp", dp_moves(lambda x, y, c: (x + 1, y, c))),
    "y^3": ("dp", dp_moves(lambda x, y, c: (x, y ^ 3, c))),
    "z^1": ("tensor", tensor_moves(lambda z, x: (z ^ 1, x))),
    "z^3": ("tensor", tensor_moves(lambda z, x: (z ^ 3, x))),
    "z^2": ("tensor", tensor_moves(lambda z, x: (z ^ 2, x))),
    "xhi": ("tensor", tensor_moves(lambda z, x: (z, x + 1))),
}


def send(array, move):
    axis, pairs = MOVES[move]
    return lax.ppermute(array, axis, pairs)


def norm_rows(x):
    center = x - jnp.mean(x, axis=-1, keepdims=True)
    inv_std = lax.rsqrt(jnp.mean(center * center, axis=-1, keepdims=True) + EPSILON)
    return center * inv_std, inv_std


def gelu_and_slope(v):
    a = np.float32(np.sqrt(2 / np.pi))
    b = np.float32(a * 0.044715)
    square = v * v
    h = 0.5 * jnp.tanh(v * (a + b * square)) + 0.5
    return v * h, h + v * (2 * a + 6 * b * square) * (h - h * h)


def first_body(
    x_ref, gain_ref, bias_ref, w_ref, b_ref, cot_ref, wo_ref,
    low_ref, hidden_ref, slope_ref, grad_ref, context_ref, sum_ref, turned, total,
):
    i = pl.program_id(0)
    block, step = x_ref.shape[0], w_ref.shape[1]
    blocks, tiles = low_ref.shape[0] // block, turned.shape[0] // step

    @pl.when(i < blocks)
    def _():
        normed, _ = norm_rows(x_ref[...])
        low = (normed * gain_ref[...] + bias_ref[...]).astype(BF16)
        low_ref[pl.ds(pl.multiple_of(i * block, block), block), :] = low

    @pl.when((i >= blocks) & (i < blocks + tiles))
    def _():
        hidden, slope = gelu_and_slope(dot(low_ref[...], w_ref[...]) + b_ref[...])
        hidden = hidden.astype(BF16)
        hidden_ref[...] = hidden
        turned[pl.ds(pl.multiple_of((i - blocks) * step, step), step), :] = hidden.T
        slope_ref[...] = slope.astype(BF16)

    @pl.when(i == blocks + tiles)
    def _():
        total[...] = jnp.zeros_like(total)

    @pl.when(i >= blocks + tiles)
    def _():
        cot = cot_ref[...]
        grad_ref[...] = dot(turned[...], cot)
        total[...] += dot_nt(cot, wo_ref[...])
        sum_ref[...] = jnp.sum(cot.astype(F32), axis=0, keepdims=True)

    @pl.when(i == pl.num_programs(0) - 1)
    def _():
        context_ref[...] = total[...].astype(BF16)


def first_products(x, gain, bias, w, b, cot, w_out, block=256, step=256, wide=512):
    rows, width = x.shape
    cols, heads = w.shape[1], w_out.shape[0]
    blocks, tiles, last = rows // block, cols // step, width // wide

    def tile(j):
        return jnp.clip(j - blocks, 0, tiles - 1)

    def final(j):
        return jnp.maximum(j - blocks - tiles, 0)

    out = pl.BlockSpec((rows, step), lambda j: (0, tile(j)))
    return kernel(
        first_body,
        (
            shape((rows, width), BF16),
            shape((rows, cols), BF16),
            shape((rows, cols), BF16),
            shape((cols, width)),
            shape((rows, heads), BF16),
            shape((1, width)),
        ),
        (blocks + tiles + last,),
        [
            pl.BlockSpec((block, width), lambda j: (jnp.minimum(j, blocks - 1), 0)),
            whole((1, width)),
            whole((1, width)),
            pl.BlockSpec((width, step), lambda j: (0, tile(j))),
            pl.BlockSpec((1, step), lambda j: (0, tile(j))),
            pl.BlockSpec((rows, wide), lambda j: (0, final(j))),
            pl.BlockSpec((heads, wide), lambda j: (0, final(j))),
        ],
        (
            whole((rows, width)),
            out,
            out,
            pl.BlockSpec((cols, wide), lambda j: (0, final(j))),
            whole((rows, heads)),
            pl.BlockSpec((1, wide), lambda j: (0, final(j))),
        ),
        scratch=[pltpu.VMEM((cols, rows), BF16), pltpu.VMEM((rows, heads), F32)],
        us=20,
        vmem=60,
    )(x, gain, bias, w, b, cot, w_out)


def side_body(
    ln_ref, cot_ref, w_ref, slope_ref, proj_ref, out_ref, pre_ref, sum_ref
):
    i = pl.program_id(0)
    tile, step = w_ref.shape[0], proj_ref.shape[2]
    n = pre_ref.shape[1]
    tiles = n // tile

    @pl.when(i < tiles)
    def _():
        grad = (dot_nt(cot_ref[...], w_ref[...]) * slope_ref[...]).astype(BF16)
        pre_ref[:, pl.ds(pl.multiple_of(i * tile, tile), tile)] = grad
        sum_ref[...] = jnp.sum(grad.astype(F32), axis=0, keepdims=True)

    @pl.when(i >= tiles)
    def _():
        turned = ln_ref[...].T
        out_ref[:, :n] = dot(turned, pre_ref[...])
        for c in range(3):
            out_ref[:, n + c * step : n + (c + 1) * step] = dot(turned, proj_ref[c])


def side_grads(ln, cot, w, slope, proj, block=512, tile=256):
    rows, m = ln.shape
    n, step = w.shape[0], proj.shape[2]
    tiles = n // tile

    def first(j):
        return jnp.minimum(j, tiles - 1)

    def second(j):
        return jnp.maximum(j - tiles, 0)

    return kernel(
        side_body,
        (shape((m, n + 3 * step)), shape((rows, n), BF16), shape((1, n))),
        (tiles + m // block,),
        [
            pl.BlockSpec((rows, block), lambda j: (0, second(j))),
            whole((rows, m)),
            pl.BlockSpec((tile, m), lambda j: (first(j), 0)),
            pl.BlockSpec((rows, tile), lambda j: (0, first(j))),
            whole((3, rows, step)),
        ],
        (
            pl.BlockSpec((block, n + 3 * step), lambda j: (second(j), 0)),
            whole((rows, n)),
            pl.BlockSpec((1, tile), lambda j: (0, first(j))),
        ),
        us=18,
        vmem=60,
    )(ln, cot, w, slope, proj)


def split_body(side, one, three):
    n, step = one.shape[1], three.shape[2]
    one[...] = side[:, :n]
    for c in range(3):
        three[c] = side[:, n + c * step : n + (c + 1) * step]


def split_grads(side, n, step, tile=512):
    rows = side.shape[0]
    return kernel(
        split_body,
        (shape((rows, n)), shape((3, rows, step))),
        (rows // tile,),
        [pl.BlockSpec((tile, side.shape[1]), lambda i: (i, 0))],
        (
            pl.BlockSpec((tile, n), lambda i: (i, 0)),
            pl.BlockSpec((3, tile, step), lambda i: (0, i, 0)),
        ),
        us=11,
        vmem=40,
    )(side)


def out_grad_body(at, context, cot, theirs, away, keep, left, turned):
    @pl.when(pl.program_id(0) == 0)
    def _():
        turned[...] = context[...].T
        for i in range(4):
            row = pl.multiple_of(at[i] * 64, 64)
            left[i * 64 : (i + 1) * 64, :] = turned[pl.ds(row, 64), :]

    total = dot(left[...], cot[...])
    theirs[...] = total[:128]
    away[...] = total[128:192]
    keep[...] = total[192:]


def out_grad(at, context, cot, step=512):
    rows, width = cot.shape
    m = context.shape[1]

    def tile(count):
        return pl.BlockSpec((count, step), lambda j, at: (0, j))

    return kernel(
        out_grad_body,
        (shape((128, width)), shape((64, width)), shape((64, width))),
        (width // step,),
        [whole((rows, m)), tile(rows)],
        (tile(128), tile(64), tile(64)),
        scratch=[pltpu.VMEM((m, rows), BF16)] * 2,
        scalars=1,
        us=3,
        vmem=60,
    )(at, context, cot)


def add_parts_body(away_in, keep_in, first, second, away, keep):
    away[...] = away_in[...] + first[...]
    keep[...] = keep_in[...] + second[...]


def add_parts(away, keep, both):
    rows, width = keep.shape
    first = pl.BlockSpec((rows, width), lambda i: (0, 0))
    second = pl.BlockSpec((rows, width), lambda i: (1, 0))
    return kernel(
        add_parts_body,
        (shape((rows, width)), shape((rows, width))),
        (1,),
        [first, first, first, second],
        (first, first),
        us=2,
        vmem=16,
    )(away, keep, both, both)


def assemble_body(at, *refs):
    del at
    i = pl.program_id(0)
    for k, piece in enumerate(refs[:-1]):

        @pl.when(i == k)
        def _(piece=piece):
            refs[-1][...] = piece[...]


def assemble(at, *pieces):
    rows, width = pieces[0].shape
    return kernel(
        assemble_body,
        shape((len(pieces) * rows, width)),
        (len(pieces),),
        [whole((rows, width))] * len(pieces),
        pl.BlockSpec((rows, width), lambda i, at: (at[i], 0)),
        scalars=1,
        us=2,
        vmem=16,
    )(at, *pieces)


def copy_body(source, out):
    out[...] = source[...]


def copy_of(source, step=256):
    rows, width = source.shape
    spec = pl.BlockSpec((step, width), lambda i: (i, 0))
    return kernel(
        copy_body, shape((rows, width)), (rows // step,), [spec], spec, us=6, vmem=60    )(source)


def swap_halves(u, low, high):
    width = u.shape[1]
    return pltpu.roll(u, width - ROT // 2, 1) * low + pltpu.roll(u, ROT // 2, 1) * high


def fill_tables(pos_ref, rate_ref, cos_ref, low_ref, high_ref):
    angles = rate_ref[...] * pos_ref[...].astype(F32)
    count = ROT // 2
    entry = lax.broadcasted_iota(jnp.int32, (count, 2 * HEAD_DIM), 0)
    lane = lax.broadcasted_iota(jnp.int32, (count, 2 * HEAD_DIM), 1) % HEAD_DIM
    first = jnp.where(lane == entry, 1.0, 0.0).astype(F32)
    second = jnp.where(lane == entry + count, 1.0, 0.0).astype(F32)

    def spread(table, lanes):
        return lax.dot_general(
            table, lanes, (((0,), (0,)), ((), ())),
            precision=lax.Precision.HIGHEST, preferred_element_type=F32,
        )

    sine = jnp.sin(angles)
    kept = jnp.where(lane[:1] >= ROT, 1.0, 0.0)
    cos_ref[...] = spread(jnp.cos(angles), first + second) + kept
    low_ref[...] = spread(sine, -first)
    high_ref[...] = spread(sine, second)


def rotary_rates():
    steps_half = np.arange(0, ROT, 2).astype(np.float32) / np.float32(ROT)
    return jnp.asarray((np.float32(10000.0) ** (-steps_half))[:, None])


def qkv_body(ln_ref, w_ref, b_ref, pos_ref, rate_ref, out_ref, cos_ref, low_ref, high_ref):
    c = pl.program_id(0)

    @pl.when(c == 0)
    def _():
        fill_tables(pos_ref, rate_ref, cos_ref, low_ref, high_ref)

    u = dot(ln_ref[...], w_ref[0]) + b_ref[pl.ds(c, 1), :]

    @pl.when(c == 2)
    def _():
        out_ref[0] = u.astype(BF16)

    @pl.when(c < 2)
    def _():
        for lane in range(0, u.shape[1], 128):
            part = u[:, lane : lane + 128]
            turned = part * cos_ref[...] + swap_halves(part, low_ref[...], high_ref[...])
            out_ref[0, :, lane : lane + 128] = turned.astype(BF16)


def project(ln, w_parts, bias, positions, rates):
    rows, width = ln.shape
    cols = w_parts.shape[2]
    return kernel(
        qkv_body,
        (shape((3, rows, cols), BF16),) + (shape((rows, 128)),) * 3,
        (3,),
        [
            whole((rows, width)),
            pl.BlockSpec((1, width, cols), lambda c: (c, 0, 0)),
            whole((3, cols)),
            whole((1, rows)),
            whole((ROT // 2, 1)),
        ],
        (pl.BlockSpec((1, rows, cols), lambda c: (c, 0, 0)),) + (whole((rows, 128)),) * 3,
        us=7,
        vmem=60,
    )(ln, w_parts, bias, positions, rates)


def attention_body(
    q_ref, k_ref, v_ref, g_ref, seg_ref, cos_ref, low_ref, high_ref,
    context_ref, grad_ref, sum_ref, dq, dk, dv,
):
    rows = q_ref.shape[1]
    step = 384
    scale = np.float32(HEAD_DIM**-0.5)
    lane = lax.broadcasted_iota(jnp.int32, (rows, 128), 1)
    heads = []
    for h in range(2):
        mine = (lane >= h * HEAD_DIM) & (lane < (h + 1) * HEAD_DIM)
        heads.append(
            [
                jnp.where(mine, ref, jnp.zeros_like(ref))
                for ref in (q_ref[0] * scale.astype(BF16), k_ref[0], v_ref[0], g_ref[...])
            ]
        )
    seg_row = seg_ref[...].astype(F32)
    seg_col = jnp.broadcast_to(seg_row, (128, rows)).T[:, :1]
    dk[...] = jnp.zeros_like(dk)
    dv[...] = jnp.zeros_like(dv)
    for i in range(rows // step):
        top = slice(i * step, (i + 1) * step)
        seen = (i + 1) * step
        row = lax.broadcasted_iota(jnp.int32, (step, seen), 0) + i * step
        col = lax.broadcasted_iota(jnp.int32, (step, seen), 1)
        allowed = (seg_col[top, :] == seg_row[:, :seen]) & (col <= row)
        context = jnp.zeros((step, 128), F32)
        grad_q = jnp.zeros((step, 128), F32)
        for q, k, v, g in heads:
            scores = jnp.where(allowed, dot_nt(q[top], k[:seen]), MASKED)
            peak = jnp.max(scores, axis=-1, keepdims=True)
            raised = jnp.exp(scores - peak)
            probs = raised * (1.0 / jnp.sum(raised, axis=-1, keepdims=True))
            probs_low = probs.astype(BF16)
            context += dot(probs_low, v[:seen])
            grad_probs = dot_nt(g[top], v[:seen])
            delta = jnp.sum(probs * grad_probs, axis=-1, keepdims=True)
            grad_scores = (probs * (grad_probs - delta)).astype(BF16)
            grad_q += dot(grad_scores, k[:seen])
            dk[:seen, :] += dot_tn(grad_scores, q[top])
            dv[:seen, :] += dot_tn(probs_low, g[top])
        context_ref[top, :] = context.astype(BF16)
        dq[top, :] = grad_q * scale
    for c, grad in enumerate((dq, dk, dv)):
        u = grad[...]
        if c < 2:
            u = u * cos_ref[...] - swap_halves(u, low_ref[...], high_ref[...])
        u = u.astype(BF16)
        grad_ref[c] = u
        sum_ref[c] = jnp.sum(u.astype(F32), axis=0, keepdims=True)


def attention(qkv, grad_context, segments, tables):
    _, rows, cols = qkv.shape
    pair = pl.BlockSpec((rows, 128), lambda p: (0, p))
    return kernel(
        attention_body,
        (shape((rows, cols), BF16), shape((3, rows, cols), BF16), shape((3, 1, cols))),
        (cols // 128,),
        [pl.BlockSpec((1, rows, 128), lambda p, c=c: (c, 0, p)) for c in range(3)]
        + [pair, whole((1, rows))]
        + [whole((rows, 128))] * 3,
        (
            pair,
            pl.BlockSpec((3, rows, 128), lambda p: (0, 0, p)),
            pl.BlockSpec((3, 1, 128), lambda p: (0, 0, p)),
        ),
        scratch=[pltpu.VMEM((rows, 128), F32)] * 3,
        us=12,
        vmem=60,
    )(qkv, qkv, qkv, grad_context, segments, *tables)


def chunks_of(z):
    return jnp.stack([z ^ 2, z ^ 1, z ^ 3, z]).astype(jnp.int32)


def put_chunks(outs, total):
    row = 0
    for out in outs:
        out[...] = total[row : row + out.shape[0], :]
        row += out.shape[0]


def chunk_rows(count):
    return [count // 2, count // 2, count, count, count]


def branch_body(at, *refs):
    lefts, rights = refs[:8], refs[8:10]
    outs, hidden, context = refs[10:15], refs[15], refs[16]
    count = outs[-1].shape[0]

    @pl.when(pl.program_id(0) == 0)
    def _():
        for i in range(4):
            hidden[i * count : (i + 1) * count, :] = lefts[i][...]
            context[i * count : (i + 1) * count, :] = lefts[4 + i][...]

    total = dot(hidden[...], rights[0][...]) + dot(context[...], rights[1][...])
    put_chunks(outs, total)


def branch_sums(at, hidden, context, w_fc2, w_out, step=512):
    rows, inner = hidden.shape
    heads = context.shape[1]
    width = w_fc2.shape[1]
    count = rows // 4

    def chunk(cols, i):
        return pl.BlockSpec((count, cols), lambda j, at, i=i: (at[i], 0))

    return kernel(
        branch_body,
        [shape((n, width)) for n in chunk_rows(count)],
        (width // step,),
        [chunk(inner, i) for i in range(4)]
        + [chunk(heads, i) for i in range(4)]
        + [
            pl.BlockSpec((inner, step), lambda j, at: (0, j)),
            pl.BlockSpec((heads, step), lambda j, at: (0, j)),
        ],
        [pl.BlockSpec((n, step), lambda j, at: (0, j)) for n in chunk_rows(count)],
        scratch=[pltpu.VMEM((rows, inner), BF16), pltpu.VMEM((rows, heads), BF16)],
        scalars=1,
        us=9,
        vmem=60,
    )(at, *[hidden] * 4, *[context] * 4, w_fc2, w_out)


def grad_ln_body(at, *refs):
    lefts, rights = refs[:8], refs[8:10]
    outs, pre, proj = refs[10:15], refs[15], refs[16]
    count = outs[-1].shape[0]

    @pl.when(pl.program_id(0) == 0)
    def _():
        for i in range(4):
            pre[i * count : (i + 1) * count, :] = lefts[i][...]
            for c in range(3):
                proj[c, i * count : (i + 1) * count, :] = lefts[4 + i][c]

    total = dot_nt(pre[...], rights[0][...])
    for c in range(3):
        total += dot_nt(proj[c], rights[1][c])
    put_chunks(outs, total)


def grad_ln_sums(at, pre, proj, w_fc1, w_parts, step=512):
    rows, inner = pre.shape
    heads = proj.shape[2]
    width = w_fc1.shape[0]
    count = rows // 4
    return kernel(
        grad_ln_body,
        [shape((n, width)) for n in chunk_rows(count)],
        (width // step,),
        [pl.BlockSpec((count, inner), lambda j, at, i=i: (at[i], 0)) for i in range(4)]
        + [pl.BlockSpec((3, count, heads), lambda j, at, i=i: (0, at[i], 0)) for i in range(4)]
        + [
            pl.BlockSpec((step, inner), lambda j, at: (j, 0)),
            pl.BlockSpec((3, step, heads), lambda j, at: (0, j, 0)),
        ],
        [pl.BlockSpec((n, step), lambda j, at: (0, j)) for n in chunk_rows(count)],
        scratch=[pltpu.VMEM((rows, inner), BF16), pltpu.VMEM((3, rows, heads), BF16)],
        scalars=1,
        us=11,
        vmem=60,
    )(at, *[pre] * 4, *[proj] * 4, w_fc1, w_parts)


def add_pair_body(up_in, down_in, high, low, up, down):
    up[...] = up_in[...] + high[...]
    down[...] = down_in[...] + low[...]


def add_halves(up, down, high, low, parts=2):
    rows, width = low.shape
    step = rows // parts
    first = pl.BlockSpec((step, width), lambda i: (i, 0))
    second = pl.BlockSpec((step, width), lambda i: (i + parts, 0))
    return kernel(
        add_pair_body,
        (shape(up.shape), shape(down.shape)),
        (parts,),
        [second, first, first, first],
        (second, first),
        aliases={0: 0, 1: 1},
        us=2,
        vmem=16,
    )(up, down, high, low)


def sum_body(*refs):
    total = refs[0][...]
    for ref in refs[1:-1]:
        total = total + ref[...]
    refs[-1][...] = total


def sum_of(*arrays, parts=3):
    rows, width = arrays[0].shape
    step = rows // parts
    spec = pl.BlockSpec((step, width), lambda i: (i, 0))
    return kernel(
        sum_body, shape((rows, width)), (rows // step,), [spec] * len(arrays), spec,
        us=3,
        vmem=16,
    )(*arrays)


def take_body(at, x, cot, x_out, cot_out):
    del at
    x_out[...] = x[...]
    cot_out[...] = cot[...]


def take_rows(at, x, cot, step=48):
    count, width = x.shape[0] // 4, x.shape[1]
    parts = count // step
    here = pl.BlockSpec((step, width), lambda i, at: (i, 0))
    there = pl.BlockSpec((step, width), lambda i, at: (at[3] * parts + i, 0))
    return kernel(
        take_body,
        (shape((count, width)), shape((count, width), BF16)),
        (parts,),
        [there, there],
        (here, here),
        scalars=1,
        us=3,
        vmem=60,
    )(at, x, cot)


def last_body(at, chunk, other, x, ob, fb, rows, out):
    del at
    total = chunk[...] + other[...] + x[...] + ob[...] + fb[...]
    rows[...] = total
    out[...] = total


def output_rows(at, chunk, other, x, out_bias, fc2_bias, step=48):
    count, width = chunk.shape
    parts = count // step
    here = pl.BlockSpec((step, width), lambda i, at: (i, 0))
    there = pl.BlockSpec((step, width), lambda i, at: (at[3] * parts + i, 0))
    return kernel(
        last_body,
        (shape((count, width)), shape((4 * count, width))),
        (parts,),
        [here, here, here, whole((1, width)), whole((1, width))],
        (here, there),
        scalars=1,
        us=4,
        vmem=16,
    )(at, chunk, other, x, out_bias, fc2_bias)


def norm_back_body(at, chunk, other, x, cot, gain, rows, out, sums):
    del at

    @pl.when(pl.program_id(0) == 0)
    def _():
        sums[...] = jnp.zeros_like(sums)

    grad = chunk[...] + other[...]
    normed, inv_std = norm_rows(x[...])
    sums[0:1, :] += jnp.sum(grad * normed, axis=0, keepdims=True)
    sums[1:2, :] += jnp.sum(grad, axis=0, keepdims=True)
    scaled = grad * gain[...]
    mean_scaled = jnp.mean(scaled, axis=-1, keepdims=True)
    mean_cross = jnp.mean(scaled * normed, axis=-1, keepdims=True)
    total = cot[...].astype(F32) + inv_std * (scaled - mean_scaled - normed * mean_cross)
    rows[...] = total
    out[...] = total


def input_grad_rows(at, chunk, other, x, cot, gain, step=48):
    count, width = chunk.shape
    parts = count // step
    here = pl.BlockSpec((step, width), lambda i, at: (i, 0))
    there = pl.BlockSpec((step, width), lambda i, at: (at[3] * parts + i, 0))
    return kernel(
        norm_back_body,
        (shape((count, width)), shape((4 * count, width)), shape((2, width))),
        (parts,),
        [here, here, here, here, whole((1, width))],
        (here, there, whole((2, width))),
        scalars=1,
        us=5,
        vmem=16,
    )(at, chunk, other, x, cot, gain)


def place_body(at, *refs, starts, sizes, copies):
    i = pl.program_id(0)
    count = len(starts)
    pieces, out, extra = refs[:count], refs[count + 1], refs[count + 2 :]
    for piece, start, size in zip(pieces, starts, sizes):

        @pl.when((i >= start) & (i < start + size))
        def _(piece=piece):
            out[...] = piece[...]

    for copy, (which, first, size) in zip(extra, copies):
        begin = starts[which] + first

        @pl.when((i >= begin) & (i < begin + size))
        def _(copy=copy, which=which):
            copy[...] = pieces[which][...]


def place_rows(out, pieces, blocks, copies=(), step=48):
    width = out.shape[1]
    sizes = [piece.shape[0] // step for piece in pieces]
    starts = [sum(sizes[:k]) for k in range(len(sizes))]

    def part(start, size):
        return pl.BlockSpec((step, width), lambda i, at: (jnp.clip(i - start, 0, size - 1), 0))

    return kernel(
        partial(place_body, starts=starts, sizes=sizes, copies=copies),
        [shape(out.shape)] + [shape((size * step, width)) for _, _, size in copies],
        (sum(sizes),),
        [part(start, size) for start, size in zip(starts, sizes)]
        + [pl.BlockSpec(memory_space=ANY)],
        [pl.BlockSpec((step, width), lambda i, at: (at[i], 0))]
        + [part(starts[which] + first, size) for which, first, size in copies],
        scalars=1,
        aliases={1 + len(pieces): 0},
        us=5,
        vmem=16,
    )(blocks, *pieces, out)


class Order:
    def __init__(self):
        self.last = None

    def __call__(self, step, *args):
        if self.last is not None:
            args, _ = lax.optimization_barrier((args, self.last))
        out = step(*args)
        self.last = jax.tree.leaves(out)[0]
        return out

    def after(self, *arrays):
        arrays, _ = lax.optimization_barrier((arrays, self.last))
        return arrays

    def wait(self, array):
        array, self.last = lax.optimization_barrier((array, self.last))
        return array


ROW_GROUPS = [[x * Y * CORE + i for i in range(Y * CORE)] for x in range(X_LO)]


def scatter(part):
    return lax.psum_scatter(
        part, "dp", scatter_dimension=0, axis_index_groups=ROW_GROUPS, tiled=True
    )


def gather(piece):
    return lax.all_gather(piece, "dp", axis=0, axis_index_groups=ROW_GROUPS, tiled=True)


def per_device(
    layer_input,
    ln_gain,
    ln_bias,
    w_qkv,
    qkv_bias,
    w_out,
    out_bias,
    w_fc1,
    fc1_bias,
    w_fc2,
    fc2_bias,
    segments,
    positions,
    cotangent,
):
    width = layer_input.shape[1]
    inner, local = w_fc1.shape[1], w_qkv.shape[2]
    at = chunks_of(lax.axis_index("tensor") // X_HI)
    at_dp = lax.axis_index("dp")
    x, core = at_dp // (Y * CORE), lax.rem(at_dp, CORE)
    run = Order()
    w_parts = jnp.transpose(w_qkv, (1, 0, 2))
    blocks = at[:3, None] * 4 + jnp.arange(4, dtype=jnp.int32)[None, :]
    near, far = blocks[1:].reshape(-1), blocks[0]
    near_copies = ((0, 0, 2), (1, 2, 2))
    add = partial(sum_of, parts=1)

    ln, hidden, slope, grad_fc2, grad_context, sum_out = run(
        first_products,
        layer_input, ln_gain[None], ln_bias[None], w_fc1, fc1_bias[None], cotangent, w_out,
    )
    piece_fc2 = scatter(grad_fc2)
    qkv, *tables = run(project, ln, w_parts, qkv_bias, positions, rotary_rates())
    context, grad_proj, sum_proj = run(attention, qkv, grad_context, segments, tables)
    low, high, up, down, own = run(branch_sums, at, hidden, context, w_fc2, w_out)
    low, high = send(low, "z^1"), send(high, "z^3")
    side, grad_pre, sum_pre = run(side_grads, ln, cotangent, w_fc2, slope, grad_proj)
    low, high = run.wait(low), run.wait(high)
    piece_fc2 = run.wait(piece_fc2)
    (side,) = run.after(side)
    piece = scatter(side)
    other_fc2 = send(*run.after(piece_fc2), "xlo")
    up, down = run(add_halves, up, down, high, low)
    from_up, from_down = send(up, "z^1"), send(down, "z^3")
    g_low, g_high, g_up, g_down, g_own = run(
        grad_ln_sums, at, grad_pre, grad_proj, w_fc1, w_parts
    )
    g_low, g_high = send(g_low, "z^1"), send(g_high, "z^3")
    theirs, away, keep = run(
        out_grad,
        jnp.stack([3 - 2 * core - x, 2 - 2 * core + x, 2 * core + 1 - x, 2 * core + x]),
        context, cotangent,
    )
    theirs = send(theirs, "core")
    piece_fc2 = run(partial(sum_of, parts=4), piece_fc2, other_fc2)
    chunk = run(sum_of, own, from_up, from_down)
    away, keep = run(add_parts, away, keep, theirs)
    away = send(away, "xlo")
    g_up, g_down = run(add_halves, g_up, g_down, g_high, g_low)
    keep = run(add, keep, away)
    (piece_fc2,) = run.after(piece_fc2)
    tot_fc2 = gather(piece_fc2)
    g_up, g_down, chunk, keep = run.after(g_up, g_down, chunk, keep)
    other = send(chunk, "xhi")
    g_from_up, g_from_down = send(g_up, "z^1"), send(g_down, "z^3")
    away = send(keep, "y^1")
    x_rows, cot_rows = run(take_rows, at, layer_input, cotangent)
    keep = run(add, keep, away)
    away = send(keep, "y^3")
    rows, output = run(output_rows, at, chunk, other, x_rows, out_bias[None], fc2_bias[None])
    keep = run(add, keep, away)
    g_from_up, g_from_down = run.wait(g_from_up), run.wait(g_from_down)
    piece = run.wait(piece)
    rows, piece = run.after(rows, piece)
    other_piece = send(piece, "xlo")
    near_up, near_down = send(rows, "z^1"), send(rows, "z^3")
    g_chunk = run(sum_of, g_own, g_from_up, g_from_down)
    output, low, high = run(
        partial(place_rows, copies=near_copies), output, [near_up, near_down], near
    )
    piece = run(partial(sum_of, parts=4), piece, other_piece)
    side = gather(piece)
    g_chunk, low, high = run.after(g_chunk, low, high)
    g_other = send(g_chunk, "xhi")
    low, high = send(low, "z^3"), send(high, "z^1")
    keep = run.wait(keep)
    away = send(keep, "xlo")
    tot_fc2 = run(copy_of, tot_fc2)
    (output,) = run(place_rows, output, [low, high], far)
    g_rows, grad_input, sums = run(
        input_grad_rows, at, g_chunk, g_other, x_rows, cot_rows, ln_gain[None]
    )
    g_near_up, g_near_down = send(g_rows, "z^1"), send(g_rows, "z^3")
    biases = jnp.concatenate(
        [sum_out[0], sum_pre[0], sum_proj.reshape(-1), jnp.zeros((256,), F32)]
    ).reshape(8, width // 4)
    sums = jnp.concatenate([sums.reshape(8, width // 4), biases], axis=0)
    for move in ("core", "y^1", "y^2", "xlo"):
        sums = run(add, sums, send(sums, move))
    mine = (keep, run.wait(away))
    theirs = [send(part, "core") for part in mine]
    places = jnp.stack([2 * core + x, 2 * core + 1 - x, 2 - 2 * core + x, 3 - 2 * core - x])
    norm_sums = run.wait(sums[:8])
    other_sums = send(norm_sums, "z^1")
    tot_out = run(assemble, places, *mine, *theirs)
    rest = sums[8:].reshape(-1)
    tot_out_bias = run.wait(rest[:width])
    tot_fc1_bias = run.wait(rest[width : width + inner])
    tot_qkv_bias = run.wait(rest[width + inner : width + inner + 3 * local].reshape(3, local))
    tot_fc2_bias = run(add, tot_out_bias[None])[0]
    norm_sums = run(add, norm_sums, other_sums)
    other_sums = send(norm_sums, "z^2")
    grad_input, g_low, g_high = run(
        partial(place_rows, copies=near_copies), grad_input, [g_near_up, g_near_down], near
    )
    g_low, g_high = send(g_low, "z^3"), send(g_high, "z^1")
    tot_fc1, tot_qkv = run(lambda side: split_grads(side, inner, local), side)
    norm_sums = run(add, norm_sums, other_sums)
    (grad_input,) = run(place_rows, grad_input, [g_low, g_high], far)
    gain, shift = norm_sums.reshape(2, width)
    return (
        output,
        grad_input,
        gain,
        shift,
        jnp.transpose(tot_qkv, (1, 0, 2)),
        tot_qkv_bias,
        tot_out,
        tot_out_bias,
        tot_fc1,
        tot_fc1_bias,
        tot_fc2,
        tot_fc2_bias,
    )


def solution(mesh):
    in_specs = (
        P("dp", None),
        P(),
        P(),
        P(None, None, "tensor"),
        P(None, "tensor"),
        P("tensor", None),
        P(),
        P(None, "tensor"),
        P("tensor"),
        P("tensor", None),
        P(),
        P("dp", None),
        P("dp", None),
        P("dp", None),
    )
    out_specs = (
        P("dp", None),
        P("dp", None),
        P(),
        P(),
        P(None, None, "tensor"),
        P(None, "tensor"),
        P("tensor", None),
        P(),
        P(None, "tensor"),
        P("tensor"),
        P("tensor", None),
        P(),
    )
    return jax.shard_map(
        per_device, mesh=mesh, in_specs=in_specs, out_specs=out_specs, check_vma=False
    )
```

```python
from functools import partial

import jax
import jax.numpy as jnp
import numpy as np
from jax import lax
from jax.experimental import pallas as pl
from jax.experimental.pallas import tpu as pltpu
from jax.sharding import PartitionSpec as P

HEAD_DIM = 64
ROT = 32
EPSILON = 1e-05
MASKED = -1e30
F32, BF16 = jnp.float32, jnp.bfloat16
ANY = pl.ANY


def shape(dims, dtype=F32):
    return jax.ShapeDtypeStruct(dims, dtype)


def kernel(body, out, grid, in_specs, out_specs, scratch=(), scalars=0, aliases=None, vmem=40, us=3):
    return pl.pallas_call(
        body,
        out_shape=out,
        grid_spec=pltpu.PrefetchScalarGridSpec(
            num_scalar_prefetch=scalars,
            grid=grid,
            in_specs=in_specs,
            out_specs=out_specs,
            scratch_shapes=scratch,
        ),
        input_output_aliases=aliases or {},
        compiler_params=pltpu.CompilerParams(vmem_limit_bytes=vmem << 20),
        cost_estimate=pl.CostEstimate(
            flops=0, bytes_accessed=int(us * 3e6), transcendentals=0
        ),
    )


def whole(dims):
    return pl.BlockSpec(dims, lambda *_: (0,) * len(dims))


def dot(a, b):
    return jnp.dot(a, b, preferred_element_type=F32)


def dot_nt(a, b):
    return lax.dot_general(a, b, (((1,), (1,)), ((), ())), preferred_element_type=F32)


def dot_tn(a, b):
    return lax.dot_general(a, b, (((0,), (0,)), ((), ())), preferred_element_type=F32)


X_LO, Y, CORE = 2, 4, 2
Z, X_HI = 4, 2


def dp_moves(step):
    pairs = []
    for x in range(X_LO):
        for y in range(Y):
            for c in range(CORE):
                x2, y2, c2 = step(x, y, c)
                there = ((x2 % X_LO) * Y + y2 % Y) * CORE + c2 % CORE
                pairs.append(((x * Y + y) * CORE + c, there))
    return pairs


def tensor_moves(step):
    pairs = []
    for z in range(Z):
        for x in range(X_HI):
            z2, x2 = step(z, x)
            pairs.append((z * X_HI + x, (z2 % Z) * X_HI + x2 % X_HI))
    return pairs


MOVES = {
    "core": ("dp", dp_moves(lambda x, y, c: (x, y, c + 1))),
    "y^1": ("dp", dp_moves(lambda x, y, c: (x, y ^ 1, c))),
    "y^2": ("dp", dp_moves(lambda x, y, c: (x, y ^ 2, c))),
    "xlo": ("dp", dp_moves(lambda x, y, c: (x + 1, y, c))),
    "y^3": ("dp", dp_moves(lambda x, y, c: (x, y ^ 3, c))),
    "z^1": ("tensor", tensor_moves(lambda z, x: (z ^ 1, x))),
    "z^3": ("tensor", tensor_moves(lambda z, x: (z ^ 3, x))),
    "z^2": ("tensor", tensor_moves(lambda z, x: (z ^ 2, x))),
    "xhi": ("tensor", tensor_moves(lambda z, x: (z, x + 1))),
}


def send(array, move):
    axis, pairs = MOVES[move]
    return lax.ppermute(array, axis, pairs)


def norm_rows(x):
    center = x - jnp.mean(x, axis=-1, keepdims=True)
    inv_std = lax.rsqrt(jnp.mean(center * center, axis=-1, keepdims=True) + EPSILON)
    return center * inv_std, inv_std


def gelu_and_slope(v):
    a = np.float32(np.sqrt(2 / np.pi))
    b = np.float32(a * 0.044715)
    square = v * v
    h = 0.5 * jnp.tanh(v * (a + b * square)) + 0.5
    return v * h, h + v * (2 * a + 6 * b * square) * (h - h * h)


def first_body(
    x_ref, gain_ref, bias_ref, w_ref, b_ref, cot_ref, wo_ref,
    low_ref, hidden_ref, slope_ref, grad_ref, context_ref, sum_ref, turned, total,
):
    i = pl.program_id(0)
    block, step = x_ref.shape[0], w_ref.shape[1]
    blocks, tiles = low_ref.shape[0] // block, turned.shape[0] // step

    @pl.when(i < blocks)
    def _():
        normed, _ = norm_rows(x_ref[...])
        low = (normed * gain_ref[...] + bias_ref[...]).astype(BF16)
        low_ref[pl.ds(pl.multiple_of(i * block, block), block), :] = low

    @pl.when((i >= blocks) & (i < blocks + tiles))
    def _():
        hidden, slope = gelu_and_slope(dot(low_ref[...], w_ref[...]) + b_ref[...])
        hidden = hidden.astype(BF16)
        hidden_ref[...] = hidden
        turned[pl.ds(pl.multiple_of((i - blocks) * step, step), step), :] = hidden.T
        slope_ref[...] = slope.astype(BF16)

    @pl.when(i == blocks + tiles)
    def _():
        total[...] = jnp.zeros_like(total)

    @pl.when(i >= blocks + tiles)
    def _():
        cot = cot_ref[...]
        grad_ref[...] = dot(turned[...], cot)
        total[...] += dot_nt(cot, wo_ref[...])
        sum_ref[...] = jnp.sum(cot.astype(F32), axis=0, keepdims=True)

    @pl.when(i == pl.num_programs(0) - 1)
    def _():
        context_ref[...] = total[...].astype(BF16)


def first_products(x, gain, bias, w, b, cot, w_out, block=256, step=256, wide=512):
    rows, width = x.shape
    cols, heads = w.shape[1], w_out.shape[0]
    blocks, tiles, last = rows // block, cols // step, width // wide

    def tile(j):
        return jnp.clip(j - blocks, 0, tiles - 1)

    def final(j):
        return jnp.maximum(j - blocks - tiles, 0)

    out = pl.BlockSpec((rows, step), lambda j: (0, tile(j)))
    return kernel(
        first_body,
        (
            shape((rows, width), BF16),
            shape((rows, cols), BF16),
            shape((rows, cols), BF16),
            shape((cols, width)),
            shape((rows, heads), BF16),
            shape((1, width)),
        ),
        (blocks + tiles + last,),
        [
            pl.BlockSpec((block, width), lambda j: (jnp.minimum(j, blocks - 1), 0)),
            whole((1, width)),
            whole((1, width)),
            pl.BlockSpec((width, step), lambda j: (0, tile(j))),
            pl.BlockSpec((1, step), lambda j: (0, tile(j))),
            pl.BlockSpec((rows, wide), lambda j: (0, final(j))),
            pl.BlockSpec((heads, wide), lambda j: (0, final(j))),
        ],
        (
            whole((rows, width)),
            out,
            out,
            pl.BlockSpec((cols, wide), lambda j: (0, final(j))),
            whole((rows, heads)),
            pl.BlockSpec((1, wide), lambda j: (0, final(j))),
        ),
        scratch=[pltpu.VMEM((cols, rows), BF16), pltpu.VMEM((rows, heads), F32)],
        us=20,
        vmem=60,
    )(x, gain, bias, w, b, cot, w_out)


def side_body(
    ln_ref, cot_ref, w_ref, slope_ref, proj_ref, out_ref, pre_ref, sum_ref
):
    i = pl.program_id(0)
    tile, step = w_ref.shape[0], proj_ref.shape[2]
    n = pre_ref.shape[1]
    tiles = n // tile

    @pl.when(i < tiles)
    def _():
        grad = (dot_nt(cot_ref[...], w_ref[...]) * slope_ref[...]).astype(BF16)
        pre_ref[:, pl.ds(pl.multiple_of(i * tile, tile), tile)] = grad
        sum_ref[...] = jnp.sum(grad.astype(F32), axis=0, keepdims=True)

    @pl.when(i >= tiles)
    def _():
        turned = ln_ref[...].T
        out_ref[:, :n] = dot(turned, pre_ref[...])
        for c in range(3):
            out_ref[:, n + c * step : n + (c + 1) * step] = dot(turned, proj_ref[c])


def side_grads(ln, cot, w, slope, proj, block=512, tile=256):
    rows, m = ln.shape
    n, step = w.shape[0], proj.shape[2]
    tiles = n // tile

    def first(j):
        return jnp.minimum(j, tiles - 1)

    def second(j):
        return jnp.maximum(j - tiles, 0)

    return kernel(
        side_body,
        (shape((m, n + 3 * step)), shape((rows, n), BF16), shape((1, n))),
        (tiles + m // block,),
        [
            pl.BlockSpec((rows, block), lambda j: (0, second(j))),
            whole((rows, m)),
            pl.BlockSpec((tile, m), lambda j: (first(j), 0)),
            pl.BlockSpec((rows, tile), lambda j: (0, first(j))),
            whole((3, rows, step)),
        ],
        (
            pl.BlockSpec((block, n + 3 * step), lambda j: (second(j), 0)),
            whole((rows, n)),
            pl.BlockSpec((1, tile), lambda j: (0, first(j))),
        ),
        us=18,
        vmem=60,
    )(ln, cot, w, slope, proj)


def split_body(side, one, three):
    n, step = one.shape[1], three.shape[2]
    one[...] = side[:, :n]
    for c in range(3):
        three[c] = side[:, n + c * step : n + (c + 1) * step]


def split_grads(side, n, step, tile=512):
    rows = side.shape[0]
    return kernel(
        split_body,
        (shape((rows, n)), shape((3, rows, step))),
        (rows // tile,),
        [pl.BlockSpec((tile, side.shape[1]), lambda i: (i, 0))],
        (
            pl.BlockSpec((tile, n), lambda i: (i, 0)),
            pl.BlockSpec((3, tile, step), lambda i: (0, i, 0)),
        ),
        us=11,
        vmem=40,
    )(side)


def out_grad_body(at, context, cot, theirs, away, keep, left, turned):
    @pl.when(pl.program_id(0) == 0)
    def _():
        turned[...] = context[...].T
        for i in range(4):
            row = pl.multiple_of(at[i] * 64, 64)
            left[i * 64 : (i + 1) * 64, :] = turned[pl.ds(row, 64), :]

    total = dot(left[...], cot[...])
    theirs[...] = total[:128]
    away[...] = total[128:192]
    keep[...] = total[192:]


def out_grad(at, context, cot, step=512):
    rows, width = cot.shape
    m = context.shape[1]

    def tile(count):
        return pl.BlockSpec((count, step), lambda j, at: (0, j))

    return kernel(
        out_grad_body,
        (shape((128, width)), shape((64, width)), shape((64, width))),
        (width // step,),
        [whole((rows, m)), tile(rows)],
        (tile(128), tile(64), tile(64)),
        scratch=[pltpu.VMEM((m, rows), BF16)] * 2,
        scalars=1,
        us=3,
        vmem=60,
    )(at, context, cot)


def add_parts_body(away_in, keep_in, first, second, away, keep):
    away[...] = away_in[...] + first[...]
    keep[...] = keep_in[...] + second[...]


def add_parts(away, keep, both):
    rows, width = keep.shape
    first = pl.BlockSpec((rows, width), lambda i: (0, 0))
    second = pl.BlockSpec((rows, width), lambda i: (1, 0))
    return kernel(
        add_parts_body,
        (shape((rows, width)), shape((rows, width))),
        (1,),
        [first, first, first, second],
        (first, first),
        us=2,
        vmem=16,
    )(away, keep, both, both)


def assemble_body(at, *refs):
    del at
    i = pl.program_id(0)
    for k, piece in enumerate(refs[:-1]):

        @pl.when(i == k)
        def _(piece=piece):
            refs[-1][...] = piece[...]


def assemble(at, *pieces):
    rows, width = pieces[0].shape
    return kernel(
        assemble_body,
        shape((len(pieces) * rows, width)),
        (len(pieces),),
        [whole((rows, width))] * len(pieces),
        pl.BlockSpec((rows, width), lambda i, at: (at[i], 0)),
        scalars=1,
        us=2,
        vmem=16,
    )(at, *pieces)


def copy_body(source, out):
    out[...] = source[...]


def copy_of(source, step=256):
    rows, width = source.shape
    spec = pl.BlockSpec((step, width), lambda i: (i, 0))
    return kernel(
        copy_body, shape((rows, width)), (rows // step,), [spec], spec, us=6, vmem=60    )(source)


def swap_halves(u, low, high):
    width = u.shape[1]
    return pltpu.roll(u, width - ROT // 2, 1) * low + pltpu.roll(u, ROT // 2, 1) * high


def fill_tables(pos_ref, rate_ref, cos_ref, low_ref, high_ref):
    angles = rate_ref[...] * pos_ref[...].astype(F32)
    count = ROT // 2
    entry = lax.broadcasted_iota(jnp.int32, (count, 2 * HEAD_DIM), 0)
    lane = lax.broadcasted_iota(jnp.int32, (count, 2 * HEAD_DIM), 1) % HEAD_DIM
    first = jnp.where(lane == entry, 1.0, 0.0).astype(F32)
    second = jnp.where(lane == entry + count, 1.0, 0.0).astype(F32)

    def spread(table, lanes):
        return lax.dot_general(
            table, lanes, (((0,), (0,)), ((), ())),
            precision=lax.Precision.HIGHEST, preferred_element_type=F32,
        )

    sine = jnp.sin(angles)
    kept = jnp.where(lane[:1] >= ROT, 1.0, 0.0)
    cos_ref[...] = spread(jnp.cos(angles), first + second) + kept
    low_ref[...] = spread(sine, -first)
    high_ref[...] = spread(sine, second)


def rotary_rates():
    steps_half = np.arange(0, ROT, 2).astype(np.float32) / np.float32(ROT)
    return jnp.asarray((np.float32(10000.0) ** (-steps_half))[:, None])


def qkv_body(ln_ref, w_ref, b_ref, pos_ref, rate_ref, out_ref, cos_ref, low_ref, high_ref):
    c = pl.program_id(0)

    @pl.when(c == 0)
    def _():
        fill_tables(pos_ref, rate_ref, cos_ref, low_ref, high_ref)

    u = dot(ln_ref[...], w_ref[0]) + b_ref[pl.ds(c, 1), :]

    @pl.when(c == 2)
    def _():
        out_ref[0] = u.astype(BF16)

    @pl.when(c < 2)
    def _():
        for lane in range(0, u.shape[1], 128):
            part = u[:, lane : lane + 128]
            turned = part * cos_ref[...] + swap_halves(part, low_ref[...], high_ref[...])
            out_ref[0, :, lane : lane + 128] = turned.astype(BF16)


def project(ln, w_parts, bias, positions, rates):
    rows, width = ln.shape
    cols = w_parts.shape[2]
    return kernel(
        qkv_body,
        (shape((3, rows, cols), BF16),) + (shape((rows, 128)),) * 3,
        (3,),
        [
            whole((rows, width)),
            pl.BlockSpec((1, width, cols), lambda c: (c, 0, 0)),
            whole((3, cols)),
            whole((1, rows)),
            whole((ROT // 2, 1)),
        ],
        (pl.BlockSpec((1, rows, cols), lambda c: (c, 0, 0)),) + (whole((rows, 128)),) * 3,
        us=7,
        vmem=60,
    )(ln, w_parts, bias, positions, rates)


def attention_body(
    q_ref, k_ref, v_ref, g_ref, seg_ref, cos_ref, low_ref, high_ref,
    context_ref, grad_ref, sum_ref, dq, dk, dv,
):
    rows = q_ref.shape[1]
    step = 384
    scale = np.float32(HEAD_DIM**-0.5)
    lane = lax.broadcasted_iota(jnp.int32, (rows, 128), 1)
    heads = []
    for h in range(2):
        mine = (lane >= h * HEAD_DIM) & (lane < (h + 1) * HEAD_DIM)
        heads.append(
            [
                jnp.where(mine, ref, jnp.zeros_like(ref))
                for ref in (q_ref[0] * scale.astype(BF16), k_ref[0], v_ref[0], g_ref[...])
            ]
        )
    seg_row = seg_ref[...].astype(F32)
    seg_col = jnp.broadcast_to(seg_row, (128, rows)).T[:, :1]
    dk[...] = jnp.zeros_like(dk)
    dv[...] = jnp.zeros_like(dv)
    for i in range(rows // step):
        top = slice(i * step, (i + 1) * step)
        seen = (i + 1) * step
        row = lax.broadcasted_iota(jnp.int32, (step, seen), 0) + i * step
        col = lax.broadcasted_iota(jnp.int32, (step, seen), 1)
        allowed = (seg_col[top, :] == seg_row[:, :seen]) & (col <= row)
        context = jnp.zeros((step, 128), F32)
        grad_q = jnp.zeros((step, 128), F32)
        for q, k, v, g in heads:
            scores = jnp.where(allowed, dot_nt(q[top], k[:seen]), MASKED)
            peak = jnp.max(scores, axis=-1, keepdims=True)
            raised = jnp.exp(scores - peak)
            probs = raised * (1.0 / jnp.sum(raised, axis=-1, keepdims=True))
            probs_low = probs.astype(BF16)
            context += dot(probs_low, v[:seen])
            grad_probs = dot_nt(g[top], v[:seen])
            delta = jnp.sum(probs * grad_probs, axis=-1, keepdims=True)
            grad_scores = (probs * (grad_probs - delta)).astype(BF16)
            grad_q += dot(grad_scores, k[:seen])
            dk[:seen, :] += dot_tn(grad_scores, q[top])
            dv[:seen, :] += dot_tn(probs_low, g[top])
        context_ref[top, :] = context.astype(BF16)
        dq[top, :] = grad_q * scale
    for c, grad in enumerate((dq, dk, dv)):
        u = grad[...]
        if c < 2:
            u = u * cos_ref[...] - swap_halves(u, low_ref[...], high_ref[...])
        u = u.astype(BF16)
        grad_ref[c] = u
        sum_ref[c] = jnp.sum(u.astype(F32), axis=0, keepdims=True)


def attention(qkv, grad_context, segments, tables):
    _, rows, cols = qkv.shape
    pair = pl.BlockSpec((rows, 128), lambda p: (0, p))
    return kernel(
        attention_body,
        (shape((rows, cols), BF16), shape((3, rows, cols), BF16), shape((3, 1, cols))),
        (cols // 128,),
        [pl.BlockSpec((1, rows, 128), lambda p, c=c: (c, 0, p)) for c in range(3)]
        + [pair, whole((1, rows))]
        + [whole((rows, 128))] * 3,
        (
            pair,
            pl.BlockSpec((3, rows, 128), lambda p: (0, 0, p)),
            pl.BlockSpec((3, 1, 128), lambda p: (0, 0, p)),
        ),
        scratch=[pltpu.VMEM((rows, 128), F32)] * 3,
        us=12,
        vmem=60,
    )(qkv, qkv, qkv, grad_context, segments, *tables)


def chunks_of(z):
    return jnp.stack([z ^ 2, z ^ 1, z ^ 3, z]).astype(jnp.int32)


def put_chunks(outs, total):
    row = 0
    for out in outs:
        out[...] = total[row : row + out.shape[0], :]
        row += out.shape[0]


def chunk_rows(count):
    return [count // 2, count // 2, count, count, count]


def branch_body(at, *refs):
    lefts, rights = refs[:8], refs[8:10]
    outs, hidden, context = refs[10:15], refs[15], refs[16]
    count = outs[-1].shape[0]

    @pl.when(pl.program_id(0) == 0)
    def _():
        for i in range(4):
            hidden[i * count : (i + 1) * count, :] = lefts[i][...]
            context[i * count : (i + 1) * count, :] = lefts[4 + i][...]

    total = dot(hidden[...], rights[0][...]) + dot(context[...], rights[1][...])
    put_chunks(outs, total)


def branch_sums(at, hidden, context, w_fc2, w_out, step=512):
    rows, inner = hidden.shape
    heads = context.shape[1]
    width = w_fc2.shape[1]
    count = rows // 4

    def chunk(cols, i):
        return pl.BlockSpec((count, cols), lambda j, at, i=i: (at[i], 0))

    return kernel(
        branch_body,
        [shape((n, width)) for n in chunk_rows(count)],
        (width // step,),
        [chunk(inner, i) for i in range(4)]
        + [chunk(heads, i) for i in range(4)]
        + [
            pl.BlockSpec((inner, step), lambda j, at: (0, j)),
            pl.BlockSpec((heads, step), lambda j, at: (0, j)),
        ],
        [pl.BlockSpec((n, step), lambda j, at: (0, j)) for n in chunk_rows(count)],
        scratch=[pltpu.VMEM((rows, inner), BF16), pltpu.VMEM((rows, heads), BF16)],
        scalars=1,
        us=9,
        vmem=60,
    )(at, *[hidden] * 4, *[context] * 4, w_fc2, w_out)


def grad_ln_body(at, *refs):
    lefts, rights = refs[:8], refs[8:10]
    outs, pre, proj = refs[10:15], refs[15], refs[16]
    count = outs[-1].shape[0]

    @pl.when(pl.program_id(0) == 0)
    def _():
        for i in range(4):
            pre[i * count : (i + 1) * count, :] = lefts[i][...]
            for c in range(3):
                proj[c, i * count : (i + 1) * count, :] = lefts[4 + i][c]

    total = dot_nt(pre[...], rights[0][...])
    for c in range(3):
        total += dot_nt(proj[c], rights[1][c])
    put_chunks(outs, total)


def grad_ln_sums(at, pre, proj, w_fc1, w_parts, step=512):
    rows, inner = pre.shape
    heads = proj.shape[2]
    width = w_fc1.shape[0]
    count = rows // 4
    return kernel(
        grad_ln_body,
        [shape((n, width)) for n in chunk_rows(count)],
        (width // step,),
        [pl.BlockSpec((count, inner), lambda j, at, i=i: (at[i], 0)) for i in range(4)]
        + [pl.BlockSpec((3, count, heads), lambda j, at, i=i: (0, at[i], 0)) for i in range(4)]
        + [
            pl.BlockSpec((step, inner), lambda j, at: (j, 0)),
            pl.BlockSpec((3, step, heads), lambda j, at: (0, j, 0)),
        ],
        [pl.BlockSpec((n, step), lambda j, at: (0, j)) for n in chunk_rows(count)],
        scratch=[pltpu.VMEM((rows, inner), BF16), pltpu.VMEM((3, rows, heads), BF16)],
        scalars=1,
        us=11,
        vmem=60,
    )(at, *[pre] * 4, *[proj] * 4, w_fc1, w_parts)


def add_pair_body(up_in, down_in, high, low, up, down):
    up[...] = up_in[...] + high[...]
    down[...] = down_in[...] + low[...]


def add_halves(up, down, high, low, parts=2):
    rows, width = low.shape
    step = rows // parts
    first = pl.BlockSpec((step, width), lambda i: (i, 0))
    second = pl.BlockSpec((step, width), lambda i: (i + parts, 0))
    return kernel(
        add_pair_body,
        (shape(up.shape), shape(down.shape)),
        (parts,),
        [second, first, first, first],
        (second, first),
        aliases={0: 0, 1: 1},
        us=2,
        vmem=60,
    )(up, down, high, low)


def sum_body(*refs):
    total = refs[0][...]
    for ref in refs[1:-1]:
        total = total + ref[...]
    refs[-1][...] = total


def sum_of(*arrays, parts=3):
    rows, width = arrays[0].shape
    step = rows // parts
    spec = pl.BlockSpec((step, width), lambda i: (i, 0))
    return kernel(
        sum_body, shape((rows, width)), (rows // step,), [spec] * len(arrays), spec,
        us=3,
        vmem=60 if parts > 1 else 16,
    )(*arrays)


def take_body(at, x, cot, x_out, cot_out):
    del at
    x_out[...] = x[...]
    cot_out[...] = cot[...]


def take_rows(at, x, cot, step=48):
    count, width = x.shape[0] // 4, x.shape[1]
    parts = count // step
    here = pl.BlockSpec((step, width), lambda i, at: (i, 0))
    there = pl.BlockSpec((step, width), lambda i, at: (at[3] * parts + i, 0))
    return kernel(
        take_body,
        (shape((count, width)), shape((count, width), BF16)),
        (parts,),
        [there, there],
        (here, here),
        scalars=1,
        us=3,
        vmem=60,
    )(at, x, cot)


def last_body(at, chunk, other, x, ob, fb, rows, out):
    del at
    total = chunk[...] + other[...] + x[...] + ob[...] + fb[...]
    rows[...] = total
    out[...] = total


def output_rows(at, chunk, other, x, out_bias, fc2_bias, step=48):
    count, width = chunk.shape
    parts = count // step
    here = pl.BlockSpec((step, width), lambda i, at: (i, 0))
    there = pl.BlockSpec((step, width), lambda i, at: (at[3] * parts + i, 0))
    return kernel(
        last_body,
        (shape((count, width)), shape((4 * count, width))),
        (parts,),
        [here, here, here, whole((1, width)), whole((1, width))],
        (here, there),
        scalars=1,
        us=4,
        vmem=16,
    )(at, chunk, other, x, out_bias, fc2_bias)


def norm_back_body(at, chunk, other, x, cot, gain, rows, out, sums):
    del at

    @pl.when(pl.program_id(0) == 0)
    def _():
        sums[...] = jnp.zeros_like(sums)

    grad = chunk[...] + other[...]
    normed, inv_std = norm_rows(x[...])
    sums[0:1, :] += jnp.sum(grad * normed, axis=0, keepdims=True)
    sums[1:2, :] += jnp.sum(grad, axis=0, keepdims=True)
    scaled = grad * gain[...]
    mean_scaled = jnp.mean(scaled, axis=-1, keepdims=True)
    mean_cross = jnp.mean(scaled * normed, axis=-1, keepdims=True)
    total = cot[...].astype(F32) + inv_std * (scaled - mean_scaled - normed * mean_cross)
    rows[...] = total
    out[...] = total


def input_grad_rows(at, chunk, other, x, cot, gain, step=48):
    count, width = chunk.shape
    parts = count // step
    here = pl.BlockSpec((step, width), lambda i, at: (i, 0))
    there = pl.BlockSpec((step, width), lambda i, at: (at[3] * parts + i, 0))
    return kernel(
        norm_back_body,
        (shape((count, width)), shape((4 * count, width)), shape((2, width))),
        (parts,),
        [here, here, here, here, whole((1, width))],
        (here, there, whole((2, width))),
        scalars=1,
        us=5,
        vmem=16,
    )(at, chunk, other, x, cot, gain)


def place_body(at, *refs, starts, sizes, copies):
    i = pl.program_id(0)
    count = len(starts)
    pieces, out, extra = refs[:count], refs[count + 1], refs[count + 2 :]
    for piece, start, size in zip(pieces, starts, sizes):

        @pl.when((i >= start) & (i < start + size))
        def _(piece=piece):
            out[...] = piece[...]

    for copy, (which, first, size) in zip(extra, copies):
        begin = starts[which] + first

        @pl.when((i >= begin) & (i < begin + size))
        def _(copy=copy, which=which):
            copy[...] = pieces[which][...]


def place_rows(out, pieces, blocks, copies=(), step=48):
    width = out.shape[1]
    sizes = [piece.shape[0] // step for piece in pieces]
    starts = [sum(sizes[:k]) for k in range(len(sizes))]

    def part(start, size):
        return pl.BlockSpec((step, width), lambda i, at: (jnp.clip(i - start, 0, size - 1), 0))

    return kernel(
        partial(place_body, starts=starts, sizes=sizes, copies=copies),
        [shape(out.shape)] + [shape((size * step, width)) for _, _, size in copies],
        (sum(sizes),),
        [part(start, size) for start, size in zip(starts, sizes)]
        + [pl.BlockSpec(memory_space=ANY)],
        [pl.BlockSpec((step, width), lambda i, at: (at[i], 0))]
        + [part(starts[which] + first, size) for which, first, size in copies],
        scalars=1,
        aliases={1 + len(pieces): 0},
        us=5,
        vmem=16,
    )(blocks, *pieces, out)


class Order:
    def __init__(self):
        self.last = None

    def __call__(self, step, *args):
        if self.last is not None:
            args, _ = lax.optimization_barrier((args, self.last))
        out = step(*args)
        self.last = jax.tree.leaves(out)[0]
        return out

    def after(self, *arrays):
        arrays, _ = lax.optimization_barrier((arrays, self.last))
        return arrays

    def wait(self, array):
        array, self.last = lax.optimization_barrier((array, self.last))
        return array


ROW_GROUPS = [[x * Y * CORE + i for i in range(Y * CORE)] for x in range(X_LO)]


def scatter(part):
    return lax.psum_scatter(
        part, "dp", scatter_dimension=0, axis_index_groups=ROW_GROUPS, tiled=True
    )


def gather(piece):
    return lax.all_gather(piece, "dp", axis=0, axis_index_groups=ROW_GROUPS, tiled=True)


def per_device(
    layer_input,
    ln_gain,
    ln_bias,
    w_qkv,
    qkv_bias,
    w_out,
    out_bias,
    w_fc1,
    fc1_bias,
    w_fc2,
    fc2_bias,
    segments,
    positions,
    cotangent,
):
    width = layer_input.shape[1]
    inner, local = w_fc1.shape[1], w_qkv.shape[2]
    at = chunks_of(lax.axis_index("tensor") // X_HI)
    at_dp = lax.axis_index("dp")
    x, core = at_dp // (Y * CORE), lax.rem(at_dp, CORE)
    run = Order()
    w_parts = jnp.transpose(w_qkv, (1, 0, 2))
    blocks = at[:3, None] * 4 + jnp.arange(4, dtype=jnp.int32)[None, :]
    near, far = blocks[1:].reshape(-1), blocks[0]
    near_copies = ((0, 0, 2), (1, 2, 2))
    add = partial(sum_of, parts=1)

    ln, hidden, slope, grad_fc2, grad_context, sum_out = run(
        first_products,
        layer_input, ln_gain[None], ln_bias[None], w_fc1, fc1_bias[None], cotangent, w_out,
    )
    piece_fc2 = scatter(grad_fc2)
    qkv, *tables = run(project, ln, w_parts, qkv_bias, positions, rotary_rates())
    context, grad_proj, sum_proj = run(attention, qkv, grad_context, segments, tables)
    low, high, up, down, own = run(branch_sums, at, hidden, context, w_fc2, w_out)
    low, high = send(low, "z^1"), send(high, "z^3")
    side, grad_pre, sum_pre = run(side_grads, ln, cotangent, w_fc2, slope, grad_proj)
    low, high = run.wait(low), run.wait(high)
    piece_fc2 = run.wait(piece_fc2)
    (side,) = run.after(side)
    piece = scatter(side)
    other_fc2 = send(*run.after(piece_fc2), "xlo")
    up, down = run(add_halves, up, down, high, low)
    from_up, from_down = send(up, "z^1"), send(down, "z^3")
    g_low, g_high, g_up, g_down, g_own = run(
        grad_ln_sums, at, grad_pre, grad_proj, w_fc1, w_parts
    )
    g_low, g_high = send(g_low, "z^1"), send(g_high, "z^3")
    theirs, away, keep = run(
        out_grad,
        jnp.stack([3 - 2 * core - x, 2 - 2 * core + x, 2 * core + 1 - x, 2 * core + x]),
        context, cotangent,
    )
    theirs = send(theirs, "core")
    piece_fc2 = run(partial(sum_of, parts=4), piece_fc2, other_fc2)
    chunk = run(sum_of, own, from_up, from_down)
    away, keep = run(add_parts, away, keep, theirs)
    away = send(away, "xlo")
    g_up, g_down = run(add_halves, g_up, g_down, g_high, g_low)
    keep = run(add, keep, away)
    (piece_fc2,) = run.after(piece_fc2)
    tot_fc2 = gather(piece_fc2)
    g_up, g_down, chunk, keep = run.after(g_up, g_down, chunk, keep)
    other = send(chunk, "xhi")
    g_from_up, g_from_down = send(g_up, "z^1"), send(g_down, "z^3")
    away = send(keep, "y^1")
    x_rows, cot_rows = run(take_rows, at, layer_input, cotangent)
    keep = run(add, keep, away)
    away = send(keep, "y^3")
    rows, output = run(output_rows, at, chunk, other, x_rows, out_bias[None], fc2_bias[None])
    keep = run(add, keep, away)
    g_from_up, g_from_down = run.wait(g_from_up), run.wait(g_from_down)
    piece = run.wait(piece)
    rows, piece = run.after(rows, piece)
    other_piece = send(piece, "xlo")
    near_up, near_down = send(rows, "z^1"), send(rows, "z^3")
    g_chunk = run(sum_of, g_own, g_from_up, g_from_down)
    piece = run(
        lambda piece, other, *_: sum_of(piece, other, parts=4),
        piece, other_piece, near_up, near_down, g_chunk,
    )
    side = gather(piece)
    (g_chunk,) = run.after(g_chunk)
    g_other = send(g_chunk, "xhi")
    output, low, high = run(
        partial(place_rows, copies=near_copies), output, [near_up, near_down], near
    )
    low, high = send(low, "z^3"), send(high, "z^1")
    keep = run.wait(keep)
    away = send(keep, "xlo")
    tot_fc2 = run(copy_of, tot_fc2)
    (output,) = run(place_rows, output, [low, high], far)
    g_rows, grad_input, sums = run(
        input_grad_rows, at, g_chunk, g_other, x_rows, cot_rows, ln_gain[None]
    )
    g_near_up, g_near_down = send(g_rows, "z^1"), send(g_rows, "z^3")
    biases = jnp.concatenate(
        [sum_out[0], sum_pre[0], sum_proj.reshape(-1), jnp.zeros((256,), F32)]
    ).reshape(8, width // 4)
    sums = jnp.concatenate([sums.reshape(8, width // 4), biases], axis=0)
    for move in ("core", "y^1", "y^2", "xlo"):
        sums = run(add, sums, send(sums, move))
    mine = (keep, run.wait(away))
    theirs = [send(part, "core") for part in mine]
    places = jnp.stack([2 * core + x, 2 * core + 1 - x, 2 - 2 * core + x, 3 - 2 * core - x])
    norm_sums = run.wait(sums[:8])
    other_sums = send(norm_sums, "z^1")
    tot_out = run(assemble, places, *mine, *theirs)
    rest = sums[8:].reshape(-1)
    tot_out_bias = run.wait(rest[:width])
    tot_fc1_bias = run.wait(rest[width : width + inner])
    tot_qkv_bias = run.wait(rest[width + inner : width + inner + 3 * local].reshape(3, local))
    tot_fc2_bias = run(add, tot_out_bias[None])[0]
    norm_sums = run(add, norm_sums, other_sums)
    other_sums = send(norm_sums, "z^2")
    grad_input, g_low, g_high = run(
        partial(place_rows, copies=near_copies), grad_input, [g_near_up, g_near_down], near
    )
    g_low, g_high = send(g_low, "z^3"), send(g_high, "z^1")
    tot_fc1, tot_qkv = run(lambda side: split_grads(side, inner, local), side)
    norm_sums = run(add, norm_sums, other_sums)
    (grad_input,) = run(place_rows, grad_input, [g_low, g_high], far)
    gain, shift = norm_sums.reshape(2, width)
    return (
        output,
        grad_input,
        gain,
        shift,
        jnp.transpose(tot_qkv, (1, 0, 2)),
        tot_qkv_bias,
        tot_out,
        tot_out_bias,
        tot_fc1,
        tot_fc1_bias,
        tot_fc2,
        tot_fc2_bias,
    )


def solution(mesh):
    in_specs = (
        P("dp", None),
        P(),
        P(),
        P(None, None, "tensor"),
        P(None, "tensor"),
        P("tensor", None),
        P(),
        P(None, "tensor"),
        P("tensor"),
        P("tensor", None),
        P(),
        P("dp", None),
        P("dp", None),
        P("dp", None),
    )
    out_specs = (
        P("dp", None),
        P("dp", None),
        P(),
        P(),
        P(None, None, "tensor"),
        P(None, "tensor"),
        P("tensor", None),
        P(),
        P(None, "tensor"),
        P("tensor"),
        P("tensor", None),
        P(),
    )
    return jax.shard_map(
        per_device, mesh=mesh, in_specs=in_specs, out_specs=out_specs, check_vma=False
    )
```

```python
from functools import partial

import jax
import jax.numpy as jnp
import numpy as np
from jax import lax
from jax.experimental import pallas as pl
from jax.experimental.pallas import tpu as pltpu
from jax.sharding import PartitionSpec as P

HEAD_DIM = 64
ROT = 32
EPSILON = 1e-05
MASKED = -1e30
F32, BF16 = jnp.float32, jnp.bfloat16
ANY = pl.ANY


def shape(dims, dtype=F32):
    return jax.ShapeDtypeStruct(dims, dtype)


def kernel(body, out, grid, in_specs, out_specs, scratch=(), scalars=0, aliases=None, vmem=40, us=3):
    return pl.pallas_call(
        body,
        out_shape=out,
        grid_spec=pltpu.PrefetchScalarGridSpec(
            num_scalar_prefetch=scalars,
            grid=grid,
            in_specs=in_specs,
            out_specs=out_specs,
            scratch_shapes=scratch,
        ),
        input_output_aliases=aliases or {},
        compiler_params=pltpu.CompilerParams(vmem_limit_bytes=vmem << 20),
        cost_estimate=pl.CostEstimate(
            flops=0, bytes_accessed=int(us * 3e6), transcendentals=0
        ),
    )


def whole(dims):
    return pl.BlockSpec(dims, lambda *_: (0,) * len(dims))


def dot(a, b):
    return jnp.dot(a, b, preferred_element_type=F32)


def dot_nt(a, b):
    return lax.dot_general(a, b, (((1,), (1,)), ((), ())), preferred_element_type=F32)


def dot_tn(a, b):
    return lax.dot_general(a, b, (((0,), (0,)), ((), ())), preferred_element_type=F32)


X_LO, Y, CORE = 2, 4, 2
Z, X_HI = 4, 2


def dp_moves(step):
    pairs = []
    for x in range(X_LO):
        for y in range(Y):
            for c in range(CORE):
                x2, y2, c2 = step(x, y, c)
                there = ((x2 % X_LO) * Y + y2 % Y) * CORE + c2 % CORE
                pairs.append(((x * Y + y) * CORE + c, there))
    return pairs


def tensor_moves(step):
    pairs = []
    for z in range(Z):
        for x in range(X_HI):
            z2, x2 = step(z, x)
            pairs.append((z * X_HI + x, (z2 % Z) * X_HI + x2 % X_HI))
    return pairs


MOVES = {
    "core": ("dp", dp_moves(lambda x, y, c: (x, y, c + 1))),
    "y^1": ("dp", dp_moves(lambda x, y, c: (x, y ^ 1, c))),
    "y^2": ("dp", dp_moves(lambda x, y, c: (x, y ^ 2, c))),
    "xlo": ("dp", dp_moves(lambda x, y, c: (x + 1, y, c))),
    "y^3": ("dp", dp_moves(lambda x, y, c: (x, y ^ 3, c))),
    "z^1": ("tensor", tensor_moves(lambda z, x: (z ^ 1, x))),
    "z^3": ("tensor", tensor_moves(lambda z, x: (z ^ 3, x))),
    "z^2": ("tensor", tensor_moves(lambda z, x: (z ^ 2, x))),
    "xhi": ("tensor", tensor_moves(lambda z, x: (z, x + 1))),
}


def send(array, move):
    axis, pairs = MOVES[move]
    return lax.ppermute(array, axis, pairs)


def norm_rows(x):
    center = x - jnp.mean(x, axis=-1, keepdims=True)
    inv_std = lax.rsqrt(jnp.mean(center * center, axis=-1, keepdims=True) + EPSILON)
    return center * inv_std, inv_std


def gelu_and_slope(v):
    a = np.float32(np.sqrt(2 / np.pi))
    b = np.float32(a * 0.044715)
    square = v * v
    h = 0.5 * jnp.tanh(v * (a + b * square)) + 0.5
    return v * h, h + v * (2 * a + 6 * b * square) * (h - h * h)


def first_body(
    x_ref, gain_ref, bias_ref, w_ref, b_ref, cot_ref, wo_ref,
    low_ref, hidden_ref, slope_ref, grad_ref, context_ref, sum_ref, turned, total,
):
    i = pl.program_id(0)
    block, step = x_ref.shape[0], w_ref.shape[1]
    blocks, tiles = low_ref.shape[0] // block, turned.shape[0] // step

    @pl.when(i < blocks)
    def _():
        normed, _ = norm_rows(x_ref[...])
        low = (normed * gain_ref[...] + bias_ref[...]).astype(BF16)
        low_ref[pl.ds(pl.multiple_of(i * block, block), block), :] = low

    @pl.when((i >= blocks) & (i < blocks + tiles))
    def _():
        hidden, slope = gelu_and_slope(dot(low_ref[...], w_ref[...]) + b_ref[...])
        hidden = hidden.astype(BF16)
        hidden_ref[...] = hidden
        turned[pl.ds(pl.multiple_of((i - blocks) * step, step), step), :] = hidden.T
        slope_ref[...] = slope.astype(BF16)

    @pl.when(i == blocks + tiles)
    def _():
        total[...] = jnp.zeros_like(total)

    @pl.when(i >= blocks + tiles)
    def _():
        cot = cot_ref[...]
        grad_ref[...] = dot(turned[...], cot)
        total[...] += dot_nt(cot, wo_ref[...])
        sum_ref[...] = jnp.sum(cot.astype(F32), axis=0, keepdims=True)

    @pl.when(i == pl.num_programs(0) - 1)
    def _():
        context_ref[...] = total[...].astype(BF16)


def first_products(x, gain, bias, w, b, cot, w_out, block=256, step=256, wide=512):
    rows, width = x.shape
    cols, heads = w.shape[1], w_out.shape[0]
    blocks, tiles, last = rows // block, cols // step, width // wide

    def tile(j):
        return jnp.clip(j - blocks, 0, tiles - 1)

    def final(j):
        return jnp.maximum(j - blocks - tiles, 0)

    out = pl.BlockSpec((rows, step), lambda j: (0, tile(j)))
    return kernel(
        first_body,
        (
            shape((rows, width), BF16),
            shape((rows, cols), BF16),
            shape((rows, cols), BF16),
            shape((cols, width)),
            shape((rows, heads), BF16),
            shape((1, width)),
        ),
        (blocks + tiles + last,),
        [
            pl.BlockSpec((block, width), lambda j: (jnp.minimum(j, blocks - 1), 0)),
            whole((1, width)),
            whole((1, width)),
            pl.BlockSpec((width, step), lambda j: (0, tile(j))),
            pl.BlockSpec((1, step), lambda j: (0, tile(j))),
            pl.BlockSpec((rows, wide), lambda j: (0, final(j))),
            pl.BlockSpec((heads, wide), lambda j: (0, final(j))),
        ],
        (
            whole((rows, width)),
            out,
            out,
            pl.BlockSpec((cols, wide), lambda j: (0, final(j))),
            whole((rows, heads)),
            pl.BlockSpec((1, wide), lambda j: (0, final(j))),
        ),
        scratch=[pltpu.VMEM((cols, rows), BF16), pltpu.VMEM((rows, heads), F32)],
        us=20,
        vmem=60,
    )(x, gain, bias, w, b, cot, w_out)


def side_body(
    ln_ref, cot_ref, w_ref, slope_ref, proj_ref, context_ref, out_ref, pre_ref, sum_ref
):
    i = pl.program_id(0)
    tile, step = w_ref.shape[0], proj_ref.shape[2]
    n, block = pre_ref.shape[1], ln_ref.shape[1]
    tiles = n // tile

    @pl.when(i < tiles)
    def _():
        grad = (dot_nt(cot_ref[...], w_ref[...]) * slope_ref[...]).astype(BF16)
        pre_ref[:, pl.ds(pl.multiple_of(i * tile, tile), tile)] = grad
        sum_ref[...] = jnp.sum(grad.astype(F32), axis=0, keepdims=True)

    @pl.when(i >= tiles)
    def _():
        turned = ln_ref[...].T
        out_ref[:, :n] = dot(turned, pre_ref[...])
        for c in range(3):
            out_ref[:, n + c * step : n + (c + 1) * step] = dot(turned, proj_ref[c])
        cot = cot_ref[:, pl.ds(pl.multiple_of((i - tiles) * block, block), block)]
        out_ref[:, n + 3 * step :] = dot(cot.T, context_ref[...])


def side_grads(ln, cot, w, slope, proj, context, block=512, tile=256):
    rows, m = ln.shape
    n, step = w.shape[0], proj.shape[2]
    tiles = n // tile

    def first(j):
        return jnp.minimum(j, tiles - 1)

    def second(j):
        return jnp.maximum(j - tiles, 0)

    return kernel(
        side_body,
        (shape((m, n + 4 * step)), shape((rows, n), BF16), shape((1, n))),
        (tiles + m // block,),
        [
            pl.BlockSpec((rows, block), lambda j: (0, second(j))),
            whole((rows, m)),
            pl.BlockSpec((tile, m), lambda j: (first(j), 0)),
            pl.BlockSpec((rows, tile), lambda j: (0, first(j))),
            whole((3, rows, step)),
            whole((rows, step)),
        ],
        (
            pl.BlockSpec((block, n + 4 * step), lambda j: (second(j), 0)),
            whole((rows, n)),
            pl.BlockSpec((1, tile), lambda j: (0, first(j))),
        ),
        us=18,
        vmem=60,
    )(ln, cot, w, slope, proj, context)


def split_body(side, one, three, turned):
    n, step = one.shape[1], three.shape[2]
    one[...] = side[:, :n]
    for c in range(3):
        three[c] = side[:, n + c * step : n + (c + 1) * step]
    turned[...] = side[:, n + 3 * step :].T


def split_grads(side, n, step, tile=512):
    rows = side.shape[0]
    return kernel(
        split_body,
        (shape((rows, n)), shape((3, rows, step)), shape((step, rows))),
        (rows // tile,),
        [pl.BlockSpec((tile, side.shape[1]), lambda i: (i, 0))],
        (
            pl.BlockSpec((tile, n), lambda i: (i, 0)),
            pl.BlockSpec((3, tile, step), lambda i: (0, i, 0)),
            pl.BlockSpec((step, tile), lambda i: (0, i)),
        ),
        us=12,
        vmem=40,
    )(side)


def copy_body(source, out):
    out[...] = source[...]


def copy_of(source, step=256):
    rows, width = source.shape
    spec = pl.BlockSpec((step, width), lambda i: (i, 0))
    return kernel(
        copy_body, shape((rows, width)), (rows // step,), [spec], spec, us=6, vmem=60    )(source)


def swap_halves(u, low, high):
    width = u.shape[1]
    return pltpu.roll(u, width - ROT // 2, 1) * low + pltpu.roll(u, ROT // 2, 1) * high


def fill_tables(pos_ref, rate_ref, cos_ref, low_ref, high_ref):
    angles = rate_ref[...] * pos_ref[...].astype(F32)
    count = ROT // 2
    entry = lax.broadcasted_iota(jnp.int32, (count, 2 * HEAD_DIM), 0)
    lane = lax.broadcasted_iota(jnp.int32, (count, 2 * HEAD_DIM), 1) % HEAD_DIM
    first = jnp.where(lane == entry, 1.0, 0.0).astype(F32)
    second = jnp.where(lane == entry + count, 1.0, 0.0).astype(F32)

    def spread(table, lanes):
        return lax.dot_general(
            table, lanes, (((0,), (0,)), ((), ())),
            precision=lax.Precision.HIGHEST, preferred_element_type=F32,
        )

    sine = jnp.sin(angles)
    kept = jnp.where(lane[:1] >= ROT, 1.0, 0.0)
    cos_ref[...] = spread(jnp.cos(angles), first + second) + kept
    low_ref[...] = spread(sine, -first)
    high_ref[...] = spread(sine, second)


def rotary_rates():
    steps_half = np.arange(0, ROT, 2).astype(np.float32) / np.float32(ROT)
    return jnp.asarray((np.float32(10000.0) ** (-steps_half))[:, None])


def qkv_body(ln_ref, w_ref, b_ref, pos_ref, rate_ref, out_ref, cos_ref, low_ref, high_ref):
    c = pl.program_id(0)

    @pl.when(c == 0)
    def _():
        fill_tables(pos_ref, rate_ref, cos_ref, low_ref, high_ref)

    u = dot(ln_ref[...], w_ref[0]) + b_ref[pl.ds(c, 1), :]

    @pl.when(c == 2)
    def _():
        out_ref[0] = u.astype(BF16)

    @pl.when(c < 2)
    def _():
        for lane in range(0, u.shape[1], 128):
            part = u[:, lane : lane + 128]
            turned = part * cos_ref[...] + swap_halves(part, low_ref[...], high_ref[...])
            out_ref[0, :, lane : lane + 128] = turned.astype(BF16)


def project(ln, w_parts, bias, positions, rates):
    rows, width = ln.shape
    cols = w_parts.shape[2]
    return kernel(
        qkv_body,
        (shape((3, rows, cols), BF16),) + (shape((rows, 128)),) * 3,
        (3,),
        [
            whole((rows, width)),
            pl.BlockSpec((1, width, cols), lambda c: (c, 0, 0)),
            whole((3, cols)),
            whole((1, rows)),
            whole((ROT // 2, 1)),
        ],
        (pl.BlockSpec((1, rows, cols), lambda c: (c, 0, 0)),) + (whole((rows, 128)),) * 3,
        us=7,
        vmem=60,
    )(ln, w_parts, bias, positions, rates)


def attention_body(
    q_ref, k_ref, v_ref, g_ref, seg_ref, cos_ref, low_ref, high_ref,
    context_ref, grad_ref, sum_ref, dq, dk, dv,
):
    rows = q_ref.shape[1]
    step = 384
    scale = np.float32(HEAD_DIM**-0.5)
    lane = lax.broadcasted_iota(jnp.int32, (rows, 128), 1)
    heads = []
    for h in range(2):
        mine = (lane >= h * HEAD_DIM) & (lane < (h + 1) * HEAD_DIM)
        heads.append(
            [
                jnp.where(mine, ref, jnp.zeros_like(ref))
                for ref in (q_ref[0] * scale.astype(BF16), k_ref[0], v_ref[0], g_ref[...])
            ]
        )
    seg_row = seg_ref[...].astype(F32)
    seg_col = jnp.broadcast_to(seg_row, (128, rows)).T[:, :1]
    dk[...] = jnp.zeros_like(dk)
    dv[...] = jnp.zeros_like(dv)
    for i in range(rows // step):
        top = slice(i * step, (i + 1) * step)
        seen = (i + 1) * step
        row = lax.broadcasted_iota(jnp.int32, (step, seen), 0) + i * step
        col = lax.broadcasted_iota(jnp.int32, (step, seen), 1)
        allowed = (seg_col[top, :] == seg_row[:, :seen]) & (col <= row)
        context = jnp.zeros((step, 128), F32)
        grad_q = jnp.zeros((step, 128), F32)
        for q, k, v, g in heads:
            scores = jnp.where(allowed, dot_nt(q[top], k[:seen]), MASKED)
            peak = jnp.max(scores, axis=-1, keepdims=True)
            raised = jnp.exp(scores - peak)
            probs = raised * (1.0 / jnp.sum(raised, axis=-1, keepdims=True))
            probs_low = probs.astype(BF16)
            context += dot(probs_low, v[:seen])
            grad_probs = dot_nt(g[top], v[:seen])
            delta = jnp.sum(probs * grad_probs, axis=-1, keepdims=True)
            grad_scores = (probs * (grad_probs - delta)).astype(BF16)
            grad_q += dot(grad_scores, k[:seen])
            dk[:seen, :] += dot_tn(grad_scores, q[top])
            dv[:seen, :] += dot_tn(probs_low, g[top])
        context_ref[top, :] = context.astype(BF16)
        dq[top, :] = grad_q * scale
    for c, grad in enumerate((dq, dk, dv)):
        u = grad[...]
        if c < 2:
            u = u * cos_ref[...] - swap_halves(u, low_ref[...], high_ref[...])
        u = u.astype(BF16)
        grad_ref[c] = u
        sum_ref[c] = jnp.sum(u.astype(F32), axis=0, keepdims=True)


def attention(qkv, grad_context, segments, tables):
    _, rows, cols = qkv.shape
    pair = pl.BlockSpec((rows, 128), lambda p: (0, p))
    return kernel(
        attention_body,
        (shape((rows, cols), BF16), shape((3, rows, cols), BF16), shape((3, 1, cols))),
        (cols // 128,),
        [pl.BlockSpec((1, rows, 128), lambda p, c=c: (c, 0, p)) for c in range(3)]
        + [pair, whole((1, rows))]
        + [whole((rows, 128))] * 3,
        (
            pair,
            pl.BlockSpec((3, rows, 128), lambda p: (0, 0, p)),
            pl.BlockSpec((3, 1, 128), lambda p: (0, 0, p)),
        ),
        scratch=[pltpu.VMEM((rows, 128), F32)] * 3,
        us=12,
        vmem=60,
    )(qkv, qkv, qkv, grad_context, segments, *tables)


def chunks_of(z):
    return jnp.stack([z ^ 2, z ^ 1, z ^ 3, z]).astype(jnp.int32)


def put_chunks(outs, total):
    row = 0
    for out in outs:
        out[...] = total[row : row + out.shape[0], :]
        row += out.shape[0]


def chunk_rows(count):
    return [count // 2, count // 2, count, count, count]


def branch_body(at, *refs):
    lefts, rights = refs[:8], refs[8:10]
    outs, hidden, context = refs[10:15], refs[15], refs[16]
    count = outs[-1].shape[0]

    @pl.when(pl.program_id(0) == 0)
    def _():
        for i in range(4):
            hidden[i * count : (i + 1) * count, :] = lefts[i][...]
            context[i * count : (i + 1) * count, :] = lefts[4 + i][...]

    total = dot(hidden[...], rights[0][...]) + dot(context[...], rights[1][...])
    put_chunks(outs, total)


def branch_sums(at, hidden, context, w_fc2, w_out, step=512):
    rows, inner = hidden.shape
    heads = context.shape[1]
    width = w_fc2.shape[1]
    count = rows // 4

    def chunk(cols, i):
        return pl.BlockSpec((count, cols), lambda j, at, i=i: (at[i], 0))

    return kernel(
        branch_body,
        [shape((n, width)) for n in chunk_rows(count)],
        (width // step,),
        [chunk(inner, i) for i in range(4)]
        + [chunk(heads, i) for i in range(4)]
        + [
            pl.BlockSpec((inner, step), lambda j, at: (0, j)),
            pl.BlockSpec((heads, step), lambda j, at: (0, j)),
        ],
        [pl.BlockSpec((n, step), lambda j, at: (0, j)) for n in chunk_rows(count)],
        scratch=[pltpu.VMEM((rows, inner), BF16), pltpu.VMEM((rows, heads), BF16)],
        scalars=1,
        us=9,
        vmem=60,
    )(at, *[hidden] * 4, *[context] * 4, w_fc2, w_out)


def grad_ln_body(at, *refs):
    lefts, rights = refs[:8], refs[8:10]
    outs, pre, proj = refs[10:15], refs[15], refs[16]
    count = outs[-1].shape[0]

    @pl.when(pl.program_id(0) == 0)
    def _():
        for i in range(4):
            pre[i * count : (i + 1) * count, :] = lefts[i][...]
            for c in range(3):
                proj[c, i * count : (i + 1) * count, :] = lefts[4 + i][c]

    total = dot_nt(pre[...], rights[0][...])
    for c in range(3):
        total += dot_nt(proj[c], rights[1][c])
    put_chunks(outs, total)


def grad_ln_sums(at, pre, proj, w_fc1, w_parts, step=512):
    rows, inner = pre.shape
    heads = proj.shape[2]
    width = w_fc1.shape[0]
    count = rows // 4
    return kernel(
        grad_ln_body,
        [shape((n, width)) for n in chunk_rows(count)],
        (width // step,),
        [pl.BlockSpec((count, inner), lambda j, at, i=i: (at[i], 0)) for i in range(4)]
        + [pl.BlockSpec((3, count, heads), lambda j, at, i=i: (0, at[i], 0)) for i in range(4)]
        + [
            pl.BlockSpec((step, inner), lambda j, at: (j, 0)),
            pl.BlockSpec((3, step, heads), lambda j, at: (0, j, 0)),
        ],
        [pl.BlockSpec((n, step), lambda j, at: (0, j)) for n in chunk_rows(count)],
        scratch=[pltpu.VMEM((rows, inner), BF16), pltpu.VMEM((3, rows, heads), BF16)],
        scalars=1,
        us=11,
        vmem=60,
    )(at, *[pre] * 4, *[proj] * 4, w_fc1, w_parts)


def add_pair_body(up_in, down_in, high, low, up, down):
    up[...] = up_in[...] + high[...]
    down[...] = down_in[...] + low[...]


def add_halves(up, down, high, low, parts=2):
    rows, width = low.shape
    step = rows // parts
    first = pl.BlockSpec((step, width), lambda i: (i, 0))
    second = pl.BlockSpec((step, width), lambda i: (i + parts, 0))
    return kernel(
        add_pair_body,
        (shape(up.shape), shape(down.shape)),
        (parts,),
        [second, first, first, first],
        (second, first),
        aliases={0: 0, 1: 1},
        us=2,
        vmem=16,
    )(up, down, high, low)


def sum_body(*refs):
    total = refs[0][...]
    for ref in refs[1:-1]:
        total = total + ref[...]
    refs[-1][...] = total


def sum_of(*arrays, parts=3):
    rows, width = arrays[0].shape
    step = rows // parts
    spec = pl.BlockSpec((step, width), lambda i: (i, 0))
    return kernel(
        sum_body, shape((rows, width)), (rows // step,), [spec] * len(arrays), spec,
        us=3,
        vmem=16,
    )(*arrays)


def take_body(at, x, cot, x_out, cot_out):
    del at
    x_out[...] = x[...]
    cot_out[...] = cot[...]


def take_rows(at, x, cot, step=48):
    count, width = x.shape[0] // 4, x.shape[1]
    parts = count // step
    here = pl.BlockSpec((step, width), lambda i, at: (i, 0))
    there = pl.BlockSpec((step, width), lambda i, at: (at[3] * parts + i, 0))
    return kernel(
        take_body,
        (shape((count, width)), shape((count, width), BF16)),
        (parts,),
        [there, there],
        (here, here),
        scalars=1,
        us=3,
        vmem=60,
    )(at, x, cot)


def last_body(at, chunk, other, x, ob, fb, rows, out):
    del at
    total = chunk[...] + other[...] + x[...] + ob[...] + fb[...]
    rows[...] = total
    out[...] = total


def output_rows(at, chunk, other, x, out_bias, fc2_bias, step=48):
    count, width = chunk.shape
    parts = count // step
    here = pl.BlockSpec((step, width), lambda i, at: (i, 0))
    there = pl.BlockSpec((step, width), lambda i, at: (at[3] * parts + i, 0))
    return kernel(
        last_body,
        (shape((count, width)), shape((4 * count, width))),
        (parts,),
        [here, here, here, whole((1, width)), whole((1, width))],
        (here, there),
        scalars=1,
        us=4,
        vmem=16,
    )(at, chunk, other, x, out_bias, fc2_bias)


def norm_back_body(at, chunk, other, x, cot, gain, rows, out, sums):
    del at

    @pl.when(pl.program_id(0) == 0)
    def _():
        sums[...] = jnp.zeros_like(sums)

    grad = chunk[...] + other[...]
    normed, inv_std = norm_rows(x[...])
    sums[0:1, :] += jnp.sum(grad * normed, axis=0, keepdims=True)
    sums[1:2, :] += jnp.sum(grad, axis=0, keepdims=True)
    scaled = grad * gain[...]
    mean_scaled = jnp.mean(scaled, axis=-1, keepdims=True)
    mean_cross = jnp.mean(scaled * normed, axis=-1, keepdims=True)
    total = cot[...].astype(F32) + inv_std * (scaled - mean_scaled - normed * mean_cross)
    rows[...] = total
    out[...] = total


def input_grad_rows(at, chunk, other, x, cot, gain, step=48):
    count, width = chunk.shape
    parts = count // step
    here = pl.BlockSpec((step, width), lambda i, at: (i, 0))
    there = pl.BlockSpec((step, width), lambda i, at: (at[3] * parts + i, 0))
    return kernel(
        norm_back_body,
        (shape((count, width)), shape((4 * count, width)), shape((2, width))),
        (parts,),
        [here, here, here, here, whole((1, width))],
        (here, there, whole((2, width))),
        scalars=1,
        us=5,
        vmem=16,
    )(at, chunk, other, x, cot, gain)


def place_body(at, *refs, starts, sizes, copies):
    i = pl.program_id(0)
    count = len(starts)
    pieces, out, extra = refs[:count], refs[count + 1], refs[count + 2 :]
    for piece, start, size in zip(pieces, starts, sizes):

        @pl.when((i >= start) & (i < start + size))
        def _(piece=piece):
            out[...] = piece[...]

    for copy, (which, first, size) in zip(extra, copies):
        begin = starts[which] + first

        @pl.when((i >= begin) & (i < begin + size))
        def _(copy=copy, which=which):
            copy[...] = pieces[which][...]


def place_rows(out, pieces, blocks, copies=(), step=48):
    width = out.shape[1]
    sizes = [piece.shape[0] // step for piece in pieces]
    starts = [sum(sizes[:k]) for k in range(len(sizes))]

    def part(start, size):
        return pl.BlockSpec((step, width), lambda i, at: (jnp.clip(i - start, 0, size - 1), 0))

    return kernel(
        partial(place_body, starts=starts, sizes=sizes, copies=copies),
        [shape(out.shape)] + [shape((size * step, width)) for _, _, size in copies],
        (sum(sizes),),
        [part(start, size) for start, size in zip(starts, sizes)]
        + [pl.BlockSpec(memory_space=ANY)],
        [pl.BlockSpec((step, width), lambda i, at: (at[i], 0))]
        + [part(starts[which] + first, size) for which, first, size in copies],
        scalars=1,
        aliases={1 + len(pieces): 0},
        us=5,
        vmem=16,
    )(blocks, *pieces, out)


class Order:
    def __init__(self):
        self.last = None

    def __call__(self, step, *args):
        if self.last is not None:
            args, _ = lax.optimization_barrier((args, self.last))
        out = step(*args)
        self.last = jax.tree.leaves(out)[0]
        return out

    def after(self, *arrays):
        arrays, _ = lax.optimization_barrier((arrays, self.last))
        return arrays

    def wait(self, array):
        array, self.last = lax.optimization_barrier((array, self.last))
        return array


ROW_GROUPS = [[x * Y * CORE + i for i in range(Y * CORE)] for x in range(X_LO)]


def scatter(part):
    return lax.psum_scatter(
        part, "dp", scatter_dimension=0, axis_index_groups=ROW_GROUPS, tiled=True
    )


def gather(piece):
    return lax.all_gather(piece, "dp", axis=0, axis_index_groups=ROW_GROUPS, tiled=True)


def per_device(
    layer_input,
    ln_gain,
    ln_bias,
    w_qkv,
    qkv_bias,
    w_out,
    out_bias,
    w_fc1,
    fc1_bias,
    w_fc2,
    fc2_bias,
    segments,
    positions,
    cotangent,
):
    width = layer_input.shape[1]
    inner, local = w_fc1.shape[1], w_qkv.shape[2]
    at = chunks_of(lax.axis_index("tensor") // X_HI)
    run = Order()
    w_parts = jnp.transpose(w_qkv, (1, 0, 2))
    blocks = at[:3, None] * 4 + jnp.arange(4, dtype=jnp.int32)[None, :]
    near, far = blocks[1:].reshape(-1), blocks[0]
    near_copies = ((0, 0, 2), (1, 2, 2))
    add = partial(sum_of, parts=1)

    ln, hidden, slope, grad_fc2, grad_context, sum_out = run(
        first_products,
        layer_input, ln_gain[None], ln_bias[None], w_fc1, fc1_bias[None], cotangent, w_out,
    )
    piece_fc2 = scatter(grad_fc2)
    qkv, *tables = run(project, ln, w_parts, qkv_bias, positions, rotary_rates())
    context, grad_proj, sum_proj = run(attention, qkv, grad_context, segments, tables)
    low, high, up, down, own = run(branch_sums, at, hidden, context, w_fc2, w_out)
    low, high = send(low, "z^1"), send(high, "z^3")
    side, grad_pre, sum_pre = run(side_grads, ln, cotangent, w_fc2, slope, grad_proj, context)
    low, high = run.wait(low), run.wait(high)
    piece_fc2 = run.wait(piece_fc2)
    (side,) = run.after(side)
    piece = scatter(side)
    other_fc2 = send(*run.after(piece_fc2), "xlo")
    up, down = run(add_halves, up, down, high, low)
    from_up, from_down = send(up, "z^1"), send(down, "z^3")
    g_low, g_high, g_up, g_down, g_own = run(
        grad_ln_sums, at, grad_pre, grad_proj, w_fc1, w_parts
    )
    g_low, g_high = send(g_low, "z^1"), send(g_high, "z^3")
    piece_fc2 = run(partial(sum_of, parts=4), piece_fc2, other_fc2)
    chunk = run(sum_of, own, from_up, from_down)
    other = send(chunk, "xhi")
    g_up, g_down = run(add_halves, g_up, g_down, g_high, g_low)
    g_from_up, g_from_down = send(g_up, "z^1"), send(g_down, "z^3")
    x_rows, cot_rows = run(take_rows, at, layer_input, cotangent)
    rows, output = run(output_rows, at, chunk, other, x_rows, out_bias[None], fc2_bias[None])
    g_from_up, g_from_down = run.wait(g_from_up), run.wait(g_from_down)
    piece = run.wait(piece)
    (piece_fc2,) = run.after(piece_fc2)
    tot_fc2 = gather(piece_fc2)
    rows, piece = run.after(rows, piece)
    other_piece = send(piece, "xlo")
    near_up, near_down = send(rows, "z^1"), send(rows, "z^3")
    g_chunk = run(sum_of, g_own, g_from_up, g_from_down)
    output, low, high = run(
        partial(place_rows, copies=near_copies), output, [near_up, near_down], near
    )
    piece = run(partial(sum_of, parts=4), piece, other_piece)
    side = gather(piece)
    g_chunk, low, high = run.after(g_chunk, low, high)
    g_other = send(g_chunk, "xhi")
    low, high = send(low, "z^3"), send(high, "z^1")
    tot_fc2 = run(copy_of, tot_fc2)
    (output,) = run(place_rows, output, [low, high], far)
    g_rows, grad_input, sums = run(
        input_grad_rows, at, g_chunk, g_other, x_rows, cot_rows, ln_gain[None]
    )
    g_near_up, g_near_down = send(g_rows, "z^1"), send(g_rows, "z^3")
    biases = jnp.concatenate(
        [sum_out[0], sum_pre[0], sum_proj.reshape(-1), jnp.zeros((256,), F32)]
    ).reshape(8, width // 4)
    sums = jnp.concatenate([sums.reshape(8, width // 4), biases], axis=0)
    for move in ("core", "y^1", "y^2", "xlo"):
        sums = run(add, sums, send(sums, move))
    norm_sums = run.wait(sums[:8])
    other_sums = send(norm_sums, "z^1")
    rest = sums[8:].reshape(-1)
    tot_out_bias = run.wait(rest[:width])
    tot_fc1_bias = run.wait(rest[width : width + inner])
    tot_qkv_bias = run.wait(rest[width + inner : width + inner + 3 * local].reshape(3, local))
    tot_fc2_bias = run(add, tot_out_bias[None])[0]
    norm_sums = run(add, norm_sums, other_sums)
    other_sums = send(norm_sums, "z^2")
    norm_sums = run(add, norm_sums, other_sums)
    grad_input, g_low, g_high = run(
        partial(place_rows, copies=near_copies), grad_input, [g_near_up, g_near_down], near
    )
    g_low, g_high = send(g_low, "z^3"), send(g_high, "z^1")
    norm_sums = norm_sums.reshape(2, width)
    gain, shift = run.wait(norm_sums[0]), run.wait(norm_sums[1])
    tot_fc1, tot_qkv, tot_out = run(lambda side: split_grads(side, inner, local), side)
    (grad_input,) = run(place_rows, grad_input, [g_low, g_high], far)
    return (
        output,
        grad_input,
        gain,
        shift,
        jnp.transpose(tot_qkv, (1, 0, 2)),
        tot_qkv_bias,
        tot_out,
        tot_out_bias,
        tot_fc1,
        tot_fc1_bias,
        tot_fc2,
        tot_fc2_bias,
    )


def solution(mesh):
    in_specs = (
        P("dp", None),
        P(),
        P(),
        P(None, None, "tensor"),
        P(None, "tensor"),
        P("tensor", None),
        P(),
        P(None, "tensor"),
        P("tensor"),
        P("tensor", None),
        P(),
        P("dp", None),
        P("dp", None),
        P("dp", None),
    )
    out_specs = (
        P("dp", None),
        P("dp", None),
        P(),
        P(),
        P(None, None, "tensor"),
        P(None, "tensor"),
        P("tensor", None),
        P(),
        P(None, "tensor"),
        P("tensor"),
        P("tensor", None),
        P(),
    )
    return jax.shard_map(
        per_device, mesh=mesh, in_specs=in_specs, out_specs=out_specs, check_vma=False
    )
```
